128 devices in a mesh: dp: 16 (over y, x_hi, core), tensor: 8 (over x_lo, z).
Axes of the slice: x: 4 (x_hi: 2, x_lo: 2; x = x_hi * 2 + x_lo), y: 4, z: 4, core: 2. Of those that a mesh axis runs over, the one named last changes fastest.
Arguments:
- tokens: bfloat16 [32768, 1024], P(('dp', 'tensor')), may hold values from -6 to 6
- lengths: int32 [16, 3], P('dp'), may hold values from 1 to 1536, 2048 in all within a row
- token_order: int32 [16, 2048], P('dp'), may hold values from 0 to 2047, each once within a row
- routes: int32 [32768, 8], P(('dp', 'tensor')), may hold values from 0 to 31, all different within a row; in each aligned block of 256 rows (0 to 255, 256 to 511, ...) at most 80 rows name the same one
- cotangent: bfloat16 [32768, 1024], P(('dp', 'tensor')), may hold values from -6 to 6
- attn_gain: bfloat16 [1024], P(('dp', 'tensor')), may hold values from 0.099609375 to 1.8984375
- ffn_gain: bfloat16 [1024], P(('dp', 'tensor')), may hold values from 0.099609375 to 1.8984375
- router: bfloat16 [1024, 32], P(('dp', 'tensor')), may hold values from -0.09375 to 0.09375
- w_query: bfloat16 [1024, 1024], P('dp', 'tensor'), may hold values from -0.1875 to 0.1875
- w_key: bfloat16 [1024, 512], P('dp', 'tensor'), may hold values from -0.1875 to 0.1875
- w_value: bfloat16 [1024, 512], P('dp', 'tensor'), may hold values from -0.1875 to 0.1875
- w_output: bfloat16 [1024, 1024], P('tensor', 'dp'), may hold values from -0.75 to 0.75
- query_gain: bfloat16 [16, 64], P('tensor', 'dp'), may hold values from 0.099609375 to 1.8984375
- key_gain: bfloat16 [8, 64], P('tensor', 'dp'), may hold values from 0.099609375 to 1.8984375
- w_gate: bfloat16 [32, 1024, 512], P('tensor', 'dp'), may hold values from -0.1875 to 0.1875
- w_up: bfloat16 [32, 1024, 512], P('tensor', 'dp'), may hold values from -0.1875 to 0.1875
- w_down: bfloat16 [32, 512, 1024], P('tensor', None, 'dp'), may hold values from -0.75 to 0.75
Outputs:
- layer_out: float32 [32768, 1024], P(('dp', 'tensor'))
- grad_tokens: float32 [32768, 1024], P(('dp', 'tensor'))
- grad_attn_gain: float32 [1024], P(('dp', 'tensor'))
- grad_ffn_gain: float32 [1024], P(('dp', 'tensor'))
- grad_router: float32 [1024, 32], P(('dp', 'tensor'))
- grad_w_query: float32 [1024, 1024], P('dp', 'tensor')
- grad_w_key: float32 [1024, 512], P('dp', 'tensor')
- grad_w_value: float32 [1024, 512], P('dp', 'tensor')
- grad_w_output: float32 [1024, 1024], P('tensor', 'dp')
- grad_query_gain: float32 [16, 64], P('tensor', 'dp')
- grad_key_gain: float32 [8, 64], P('tensor', 'dp')
- grad_w_gate: float32 [32, 1024, 512], P('tensor', 'dp')
- grad_w_up: float32 [32, 1024, 512], P('tensor', 'dp')
- grad_w_down: float32 [32, 512, 1024], P('tensor', None, 'dp')
The draws below stay inside these ranges and needn't reach their ends.
Inputs may be any that keep to these rules, and one draw needn't show every extreme that they name: `token_order`: each row is a permutation: the rows of group g hold the places of its packed stream. Each row holds 3 lengths summing to 2048; the longest is exactly 1536. `routes`: each row names 8 different experts; in the 256 rows of one device no expert is named more than 80 times, a bound that some block reaches.
All inputs are finite; a program needn't handle non-finite values.
Results may differ from the reference program's by a relative error of at most 0.028.
Values may be sent and summed in bfloat16 or wider, within the bound.
A program may use at most 192 MiB of HBM per device.

```python
import math
import jax
import jax.numpy as jnp
import numpy as np
from jax import lax

D = 1024
H = 16
HD = 64
KVH = 8
E = 32
F = 512
TOPK = 8
TOK_DEV = 256
SEQS = 3
CAP = 80
GROUP = 2048
TOKENS = 32768
N_DP = 16


def level_of(stream_key, shape, split, least, high):
    gain = 1.0
    for dim, shards_of in split:
        heights = jax.random.uniform(jax.random.fold_in(jax.random.fold_in(stream_key, 6), dim), (shards_of,), jnp.float32, least / len(split), high / len(split))
        gain = gain * jnp.repeat(jnp.exp(heights), shape[dim] // shards_of).reshape((-1,) + (1,) * (len(shape) - 1 - dim))
    return gain


def profile(number_of, total, most, skew):
    weights = [(1 << 20) // math.isqrt(rank ** skew) + 1 for rank in range(2, number_of + 1)]
    spare, counts = total - most - (number_of - 1), [1] * (number_of - 1)
    while spare > 0:
        movable = [i for i in range(number_of - 1) if counts[i] < most]
        whole, budget = sum([weights[i] for i in movable]), spare
        for i in movable:
            addition = min(most - counts[i], max(1, budget * weights[i] // whole), spare)
            counts[i] = counts[i] + addition
            spare = spare - addition
    return np.array([most] + counts)


def uneven(own_key, number_of, total, bound, lean):
    if number_of == 2:
        one = jax.random.randint(own_key, (), max(1, total - bound), min(bound, total - 1) + 1)
        return jnp.stack([one, total - one])
    sizes = jnp.asarray(profile(number_of, total, bound, lean), jnp.int32)
    twos = (number_of - 1) // 2
    donor, taker = sizes[1:1 + 2 * twos:2], sizes[2:2 + 2 * twos:2]
    room = jnp.minimum(donor - 1, bound - taker)
    shifted = jax.random.randint(jax.random.fold_in(own_key, 1), (twos,), 0, 1 << 20) % (room + 1)
    sizes = sizes.at[1:1 + 2 * twos:2].set(donor - shifted).at[2:2 + 2 * twos:2].set(taker + shifted)
    return sizes[jax.random.permutation(jax.random.fold_in(own_key, 2), number_of)]


def routed_block(key, own, number, rows, amount, top, limit, skew):
    ranking = jax.random.permutation(key, amount)
    heavy_load, ordinary = portions_of(amount, rows * top, limit, skew, True), portions_of(amount, rows * top, limit, skew, False)
    places = jnp.arange(amount)

    def named(sizes, rotation):
        used = int((sizes > 0).sum())
        fixed = max(1, used // 4)
        shifted = fixed + (places - fixed + rotation * (used - fixed)) % max(1, amount - fixed)
        return jnp.zeros((amount,), jnp.int32).at[ranking[jnp.where(places < fixed, places, shifted)]].set(jnp.asarray(sizes, jnp.int32))

    sizes = jnp.where(number % 4 == 0, named(heavy_load, number // 4), named(ordinary, number - number // 4 - 1))
    mixed = jax.random.permutation(jax.random.fold_in(own, 3), amount)
    giver, sink = mixed[0:amount // 2 * 2:2], mixed[1:amount // 2 * 2:2]
    slack = jnp.minimum(sizes[giver] - 1, limit - sizes[sink]) // 2
    slack = jnp.where((giver == ranking[0]) | (sink == ranking[0]) | (sizes[sink] == 0), 0, jnp.maximum(slack, 0))
    shifted = jax.random.randint(jax.random.fold_in(own, 4), (amount // 2,), 0, 1 << 20) % (slack + 1)
    sizes = sizes.at[giver].add(-shifted).at[sink].add(shifted)
    members = jnp.searchsorted(jnp.cumsum(sizes), jnp.arange(rows * top), side="right").astype(jnp.int32)
    table = members.reshape(top, rows).T
    table = table[jax.random.permutation(jax.random.fold_in(own, 1), rows)]
    rotation = jax.random.randint(jax.random.fold_in(own, 2), (rows, 1), 0, top)
    return jnp.take_along_axis(table, (jnp.arange(top)[None, :] + rotation) % top, axis=1)


def portions_of(count, total, most, skew, full):
    loads = [(1 << 20) // math.isqrt(grade ** skew) + 1 for grade in range(1, count + 1)]
    largest = most if full else min(most, max(-(-total // count), total * loads[0] // sum(loads)))
    least = 1 if total - largest >= count - 1 else 0
    given, rest = [largest] + [least] * (count - 1), total - largest - least * (count - 1)
    while rest > 0:
        candidates = [i for i in range(1, count) if given[i] < largest] or [i for i in range(1, count) if given[i] < most]
        pool, remaining = sum([loads[i] for i in candidates]), rest
        for i in candidates:
            addition = min(most - given[i], max(1, remaining * loads[i] // pool), rest)
            given[i] = given[i] + addition
            rest = rest - addition
    return np.array(given)


def scatter_about(rng, shape, width, most, split=(), kind=jnp.bfloat16):
    loudness = level_of(rng, shape, split, -0.22, 0.18) if split else 1.0
    values = jax.random.normal(rng, shape, jnp.float32) * width * loudness
    return jnp.minimum(jnp.maximum(values, -most), most).astype(kind)


def setup_inputs(seed: int = 0) -> dict:
    streams_of = jax.random.split(jax.random.key(seed), 18)
    tokens = scatter_about(streams_of[0], (TOKENS, D), 1.0, 6.0, ((0, 128),))
    lengths = jax.vmap(lambda own: uneven(own, SEQS, GROUP, GROUP // 2 + GROUP // 4, 2))(jax.random.split(streams_of[1], N_DP)).reshape((N_DP, SEQS)).astype(jnp.int32)
    token_order = jax.vmap(lambda own: jax.random.permutation(own, GROUP))(jax.random.split(streams_of[2], N_DP)).reshape((N_DP, GROUP)).astype(jnp.int32)
    routes_keys = jax.random.split(jax.random.fold_in(streams_of[3], 1), TOKENS // TOK_DEV)
    routes_turns = jax.random.permutation(jax.random.fold_in(streams_of[3], 3), TOKENS // TOK_DEV)
    routes = jax.vmap(lambda own, number: routed_block(jax.random.fold_in(streams_of[3], 2), own, number, TOK_DEV, E, TOPK, CAP, 1))(routes_keys, routes_turns).reshape((TOKENS, TOPK))
    cotangent = scatter_about(streams_of[4], (TOKENS, D), 1.0, 6.0, ((0, 128),))
    attn_gain = jnp.clip(1.0 + 0.18 * jax.random.normal(streams_of[5], (D,), jnp.float32), 0.099609375, 1.8984375).astype(jnp.bfloat16)
    ffn_gain = jnp.clip(1.0 + 0.18 * jax.random.normal(streams_of[6], (D,), jnp.float32), 0.099609375, 1.8984375).astype(jnp.bfloat16)
    router = scatter_about(streams_of[7], (D, E), (4 * D) ** -0.5, 0.09375, ((0, 128),))
    w_query = scatter_about(streams_of[8], (D, H * HD), D ** -0.5, 0.1875, ((0, 16), (1, 8)))
    w_key = scatter_about(streams_of[9], (D, KVH * HD), D ** -0.5, 0.1875, ((0, 16), (1, 8)))
    w_value = scatter_about(streams_of[10], (D, KVH * HD), D ** -0.5, 0.1875, ((0, 16), (1, 8)))
    w_output = scatter_about(streams_of[11], (H * HD, D), (H * HD // 16) ** -0.5, 0.75, ((0, 8), (1, 16)))
    query_gain = jnp.clip(1.0 + 0.18 * jax.random.normal(streams_of[12], (H, HD), jnp.float32), 0.099609375, 1.8984375).astype(jnp.bfloat16)
    key_gain = jnp.clip(1.0 + 0.18 * jax.random.normal(streams_of[13], (KVH, HD), jnp.float32), 0.099609375, 1.8984375).astype(jnp.bfloat16)
    w_gate = scatter_about(streams_of[14], (E, D, F), D ** -0.5, 0.1875, ((0, 8), (1, 16)))
    w_up = scatter_about(streams_of[15], (E, D, F), D ** -0.5, 0.1875, ((0, 8), (1, 16)))
    w_down = scatter_about(streams_of[16], (E, F, D), (F // 8) ** -0.5, 0.75, ((0, 8), (2, 16)))
    return {"tokens": tokens, "lengths": lengths, "token_order": token_order, "routes": routes, "cotangent": cotangent, "attn_gain": attn_gain, "ffn_gain": ffn_gain, "router": router, "w_query": w_query, "w_key": w_key, "w_value": w_value, "w_output": w_output, "query_gain": query_gain, "key_gain": key_gain, "w_gate": w_gate, "w_up": w_up, "w_down": w_down}


epsilon = 1e-06
rotary_base = 10000.0
masked_score = -1e+30
highest = lax.Precision.HIGHEST

@jax.custom_vjp
def low(v):
    return lax.optimization_barrier(v.astype(jnp.bfloat16)).astype(jnp.float32)

@jax.custom_vjp
def low_back(v):
    return v

def low_keep(v):
    return (low(v), None)

def low_pass(kept, grad):
    return (grad,)

def back_keep(v):
    return (v, None)

def back_low(kept, grad):
    return (low(grad),)
low.defvjp(low_keep, low_pass)
low_back.defvjp(back_keep, back_low)

def rms_scale(vector, scales):
    return vector * lax.rsqrt(lax.optimization_barrier(jnp.mean(vector * vector, axis=-1, keepdims=True)) + epsilon) * scales

def rotate(vector, positions):
    half_width = vector.shape[-1] // 2
    frequency = rotary_base ** (-2.0 * jnp.arange(half_width, dtype=jnp.float32) / vector.shape[-1])
    angles = positions.astype(jnp.float32)[:, None, None] * frequency[None, None, :]
    cosine_part = jnp.cos(angles)
    sine_part = jnp.sin(angles)
    first_half = vector[..., :half_width]
    second_half = vector[..., half_width:]
    return jnp.concatenate([first_half * cosine_part - second_half * sine_part, second_half * cosine_part + first_half * sine_part], axis=-1)

def places(stream, seq_lengths):
    seq_ends = jnp.cumsum(seq_lengths).astype(jnp.int32)
    segment = lax.optimization_barrier(jnp.sum((stream[:, None] >= seq_ends[None, :]).astype(jnp.int32), axis=1)).astype(jnp.int32)
    owner_table = segment[:, None] == jnp.arange(seq_lengths.shape[0], dtype=jnp.int32)[None, :]
    seq_start = lax.optimization_barrier(jnp.sum(jnp.where(owner_table, (seq_ends - seq_lengths)[None, :], 0), axis=1)).astype(jnp.int32)
    return (segment, (stream - seq_start).astype(jnp.int32))

def slot_index(route_rows):
    blocks = route_rows.shape[0] // TOK_DEV
    flat_picks = route_rows.reshape(blocks, TOK_DEV * TOPK).astype(jnp.int32)
    onehot = (flat_picks[:, :, None] == jnp.arange(E, dtype=jnp.int32)[None, None, :]).astype(jnp.int32)
    slot_rank = lax.optimization_barrier(jnp.sum(onehot * (jnp.cumsum(onehot, axis=1).astype(jnp.int32) - 1), axis=2)).astype(jnp.int32)
    block_base = jnp.arange(blocks, dtype=jnp.int32)[:, None] * (E * CAP)
    return (block_base + flat_picks * CAP + slot_rank).reshape(-1).astype(jnp.int32)

def group_layer(inputs, stream, seq_lengths, route_rows, attn_gain, ffn_gain, router, w_query, w_key, w_value, w_output, query_gain, key_gain, w_gate, w_up, w_down):
    group_rows = inputs.shape[0]
    segment, positions = places(stream, seq_lengths)
    normed = low(rms_scale(inputs, attn_gain))
    query_heads = low_back(jnp.dot(normed, w_query, precision=highest)).reshape(group_rows, H, HD)
    key_heads = low_back(jnp.dot(normed, w_key, precision=highest)).reshape(group_rows, KVH, HD)
    value_heads = low(low_back(jnp.dot(normed, w_value, precision=highest))).reshape(group_rows, KVH, HD)
    query_heads = low(rotate(rms_scale(query_heads, query_gain), positions))
    key_heads = low(rotate(rms_scale(key_heads, key_gain), positions))
    key_heads = jnp.repeat(key_heads, H // KVH, axis=1)
    value_heads = jnp.repeat(value_heads, H // KVH, axis=1)
    block_len = min(512, group_rows)

    def attend(start_row):
        query_block = lax.dynamic_slice_in_dim(query_heads, start_row, block_len, 0)
        seg_block = lax.dynamic_slice_in_dim(segment, start_row, block_len, 0)
        place_block = lax.dynamic_slice_in_dim(stream, start_row, block_len, 0)
        scores = low_back(jnp.einsum('qhd,khd->hqk', query_block, key_heads, precision=highest) * HD ** (-0.5))
        allowed = (seg_block[:, None] == segment[None, :]) & (stream[None, :] <= place_block[:, None])
        scores = jnp.where(allowed[None], scores, masked_score)
        row_peak = lax.optimization_barrier(jnp.max(scores, axis=-1, keepdims=True))
        exponent = jnp.exp(scores - row_peak)
        probability = low(exponent / lax.optimization_barrier(jnp.sum(exponent, axis=-1, keepdims=True)))
        return jnp.einsum('hqk,khd->qhd', probability, value_heads, precision=highest)
    start_rows = jnp.arange(group_rows // block_len, dtype=jnp.int32) * block_len
    mixed_heads = lax.map(jax.checkpoint(attend), start_rows).reshape(group_rows, H * HD)
    mixed_heads = low(low_back(mixed_heads))
    hidden = inputs + low_back(jnp.dot(mixed_heads, w_output, precision=highest))
    normed2 = low(rms_scale(hidden, ffn_gain))
    logits = low_back(jnp.dot(normed2, router, precision=highest))
    chosen = jnp.take_along_axis(logits, route_rows, axis=1)
    gate_probs = jax.nn.softmax(chosen, axis=-1)
    blocks = group_rows // TOK_DEV
    slots = slot_index(route_rows)
    copies = low_back(jnp.repeat(normed2, TOPK, axis=0))
    buffer = jnp.zeros((blocks * E * CAP, D), jnp.float32).at[slots].set(copies)
    buffer = buffer.reshape(blocks, E, CAP, D).transpose(1, 0, 2, 3).reshape(E, blocks * CAP, D)
    gate_act = low_back(jnp.einsum('erd,edf->erf', buffer, w_gate, precision=highest))
    up_act = low_back(jnp.einsum('erd,edf->erf', buffer, w_up, precision=highest))
    inner_act = low(jax.nn.silu(gate_act) * up_act)
    expert_out = low(low_back(jnp.einsum('erf,efd->erd', inner_act, w_down, precision=highest)))
    expert_out = expert_out.reshape(E, blocks, CAP, D).transpose(1, 0, 2, 3).reshape(blocks * E * CAP, D)
    picked = expert_out[slots].reshape(group_rows, TOPK, D)
    return hidden + lax.optimization_barrier(jnp.sum(gate_probs[:, :, None] * picked, axis=1))

def reference(tokens, lengths, token_order, routes, cotangent, attn_gain, ffn_gain, router, w_query, w_key, w_value, w_output, query_gain, key_gain, w_gate, w_up, w_down):
    params = tuple((item.astype(jnp.float32) for item in (attn_gain, ffn_gain, router, w_query, w_key, w_value, w_output, query_gain, key_gain, w_gate, w_up, w_down)))
    grouped_routes = routes.reshape(N_DP, GROUP, TOPK)

    def forward(inputs, *weights):
        grouped = inputs.reshape(N_DP, GROUP, D)

        def step(totals, group_item):
            group_in, stream, seq_lengths, route_rows = group_item
            return (totals, group_layer(group_in, stream, seq_lengths, route_rows, *weights))
        _, results = lax.scan(jax.checkpoint(step), jnp.zeros((), jnp.float32), (grouped, token_order, lengths, grouped_routes))
        return results.reshape(TOKENS, D)
    result, pull = jax.vjp(forward, tokens.astype(jnp.float32), *params)
    grads = pull(cotangent.astype(jnp.float32))
    return (result, grads[0], grads[1], grads[2], grads[3], grads[4], grads[5], grads[6], grads[7], grads[8], grads[9], grads[10], grads[11], grads[12])
```

```python
import functools

import jax
import jax.numpy as jnp
from jax import lax
from jax.experimental import pallas as pl
from jax.experimental.pallas import tpu as pltpu
from jax.sharding import PartitionSpec as P

CAP = 80
EPS = 1e-06
ROTARY_BASE = 10000.0
MASKED = -1e30
MESH = pl.DeviceIdType.MESH
bf16 = jnp.bfloat16
f32 = jnp.float32


def tiny_gather_kernel(n, x, o, send_sem, recv_sem, local_sem):
    me = lax.axis_index("tensor")
    barrier = pltpu.get_barrier_semaphore()
    for k in range(1, n):
        pl.semaphore_signal(
            barrier, inc=1, device_id={"tensor": lax.rem(me + k, n)}, device_id_type=MESH
        )
    pl.semaphore_wait(barrier, n - 1)
    own = pltpu.make_async_copy(x, o.at[me], local_sem)
    own.start()
    copies = []
    for k in range(1, n):
        copy = pltpu.make_async_remote_copy(
            src_ref=x,
            dst_ref=o.at[me],
            send_sem=send_sem.at[k],
            recv_sem=recv_sem.at[k],
            device_id={"tensor": lax.rem(me + k, n)},
            device_id_type=MESH,
        )
        copy.start()
        copies.append(copy)
    for copy in copies:
        copy.wait()
    own.wait()


def tiny_gather(x, collective_id):
    n = 8
    return pl.pallas_call(
        functools.partial(tiny_gather_kernel, n),
        out_shape=jax.ShapeDtypeStruct((n,) + x.shape, x.dtype),
        in_specs=[pl.BlockSpec(memory_space=pl.ANY)],
        out_specs=pl.BlockSpec(memory_space=pl.ANY),
        scratch_shapes=[
            pltpu.SemaphoreType.DMA((n,)),
            pltpu.SemaphoreType.DMA((n,)),
            pltpu.SemaphoreType.DMA,
        ],
        compiler_params=pltpu.CompilerParams(collective_id=collective_id, has_side_effects=True),
        name="tiny_gather",
    )(x)


def row_gather_kernel(count, *refs):
    xs, outs = refs[:count], refs[count : 2 * count]
    send_sem, recv_sem, local_sem = refs[2 * count :]
    me = lax.axis_index("tensor")
    z = lax.rem(me, 4)
    side = me // 4
    right, left = lax.rem(z + 1, 4), lax.rem(z + 3, 4)
    here, there = side * 4, (1 - side) * 4
    partner = there + z
    barrier = pltpu.get_barrier_semaphore()
    for peer in (partner, here + right, here + left):
        pl.semaphore_signal(barrier, inc=1, device_id={"tensor": peer}, device_id_type=MESH)
    pl.semaphore_wait(barrier, 3)

    def send(index, a, src, dst, peer):
        copy = pltpu.make_async_remote_copy(
            src_ref=src,
            dst_ref=dst,
            send_sem=send_sem.at[a, index],
            recv_sem=recv_sem.at[a, index],
            device_id={"tensor": peer},
            device_id_type=MESH,
        )
        copy.start()
        return copy

    owns, done = [], []
    first = []
    for a in range(count):
        x, o = xs[a], outs[a]
        own = pltpu.make_async_copy(x, o.at[me], local_sem.at[a])
        own.start()
        owns.append(own)
        first.append(
            (
                send(0, a, x, o.at[me], partner),
                send(1, a, x, o.at[me], here + right),
                send(2, a, x, o.at[me], here + left),
            )
        )
    for a in range(count):
        o = outs[a]
        half = o.shape[1] // 2
        low, high = pl.ds(0, half), pl.ds(half, half)
        to_partner, to_right, to_left = first[a]
        to_partner.wait_recv()
        pass_right = send(3, a, o.at[partner], o.at[partner], here + right)
        pass_left = send(4, a, o.at[partner], o.at[partner], here + left)
        to_right.wait_recv()
        far = [send(5, a, o.at[here + left, low], o.at[here + left, low], here + right)]
        to_left.wait_recv()
        far += [send(6, a, o.at[here + right, high], o.at[here + right, high], here + left)]
        pass_right.wait_recv()
        far += [send(7, a, o.at[there + left, low], o.at[there + left, low], here + right)]
        pass_left.wait_recv()
        far += [send(8, a, o.at[there + right, high], o.at[there + right, high], here + left)]
        done.append((far, (to_partner, to_right, to_left, pass_right, pass_left)))
    for far, near in done:
        for copy in far:
            copy.wait()
        for copy in near:
            copy.wait_send()
    for own in owns:
        own.wait()


def row_gather(arrays, collective_id):
    count = len(arrays)
    out = pl.pallas_call(
        functools.partial(row_gather_kernel, count),
        out_shape=[jax.ShapeDtypeStruct((8,) + x.shape, x.dtype) for x in arrays],
        in_specs=[pl.BlockSpec(memory_space=pl.ANY)] * count,
        out_specs=[pl.BlockSpec(memory_space=pl.ANY)] * count,
        scratch_shapes=[
            pltpu.SemaphoreType.DMA((count, 9)),
            pltpu.SemaphoreType.DMA((count, 9)),
            pltpu.SemaphoreType.DMA((count,)),
        ],
        compiler_params=pltpu.CompilerParams(collective_id=collective_id, has_side_effects=True),
        name="row_gather",
    )(*arrays)
    return out


def exchange(x):
    return lax.all_to_all(x, "tensor", 0, 0, tiled=False)


def dot(a, b, dims=((1,), (0,)), out=f32):
    return lax.dot_general(a, b, (dims, ((), ())), preferred_element_type=out)


def rms_scale(vector, scales):
    return vector * lax.rsqrt(jnp.mean(vector * vector, axis=-1, keepdims=True) + EPS) * scales


def rotate(vector, positions):
    half_width = vector.shape[-1] // 2
    frequency = ROTARY_BASE ** (-2.0 * jnp.arange(half_width, dtype=f32) / vector.shape[-1])
    angles = positions.astype(f32)[:, None, None] * frequency[None, None, :]
    cosine_part = jnp.cos(angles)
    sine_part = jnp.sin(angles)
    first_half = vector[..., :half_width]
    second_half = vector[..., half_width:]
    return jnp.concatenate(
        [
            first_half * cosine_part - second_half * sine_part,
            second_half * cosine_part + first_half * sine_part,
        ],
        axis=-1,
    )


def places(stream, seq_lengths):
    seq_ends = jnp.cumsum(seq_lengths)
    segment = jnp.sum((stream[:, None] >= seq_ends[None, :]).astype(jnp.int32), axis=1)
    owner_table = segment[:, None] == jnp.arange(seq_lengths.shape[0], dtype=jnp.int32)[None, :]
    seq_start = jnp.sum(jnp.where(owner_table, (seq_ends - seq_lengths)[None, :], 0), axis=1)
    return (segment, stream - seq_start)


def attend(query_low, key_low, value_low, segment, stream, scale):
    group_rows = query_low.shape[0]
    block_len = 512
    start_rows = jnp.arange(group_rows // block_len, dtype=jnp.int32) * block_len

    def forward_block(start_row):
        scores, _ = scores_for(query_low, key_low, segment, stream, scale, start_row, block_len)
        row_peak = jnp.max(scores, axis=-1, keepdims=True)
        exponent = jnp.exp(scores - row_peak)
        row_total = jnp.sum(exponent, axis=-1, keepdims=True)
        prob_low = (exponent / row_total).astype(bf16)
        mixed_block = jnp.einsum("rqs,sd->qrd", prob_low, value_low, preferred_element_type=f32)
        return (mixed_block.reshape(block_len, -1).astype(bf16), row_peak + jnp.log(row_total))

    mixed_blocks, log_totals = lax.map(forward_block, start_rows)
    return mixed_blocks.reshape(group_rows, -1), log_totals


def scores_for(query_low, key_low, segment, stream, scale, start_row, block_len):
    query_block = lax.dynamic_slice_in_dim(query_low, start_row, block_len, 0)
    seg_block = lax.dynamic_slice_in_dim(segment, start_row, block_len, 0)
    place_block = lax.dynamic_slice_in_dim(stream, start_row, block_len, 0)
    raw = jnp.einsum("qrd,sd->rqs", query_block, key_low, preferred_element_type=f32) * scale
    allowed = (seg_block[:, None] == segment[None, :]) & (stream[None, :] <= place_block[:, None])
    return (jnp.where(allowed[None], raw, MASKED), query_block)


def attend_back(query_low, key_low, value_low, segment, stream, scale, log_totals, mixed_grad):
    group_rows, heads, head_dim = query_low.shape
    block_len = 512
    start_rows = jnp.arange(group_rows // block_len, dtype=jnp.int32) * block_len

    def backward_block(totals, block_item):
        key_total, value_total = totals
        start_row, log_total = block_item
        scores, query_block = scores_for(
            query_low, key_low, segment, stream, scale, start_row, block_len
        )
        probability = jnp.exp(scores - log_total)
        prob_low = probability.astype(bf16)
        grad_block = lax.dynamic_slice_in_dim(mixed_grad, start_row, block_len, 0)
        value_total = value_total + jnp.einsum(
            "rqs,qrd->sd", prob_low, grad_block, preferred_element_type=f32
        )
        prob_grad = jnp.einsum("qrd,sd->rqs", grad_block, value_low, preferred_element_type=f32)
        inner_sum = jnp.sum(probability * prob_grad, axis=-1, keepdims=True)
        score_grad = (probability * (prob_grad - inner_sum)).astype(bf16)
        key_total = (
            key_total
            + jnp.einsum("rqs,qrd->sd", score_grad, query_block, preferred_element_type=f32)
            * scale
        )
        query_part = (
            jnp.einsum("rqs,sd->qrd", score_grad, key_low, preferred_element_type=f32) * scale
        )
        return ((key_total, value_total), query_part)

    zero = jnp.zeros((group_rows, head_dim), f32)
    (key_grad, value_grad), query_parts = lax.scan(
        backward_block, (zero, zero), (start_rows, log_totals)
    )
    return query_parts.reshape(group_rows, heads, head_dim), key_grad, value_grad


def per_device(
    tokens,
    lengths,
    token_order,
    routes,
    cotangent,
    attn_gain,
    ffn_gain,
    router,
    w_query,
    w_key,
    w_value,
    w_output,
    query_gain,
    key_gain,
    w_gate,
    w_up,
    w_down,
):
    rows, width = tokens.shape
    ranks = 8
    group_rows = rows * ranks
    experts, top_count = router.shape[1], routes.shape[1]
    local_experts, _, hidden_width = w_gate.shape
    head_local, kv_local, head_dim = query_gain.shape[0], key_gain.shape[0], 64
    dp_rows = w_query.shape[0]
    qkv_width = (head_local + 2 * kv_local) * head_dim
    scale = head_dim ** (-0.5)
    rank = lax.axis_index("tensor")

    wkv = jnp.concatenate([w_key, w_value], axis=1)
    small_own = jnp.concatenate([attn_gain[:, None], ffn_gain[:, None], router], axis=1)
    small_own = jnp.pad(small_own, ((0, 16 - small_own.shape[0]), (0, 128 - small_own.shape[1])))
    route_rows = routes.astype(bf16).reshape(-1, 128)
    payload = jnp.concatenate([w_query, wkv, w_output.T, small_own, route_rows], axis=0)
    gathered = tiny_gather(payload, 1)
    qkv_parts = gathered[:, : 2 * dp_rows].reshape(ranks, 2, dp_rows, 128)
    wqkv_cols = qkv_parts.transpose(2, 0, 1, 3).reshape(dp_rows, ranks * 256)
    wo_cols = gathered[:, 2 * dp_rows : 3 * dp_rows].transpose(1, 0, 2).reshape(dp_rows, -1)
    small_rows = gathered[:, 3 * dp_rows : 3 * dp_rows + 8].reshape(dp_rows, 128)
    routes_all = (
        gathered[:, 3 * dp_rows + 16 :].reshape(group_rows, top_count).astype(jnp.int32)
    )
    head_gains = jnp.concatenate([query_gain, key_gain], axis=0)
    head_gains = jnp.pad(head_gains, ((0, dp_rows - 3), (64, 60)))
    first_payload = jnp.concatenate([w_query, wkv, small_rows + head_gains], axis=1)
    first_full = lax.all_gather(first_payload, "dp", axis=0, tiled=False)
    wqkv = first_full[:, :, :256].reshape(width, 256)
    small_full = first_full[:, :, 256:].reshape(width, 128)
    gain1 = small_full[:, 0].astype(f32)
    gain2 = small_full[:, 1].astype(f32)
    router_full = small_full[:, 2 : 2 + experts]
    hg = first_full[:, :3, 256 + 64 : 256 + 68].transpose(1, 0, 2).reshape(3, head_dim)
    qgain, kgain = hg[:2].astype(f32), hg[2:].astype(f32)
    wo_t = lax.all_gather(wo_cols, "dp", axis=0, tiled=True)
    own_experts = jnp.concatenate([w_gate, w_up, w_down.transpose(0, 2, 1)], axis=0)
    expert_full = lax.all_gather(own_experts, "dp", axis=1, tiled=True)
    gate_w = expert_full[:local_experts]
    up_w = expert_full[local_experts : 2 * local_experts]
    down_t = expert_full[2 * local_experts :]

    tokens_all, cot_all = row_gather([tokens, cotangent], 2)
    inputs_all = tokens_all.reshape(group_rows, width).astype(f32)
    cot_all = cot_all.reshape(group_rows, width)
    scaled_all = inputs_all * lax.rsqrt(
        jnp.mean(inputs_all * inputs_all, axis=-1, keepdims=True) + EPS
    )
    normed_all = (scaled_all * gain1).astype(bf16)
    proj = dot(normed_all, wqkv)
    stream = token_order[0]
    segment, positions = places(stream, lengths[0])

    def prepare(query_in, key_in, query_scales, key_scales):
        return (
            rotate(
                rms_scale(query_in.reshape(group_rows, head_local, head_dim), query_scales),
                positions,
            ),
            rotate(
                rms_scale(key_in.reshape(group_rows, kv_local, head_dim), key_scales), positions
            ),
        )

    (query_rot, key_rot), prepare_pull = jax.vjp(
        prepare, proj[:, :128], proj[:, 128:192], qgain, kgain
    )
    query_low = query_rot.astype(bf16)
    key_low = key_rot.astype(bf16)[:, 0]
    value_low = proj[:, 192:].astype(bf16)
    mixed_low, log_totals = attend(query_low, key_low, value_low, segment, stream, scale)
    mixed_own = exchange(mixed_low.reshape(ranks, rows, 128)).transpose(1, 0, 2).reshape(rows, -1)
    hidden = tokens.astype(f32) + dot(mixed_own, wo_t, ((1,), (1,)))
    r2 = lax.rsqrt(jnp.mean(hidden * hidden, axis=-1, keepdims=True) + EPS)
    normed2 = (hidden * r2 * gain2).astype(bf16)

    (normed2_all,) = row_gather([normed2], 3)
    normed2_all = normed2_all.reshape(group_rows, width)
    logits = dot(normed2_all, router_full)
    named = jnp.any(routes_all[:, :, None] == jnp.arange(experts, dtype=jnp.int32), axis=1)
    gates_all = jax.nn.softmax(jnp.where(named, logits, MASKED), axis=-1)
    blocks = ranks
    own_named = lax.dynamic_slice_in_dim(named, rank * local_experts, local_experts, 1)
    own_gates = lax.dynamic_slice_in_dim(gates_all, rank * local_experts, local_experts, 1)
    own_named = own_named.reshape(blocks, rows, local_experts)
    slot_rank = jnp.cumsum(own_named.astype(jnp.int32), axis=1) - 1
    slot_rank = jnp.where(own_named, slot_rank, -1)
    table = (
        slot_rank.transpose(0, 2, 1)[:, :, None, :]
        == jnp.arange(CAP, dtype=jnp.int32)[None, None, :, None]
    )
    table_low = table.astype(bf16)
    slots = blocks * CAP
    x_slots = jnp.einsum(
        "besl,bld->ebsd",
        table_low,
        normed2_all.reshape(blocks, rows, width),
        preferred_element_type=bf16,
    ).reshape(local_experts, slots, width)
    u_slots = jnp.einsum(
        "besl,bld->ebsd",
        table_low,
        cot_all.reshape(blocks, rows, width),
        preferred_element_type=bf16,
    ).reshape(local_experts, slots, width)
    gate_slot = jnp.sum(
        jnp.where(
            table, own_gates.reshape(blocks, rows, -1).transpose(0, 2, 1)[:, :, None, :], 0.0
        ),
        axis=3,
    )
    gate_slot = gate_slot.transpose(1, 0, 2).reshape(local_experts, slots, 1)
    gate_act = jnp.einsum("erd,edf->erf", x_slots, gate_w, preferred_element_type=f32)
    up_act = jnp.einsum("erd,edf->erf", x_slots, up_w, preferred_element_type=f32)
    sig = 1.0 / (1.0 + jnp.exp(-gate_act))
    silu = gate_act * sig
    inner_low = (silu * up_act).astype(bf16)
    expert_out = jnp.einsum("erf,edf->erd", inner_low, down_t, preferred_element_type=f32)
    u_float = u_slots.astype(f32)
    gate_grad_slot = jnp.sum(u_float * expert_out, axis=2)
    weighted = (gate_slot * expert_out).astype(bf16).reshape(local_experts, blocks, CAP, width)
    out_part = jnp.einsum("besl,ebsd->bld", table_low, weighted, preferred_element_type=bf16)
    out_grad = (gate_slot * u_float).astype(bf16)
    inner_grad = jnp.einsum("erd,edf->erf", out_grad, down_t, preferred_element_type=f32)
    gate_act_grad = (inner_grad * up_act * sig * (1.0 + gate_act * (1.0 - sig))).astype(bf16)
    up_act_grad = (inner_grad * silu).astype(bf16)
    down_grad = jnp.einsum("erd,erf->edf", out_grad, inner_low, preferred_element_type=bf16)
    gate_w_grad = jnp.einsum("erd,erf->edf", x_slots, gate_act_grad, preferred_element_type=bf16)
    up_w_grad = jnp.einsum("erd,erf->edf", x_slots, up_act_grad, preferred_element_type=bf16)
    copy_grad = jnp.einsum("erf,edf->erd", gate_act_grad, gate_w, preferred_element_type=f32)
    copy_grad += jnp.einsum("erf,edf->erd", up_act_grad, up_w, preferred_element_type=f32)
    copy_low = copy_grad.astype(bf16).reshape(local_experts, blocks, CAP, width)
    copy_part = jnp.einsum("besl,ebsd->bld", table_low, copy_low, preferred_element_type=bf16)
    gate_grad_rows = jnp.sum(
        jnp.where(
            table,
            gate_grad_slot.reshape(local_experts, blocks, CAP).transpose(1, 0, 2)[..., None],
            0.0,
        ),
        axis=2,
    ).transpose(0, 2, 1)
    grad_hi = gate_grad_rows.astype(bf16)
    grad_lo = (gate_grad_rows - grad_hi.astype(f32)).astype(bf16)
    extra = jnp.concatenate([grad_hi, grad_lo], axis=2)
    extra = jnp.pad(extra, ((0, 0), (0, 0), (0, 128 - 2 * local_experts)))
    back = exchange(jnp.concatenate([copy_part, extra], axis=2))
    expert_sums = lax.psum_scatter(
        jnp.concatenate([gate_w_grad, up_w_grad, down_grad], axis=0),
        "dp",
        scatter_dimension=1,
        tiled=True,
    ).astype(f32)
    out_sum = jnp.sum(exchange(out_part).astype(f32), axis=0)
    layer_out = hidden + out_sum

    normed2_grad = jnp.sum(back[:, :, :width].astype(f32), axis=0)
    grad_pieces = back[:, :, width : width + local_experts].astype(f32)
    grad_pieces += back[:, :, width + local_experts : width + 2 * local_experts].astype(f32)
    gate_grad_own = grad_pieces.transpose(1, 0, 2).reshape(rows, experts)
    gates_own = lax.dynamic_slice_in_dim(gates_all, rank * rows, rows, 0)
    inner_sum = jnp.sum(gates_own * gate_grad_own, axis=1, keepdims=True)
    logit_grad = (gates_own * (gate_grad_own - inner_sum)).astype(bf16)
    normed2_grad = normed2_grad + dot(logit_grad, router_full, ((1,), (1,)))
    router_grad = dot(normed2, logit_grad, ((0,), (0,)))
    scaled2 = hidden * r2
    ffn_gain_grad = jnp.sum(normed2_grad * scaled2, axis=0)
    weighted_grad = normed2_grad * gain2
    upstream = cotangent.astype(f32)
    hidden_grad = upstream + r2 * (
        weighted_grad - scaled2 * jnp.mean(weighted_grad * scaled2, axis=-1, keepdims=True)
    )
    branch = hidden_grad.astype(bf16)
    mixed_grad_own = dot(branch, wo_t).astype(bf16)
    wo_grad = dot(branch, mixed_own, ((0,), (0,)), bf16)
    mixed_grad = exchange(mixed_grad_own.reshape(rows, ranks, 128).transpose(1, 0, 2))
    mixed_grad = mixed_grad.reshape(group_rows, head_local, head_dim)

    query_rot_grad, key_rot_grad, value_grad = attend_back(
        query_low, key_low, value_low, segment, stream, scale, log_totals, mixed_grad
    )
    query_grad, key_grad, qgain_grad, kgain_grad = prepare_pull(
        (query_rot_grad, key_rot_grad[:, None])
    )
    proj_grad = jnp.concatenate([query_grad, key_grad, value_grad], axis=1).astype(bf16)
    proj_grad_own = exchange(proj_grad.reshape(ranks, rows, qkv_width))
    wqkv_all = lax.all_gather(wqkv_cols, "dp", axis=0, tiled=True)
    normed_grad = dot(
        proj_grad_own.transpose(1, 0, 2).reshape(rows, -1), wqkv_all, ((1,), (1,))
    )
    wqkv_grad = dot(normed_all, proj_grad, ((0,), (0,)))
    inputs = tokens.astype(f32)
    r1 = lax.rsqrt(jnp.mean(inputs * inputs, axis=-1, keepdims=True) + EPS)
    scaled1 = inputs * r1
    attn_gain_grad = jnp.sum(normed_grad * scaled1, axis=0)
    weighted_grad = normed_grad * gain1
    grad_tokens = hidden_grad + r1 * (
        weighted_grad - scaled1 * jnp.mean(weighted_grad * scaled1, axis=-1, keepdims=True)
    )

    small_grad = jnp.concatenate(
        [attn_gain_grad[:, None], ffn_gain_grad[:, None], router_grad], axis=1
    )
    small_grad = jnp.pad(small_grad, ((0, 0), (0, 64 - small_grad.shape[1])))
    head_grads = jnp.concatenate([qgain_grad, kgain_grad], axis=0)
    head_grads = head_grads.reshape(3, 16, head_dim // 16).transpose(1, 0, 2)
    head_grads = jnp.pad(head_grads, ((0, 0), (0, dp_rows - 3), (0, 60))).reshape(width, 64)
    first_sums = lax.psum_scatter(
        jnp.concatenate([wqkv_grad, small_grad, head_grads], axis=1),
        "dp",
        scatter_dimension=0,
        tiled=True,
    )
    wo_sums = lax.psum_scatter(wo_grad, "dp", scatter_dimension=0, tiled=True)
    wo_pieces = exchange(wo_sums.reshape(dp_rows, ranks, 128).transpose(1, 0, 2))
    small_pieces = exchange(first_sums[:, 256:].reshape(ranks, 8, 128))
    grad_w_output = jnp.sum(wo_pieces.astype(f32), axis=0).T
    small_sums = jnp.sum(small_pieces[:, :, :64], axis=0)
    head_sums = first_sums[:3, 320:324]
    return (
        layer_out,
        grad_tokens,
        small_sums[:, 0],
        small_sums[:, 1],
        small_sums[:, 2 : 2 + experts],
        first_sums[:, :128],
        first_sums[:, 128:192],
        first_sums[:, 192:256],
        grad_w_output,
        head_sums[:2],
        head_sums[2:],
        expert_sums[:local_experts],
        expert_sums[local_experts : 2 * local_experts],
        expert_sums[2 * local_experts :].transpose(0, 2, 1),
    )


def solution(mesh):
    both = ("dp", "tensor")
    return jax.shard_map(
        per_device,
        mesh=mesh,
        in_specs=(
            P(both, None),
            P("dp", None),
            P("dp", None),
            P(both, None),
            P(both, None),
            P(both),
            P(both),
            P(both, None),
            P("dp", "tensor"),
            P("dp", "tensor"),
            P("dp", "tensor"),
            P("tensor", "dp"),
            P("tensor", "dp"),
            P("tensor", "dp"),
            P("tensor", "dp", None),
            P("tensor", "dp", None),
            P("tensor", None, "dp"),
        ),
        out_specs=(
            P(both, None),
            P(both, None),
            P(both),
            P(both),
            P(both, None),
            P("dp", "tensor"),
            P("dp", "tensor"),
            P("dp", "tensor"),
            P("tensor", "dp"),
            P("tensor", "dp"),
            P("tensor", "dp"),
            P("tensor", "dp", None),
            P("tensor", "dp", None),
            P("tensor", None, "dp"),
        ),
        check_vma=False,
    )
```

```python
import functools

import jax
import jax.numpy as jnp
from jax import lax
from jax.experimental import pallas as pl
from jax.experimental.pallas import tpu as pltpu
from jax.sharding import PartitionSpec as P

CAP = 80
EPS = 1e-06
ROTARY_BASE = 10000.0
MASKED = -1e30
ROW = 256
CHUNK = 512
RANKS = 8
GROUPS = 16
MESH = pl.DeviceIdType.MESH
bf16 = jnp.bfloat16
f32 = jnp.float32


def dot(a, b, dims=((1,), (0,)), out=f32):
    return lax.dot_general(a, b, (dims, ((), ())), preferred_element_type=out)


def lane(shape):
    return lax.broadcasted_iota(jnp.int32, shape, len(shape) - 1)


def sublane(shape):
    return lax.broadcasted_iota(jnp.int32, shape, len(shape) - 2)


def whole(n):
    return [pl.BlockSpec(memory_space=pltpu.VMEM) for _ in range(n)]


def anywhere(n):
    return [pl.BlockSpec(memory_space=pl.ANY) for _ in range(n)]


def meet(ranks, groups):
    barrier = pltpu.get_barrier_semaphore()
    for peer in ranks:
        pl.semaphore_signal(barrier, inc=1, device_id={"tensor": peer}, device_id_type=MESH)
    for peer in groups:
        pl.semaphore_signal(barrier, inc=1, device_id={"dp": peer}, device_id_type=MESH)
    pl.semaphore_wait(barrier, len(ranks) + len(groups))


def push(src, dst, sems, index, peer):
    copy = pltpu.make_async_remote_copy(
        src_ref=src,
        dst_ref=dst,
        send_sem=sems[0].at[index],
        recv_sem=sems[1].at[index],
        device_id=peer,
        device_id_type=MESH,
    )
    copy.start()
    return copy


def keep(src, dst, sem):
    copy = pltpu.make_async_copy(src, dst, sem)
    copy.start()
    return copy


def others(name, size):
    me = lax.axis_index(name)
    return [lax.rem(me + k, size) for k in range(1, size)]


def neighbours():
    me = lax.axis_index("tensor")
    z = lax.rem(me, 4)
    here = me - z
    there = 4 - here
    right, left = lax.rem(z + 1, 4), lax.rem(z + 3, 4)
    return me, here, there, there + z, right, left


def start_rows(x, o, sems):
    me, here, _, partner, right, left = neighbours()
    return (
        push(x, o.at[me], sems, 0, {"tensor": partner}),
        push(x, o.at[me], sems, 1, {"tensor": here + right}),
        push(x, o.at[me], sems, 2, {"tensor": here + left}),
    )


def pass_rows(first, o, sems):
    _, here, there, partner, right, left = neighbours()
    to_right, to_left = {"tensor": here + right}, {"tensor": here + left}
    half = o.shape[1] // 2
    low, high = pl.ds(0, half), pl.ds(half, half)
    to_partner, own_right, own_left = first

    def on(index, block, part, peer):
        return push(o.at[block, part], o.at[block, part], sems, index, peer)

    both = pl.ds(0, 2 * half)
    to_partner.wait_recv()
    pass_right = on(3, partner, both, to_right)
    pass_left = on(4, partner, both, to_left)
    own_right.wait_recv()
    far = [on(5, here + left, low, to_right)]
    own_left.wait_recv()
    far += [on(6, here + right, high, to_left)]
    pass_right.wait_recv()
    far += [on(7, there + left, low, to_right)]
    pass_left.wait_recv()
    far += [on(8, there + right, high, to_left)]
    for copy in far:
        copy.wait()
    for copy in (*first, pass_right, pass_left):
        copy.wait_send()


def group_place():
    group = lax.axis_index("dp")
    core, side, y = lax.rem(group, 2), lax.rem(group // 2, 2), group // 4
    across = {"dp": group + 2 - 4 * side}
    other = {"dp": group + 1 - 2 * core}
    column = [(lax.rem(y + k, 4), {"dp": lax.rem(y + k, 4) * 4 + side * 2 + core}) for k in (2, 1, 3)]
    return y, side, core, across, column, other


def gather_first(src, o, sems):
    y, side, core, across, _, _ = group_place()
    return push(src, o.at[y, side, core], sems, 0, across)


def gather_second(first, own, o, sems):
    y, _, core, _, column, _ = group_place()
    first.wait_recv()
    own.wait()
    part = o.at[y, :, core]
    return [push(part, part, sems, 1 + k, peer) for k, (_, peer) in enumerate(column)]


def gather_third(second, o, sems):
    _, _, core, _, _, other = group_place()
    for copy in second:
        copy.wait_recv()
    part = o.at[:, :, core]
    return push(part, part, sems, 4, other)


def opening_kernel(
    tokens, payload,
    tokens_all, tiny_all, first_all, rest_all,
    row_send, row_recv, tiny_send, tiny_recv, first_send, first_recv, rest_send, rest_recv, local,
):
    me = lax.axis_index("tensor")
    y, side, core, across, column, other = group_place()
    ranks = others("tensor", RANKS)
    meet(ranks, [across["dp"], other["dp"]] + [peer["dp"] for _, peer in column])
    tiny = [
        push(payload, tiny_all.at[me], (tiny_send, tiny_recv), k, {"tensor": peer})
        for k, peer in enumerate(ranks)
    ]
    first_sems, rest_sems = (first_send, first_recv), (rest_send, rest_recv)
    own = payload.at[pl.ds(0, 144)]
    first_one = gather_first(own, first_all, first_sems)
    rows = start_rows(tokens, tokens_all, (row_send, row_recv))
    tiny_own = keep(payload, tiny_all.at[me], local.at[0])
    first_own = keep(own, first_all.at[y, side, core], local.at[1])
    tokens_own = keep(tokens, tokens_all.at[me], local.at[2])
    first_two = gather_second(first_one, first_own, first_all, first_sems)
    for copy in tiny:
        copy.wait_recv()
    tiny_own.wait()
    part = tiny_all.at[:, pl.ds(128, 80)]
    rest_one = gather_first(part, rest_all, rest_sems)
    rest_own = keep(part, rest_all.at[y, side, core], local.at[3])
    first_three = gather_third(first_two, first_all, first_sems)
    rest_two = gather_second(rest_one, rest_own, rest_all, rest_sems)
    pass_rows(rows, tokens_all, (row_send, row_recv))
    rest_three = gather_third(rest_two, rest_all, rest_sems)
    first_three.wait()
    rest_three.wait()
    for copy in (*tiny, first_one, rest_one, *first_two, *rest_two):
        copy.wait_send()
    tokens_own.wait()


def opening(tokens, payload):
    dma = pltpu.SemaphoreType.DMA
    return pl.pallas_call(
        opening_kernel,
        out_shape=[
            jax.ShapeDtypeStruct((RANKS,) + tokens.shape, bf16),
            jax.ShapeDtypeStruct((RANKS,) + payload.shape, bf16),
            jax.ShapeDtypeStruct((4, 2, 2, 144, 128), bf16),
            jax.ShapeDtypeStruct((4, 2, 2, RANKS, 80, 128), bf16),
        ],
        in_specs=anywhere(2),
        out_specs=anywhere(4),
        scratch_shapes=[dma((9,)), dma((9,)), dma((7,)), dma((7,))] + [dma((5,))] * 4 + [dma((4,))],
        compiler_params=pltpu.CompilerParams(collective_id=1, has_side_effects=True),
        name="opening",
    )(tokens, payload)


def middle_kernel(
    mixed, rest, tokens, small,
    mixed_own, hidden, normed2_all,
    landed, normed2, mix_send, mix_recv, row_send, row_recv, local,
):
    me, here, _, partner, right, left = neighbours()
    ranks = others("tensor", RANKS)
    meet(ranks, [])
    sent = [
        push(mixed.at[peer], landed.at[me], (mix_send, mix_recv), k, {"tensor": peer})
        for k, peer in enumerate(ranks)
    ]
    own = keep(mixed.at[me], landed.at[me], local.at[0])
    for copy in sent:
        copy.wait_recv()
    own.wait()
    total = tokens[...].astype(f32)
    for s in range(RANKS):
        weight = rest[:, s, 16:80, :].reshape(-1, 128)
        total = total + dot(landed[s], weight, ((1,), (1,)))
    mixed_own[...] = landed[...]
    hidden[...] = total
    scale = lax.rsqrt(jnp.mean(total * total, axis=1, keepdims=True) + EPS)
    normed2[...] = (total * scale * small[1:2, :]).astype(bf16)
    rows = start_rows(normed2, normed2_all, (row_send, row_recv))
    kept = keep(normed2, normed2_all.at[me], local.at[1])
    pass_rows(rows, normed2_all, (row_send, row_recv))
    for copy in sent:
        copy.wait_send()
    kept.wait()


def middle(mixed, rest, tokens, small):
    dma = pltpu.SemaphoreType.DMA
    rows, width = tokens.shape
    return pl.pallas_call(
        middle_kernel,
        out_shape=[
            jax.ShapeDtypeStruct(mixed.shape, bf16),
            jax.ShapeDtypeStruct((rows, width), f32),
            jax.ShapeDtypeStruct((RANKS, rows, width), bf16),
        ],
        in_specs=whole(4),
        out_specs=whole(2) + anywhere(1),
        scratch_shapes=[
            pltpu.VMEM(mixed.shape, bf16),
            pltpu.VMEM((rows, width), bf16),
            dma((7,)),
            dma((7,)),
            dma((9,)),
            dma((9,)),
            dma((2,)),
        ],
        compiler_params=pltpu.CompilerParams(
            collective_id=2, has_side_effects=True, vmem_limit_bytes=40 << 20
        ),
        name="middle",
    )(mixed, rest, tokens, small)


def named_of(routes):
    picks = routes.astype(f32)
    picks = jnp.concatenate([picks[0:8], picks[8:16]], axis=1)
    expert = sublane((32, ROW)).astype(f32)
    found = jnp.zeros((32, ROW), f32)
    for k in range(8):
        found = jnp.where(picks[k : k + 1] == expert, 1.0, found)
    return found


def gates_of(named, logits):
    logits = jnp.where(named > 0.5, logits, MASKED)
    odds = jnp.where(named > 0.5, jnp.exp(logits - jnp.max(logits, axis=0, keepdims=True)), 0.0)
    return odds / jnp.sum(odds, axis=0, keepdims=True)


def norm_back(value, scales, grad):
    scale = lax.rsqrt(jnp.mean(value * value, axis=1, keepdims=True) + EPS)
    scaled = value * scale
    weighted = grad * scales
    moved = scale * (weighted - scaled * jnp.mean(weighted * scaled, axis=1, keepdims=True))
    return moved, scaled


def turn_kernel(
    back, hidden, cotangent, routes, small, mixed_own, rest,
    hidden_grad, mixed_grad, wo_grad, small_grad,
    leaving, landed, mix_send, mix_recv, local,
):
    me = lax.axis_index("tensor")
    ranks = others("tensor", RANKS)
    meet(ranks, [])
    value = hidden[...]
    gain = small[1:2, :]
    router = small[8:40, :].astype(bf16)
    scale = lax.rsqrt(jnp.mean(value * value, axis=1, keepdims=True) + EPS)
    normed2 = (value * scale * gain).astype(bf16)
    gates = gates_of(named_of(routes[...]), dot(router, normed2, ((1,), (1,))))
    pieces = back[:, ROW : ROW + 16, 0 : 2 * ROW].reshape(RANKS * 16, 2 * ROW)
    order = lane((32, RANKS * 16))
    expert = order // 16 * 4 + order % 16
    spread = jnp.where((expert == sublane(order.shape)) & (order % 16 < 4), 1.0, 0.0).astype(bf16)
    pieces = dot(spread, pieces)
    gate_grad = pieces[:, :ROW] + pieces[:, ROW:]
    inner = jnp.sum(gates * gate_grad, axis=0, keepdims=True)
    logit_grad = (gates * (gate_grad - inner)).astype(bf16)
    grad = dot(logit_grad, router, ((0,), (0,)))
    for s in range(RANKS):
        grad = grad + back[s, 0:ROW, :].astype(f32)
    moved, scaled = norm_back(value, gain, grad)
    total = cotangent[...].astype(f32) + moved
    branch = total.astype(bf16)
    for s in range(RANKS):
        weight = rest[:, s, 16:80, :].reshape(-1, 128)
        leaving[s] = dot(branch, weight).astype(bf16)
    sent = [
        push(leaving.at[peer], landed.at[me], (mix_send, mix_recv), k, {"tensor": peer})
        for k, peer in enumerate(ranks)
    ]
    own = keep(leaving.at[me], landed.at[me], local.at[0])
    hidden_grad[...] = total
    small_grad[0:8, :] = jnp.broadcast_to(
        jnp.sum(grad * scaled, axis=0, keepdims=True), (8, grad.shape[1])
    )
    small_grad[8:40, :] = dot(logit_grad, normed2)
    for s in range(RANKS):
        part = dot(branch, mixed_own[s], ((0,), (0,)))
        wo_grad[:, s] = part.astype(bf16).reshape(GROUPS, -1, 128)
    for copy in sent:
        copy.wait()
    own.wait()
    mixed_grad[...] = landed[...]


def turn(back, hidden, cotangent, routes, small, mixed_own, rest):
    dma = pltpu.SemaphoreType.DMA
    rows, width = hidden.shape
    return pl.pallas_call(
        turn_kernel,
        out_shape=[
            jax.ShapeDtypeStruct((rows, width), f32),
            jax.ShapeDtypeStruct(mixed_own.shape, bf16),
            jax.ShapeDtypeStruct((GROUPS, RANKS, width // GROUPS, 128), bf16),
            jax.ShapeDtypeStruct((40, width), f32),
        ],
        in_specs=whole(7),
        out_specs=whole(4),
        scratch_shapes=[
            pltpu.VMEM(mixed_own.shape, bf16),
            pltpu.VMEM(mixed_own.shape, bf16),
            dma((7,)),
            dma((7,)),
            dma((1,)),
        ],
        compiler_params=pltpu.CompilerParams(
            collective_id=3, has_side_effects=True, vmem_limit_bytes=48 << 20
        ),
        name="turn",
    )(back, hidden, cotangent, routes, small, mixed_own, rest)


def closing_kernel(
    proj_grad, wide, small_grad, wqkv_all, tokens, small, hidden_grad,
    grad_tokens, wqkv_sum, wo_sum, small_sum, head_sum,
    proj_in, wide_core, wide_y, wide_x, small_core, small_y, small_x,
    wide_half, wide_pair, small_half, small_pair, wo_out, small_out, wo_last, small_last,
    proj_send, proj_recv, wide_send, wide_recv, small_send, small_recv, last_send, last_recv, local,
):
    me = lax.axis_index("tensor")
    y, side, core, across, column, other = group_place()
    ranks = others("tensor", RANKS)
    meet(ranks, [across["dp"], other["dp"]] + [peer["dp"] for _, peer in column])
    wide_sems, small_sems = (wide_send, wide_recv), (small_send, small_recv)
    away = 1 - core
    first = [
        push(wide.at[:, :, away], wide_core, wide_sems, 0, other),
        push(small_grad.at[:, :, away], small_core, small_sems, 0, other),
    ]
    proj = [
        push(proj_grad.at[peer], proj_in.at[me], (proj_send, proj_recv), k, {"tensor": peer})
        for k, peer in enumerate(ranks)
    ]
    proj_own = keep(proj_grad.at[me], proj_in.at[me], local.at[0])
    for copy in first:
        copy.wait_recv()
    wide_half[...] = (wide[:, :, core].astype(f32) + wide_core[...].astype(f32)).astype(bf16)
    small_half[...] = small_grad[:, :, core] + small_core[...]
    second = []
    for k, (at, peer) in enumerate(column):
        second.append(push(wide_half.at[at], wide_y.at[k], wide_sems, 1 + k, peer))
        second.append(push(small_half.at[at], small_y.at[k], small_sems, 1 + k, peer))
    for copy in second:
        copy.wait_recv()
    total = wide_half[y].astype(f32)
    small_total = small_half[y]
    for k in range(3):
        total = total + wide_y[k].astype(f32)
        small_total = small_total + small_y[k]
    wide_pair[...] = total.astype(bf16)
    small_pair[...] = small_total
    third = [
        push(wide_pair.at[1 - side], wide_x, wide_sems, 4, across),
        push(small_pair.at[1 - side], small_x, small_sems, 4, across),
    ]
    for copy in proj:
        copy.wait_recv()
    proj_own.wait()
    grad = jnp.zeros(grad_tokens.shape, f32)
    for s in range(RANKS):
        query = wqkv_all[:, s, 0:64, :].reshape(-1, 128)
        rest = wqkv_all[:, s, 64:128, :].reshape(-1, 128)
        grad = grad + dot(proj_in[s, :, 0:128], query, ((1,), (1,)))
        grad = grad + dot(proj_in[s, :, 128:256], rest, ((1,), (1,)))
    moved, _ = norm_back(tokens[...].astype(f32), small[0:1, :], grad)
    grad_tokens[...] = hidden_grad[...] + moved
    for copy in third:
        copy.wait_recv()
    total = wide_pair[side].astype(f32) + wide_x[...].astype(f32)
    small_total = small_pair[side] + small_x[...]
    wo_out[...] = total[:RANKS].astype(bf16)
    wqkv_sum[:, 0:128] = total[RANKS]
    wqkv_sum[:, 128:256] = total[RANKS + 1]
    head_sum[...] = small_total[0:8]
    small_out[...] = small_total.reshape(small_out.shape)
    last = []
    for a, (src, dst) in enumerate(((wo_out, wo_last), (small_out, small_last))):
        sems = last_send.at[a], last_recv.at[a]
        last += [
            push(src.at[peer], dst.at[me], sems, k, {"tensor": peer}) for k, peer in enumerate(ranks)
        ]
    kept = [
        keep(wo_out.at[me], wo_last.at[me], local.at[1]),
        keep(small_out.at[me], small_last.at[me], local.at[2]),
    ]
    for copy in last:
        copy.wait_recv()
    for copy in kept:
        copy.wait()
    total = jnp.zeros(wo_sum.shape, f32)
    small_total = jnp.zeros(small_sum.shape, f32)
    for s in range(RANKS):
        total = total + wo_last[s].astype(f32)
        small_total = small_total + small_last[s]
    wo_sum[...] = total
    small_sum[...] = small_total
    for copy in (*proj, *first, *second, *third, *last):
        copy.wait_send()


def closing(proj_grad, wide, small_grad, wqkv_all, tokens, small, hidden_grad):
    dma = pltpu.SemaphoreType.DMA
    block, shard = wide.shape[3:], wide.shape[4]
    rows = shard // RANKS
    return pl.pallas_call(
        closing_kernel,
        out_shape=[
            jax.ShapeDtypeStruct(hidden_grad.shape, f32),
            jax.ShapeDtypeStruct((shard, 256), f32),
            jax.ShapeDtypeStruct((shard, 128), f32),
            jax.ShapeDtypeStruct((rows, 128), f32),
            jax.ShapeDtypeStruct((8, 128), f32),
        ],
        in_specs=whole(7),
        out_specs=whole(5),
        scratch_shapes=[
            pltpu.VMEM(proj_grad.shape, bf16),
            pltpu.VMEM((4, 2) + block, bf16),
            pltpu.VMEM((3, 2) + block, bf16),
            pltpu.VMEM(block, bf16),
            pltpu.VMEM((4, 2, shard, 128), f32),
            pltpu.VMEM((3, 2, shard, 128), f32),
            pltpu.VMEM((shard, 128), f32),
            pltpu.VMEM((4, 2) + block, bf16),
            pltpu.VMEM((2,) + block, bf16),
            pltpu.VMEM((4, 2, shard, 128), f32),
            pltpu.VMEM((2, shard, 128), f32),
            pltpu.VMEM((RANKS, shard, 128), bf16),
            pltpu.VMEM((RANKS, rows, 128), f32),
            pltpu.VMEM((RANKS, shard, 128), bf16),
            pltpu.VMEM((RANKS, rows, 128), f32),
            dma((7,)),
            dma((7,)),
            dma((5,)),
            dma((5,)),
            dma((5,)),
            dma((5,)),
            dma((2, 7)),
            dma((2, 7)),
            dma((3,)),
        ],
        compiler_params=pltpu.CompilerParams(
            collective_id=4, has_side_effects=True, vmem_limit_bytes=48 << 20
        ),
        name="closing",
    )(proj_grad, wide, small_grad, wqkv_all, tokens, small, hidden_grad)


def sequence_start(place, lengths):
    first, second = lengths[0], lengths[0] + lengths[1]
    return jnp.where(place < first, 0, jnp.where(place < second, first, second))


def swap_halves(x):
    return jnp.where(lane(x.shape) % 64 < 32, pltpu.roll(x, 96, 1), pltpu.roll(x, 32, 1))


def head_mean(x, heads):
    low = lane(x.shape) < 64
    first = jnp.sum(jnp.where(low, x, 0.0), axis=1, keepdims=True) / 64
    if heads == 1:
        return jnp.where(low, first, 0.0)
    second = jnp.sum(jnp.where(low, 0.0, x), axis=1, keepdims=True) / 64
    return jnp.where(low, first, second)


def head_gains(first_all):
    total = jnp.zeros((8, 128), f32)
    for g in range(GROUPS):
        piece = first_all[g, 128:144, :].astype(f32)[8:16]
        total = total + pltpu.roll(jnp.where(lane(piece.shape) < 4, piece, 0.0), 4 * g, 1)
    low = lane((1, 128)) < 64
    return jnp.where(low, total[0:1], pltpu.roll(total[1:2], 64, 1)), total[2:3]


def turned(table, block, b):
    within_cos, within_sin = table[0], table[1]
    block_cos, block_sin = block[0, pl.ds(b, 1), :], block[1, pl.ds(b, 1), :]
    cos = within_cos * block_cos - within_sin * block_sin
    sin = within_sin * block_cos + within_cos * block_sin
    return cos, jnp.where(lane(sin.shape) % 64 < 32, -sin, sin)


def attend_kernel(
    lengths, x, small, first_all, table, block, order_row, order_col,
    normed, proj, stream_qkv, mixed_stream, log_total, mixed, wqkv,
    token_qkv, keys, values,
):
    rows = x.shape[0]
    blocks = rows // ROW
    q_gain, k_gain = head_gains(first_all)
    wqkv[:, 0:128] = first_all[:, 0:64, :].reshape(-1, 128)
    wqkv[:, 128:256] = first_all[:, 64:128, :].reshape(-1, 128)

    @pl.loop(0, blocks)
    def _(b):
        at = pl.ds(pl.multiple_of(b * ROW, ROW), ROW)
        v = x[at, :].astype(f32)
        r = lax.rsqrt(jnp.mean(v * v, axis=1, keepdims=True) + EPS)
        n = (v * r * small[0:1, :]).astype(bf16)
        normed[at, :] = n
        p = dot(n, wqkv[...])
        proj[at, :] = p
        q, kv = p[:, :128], p[:, 128:]
        low = lane(kv.shape) < 64
        q = q * lax.rsqrt(head_mean(q * q, 2) + EPS) * q_gain
        k = kv * lax.rsqrt(head_mean(kv * kv, 1) + EPS) * k_gain
        token_qkv[at, 0:128] = q.astype(bf16)
        token_qkv[at, 128:256] = jnp.where(low, k, kv).astype(bf16)

    @pl.loop(0, blocks)
    def _(b):
        at = pl.ds(pl.multiple_of(b * ROW, ROW), ROW)
        place = sublane((ROW, rows)) + b * ROW
        moves = jnp.where(order_row[...] == place, 1.0, 0.0).astype(bf16)
        moved = dot(moves, token_qkv[...])
        cos, sin = turned(table, block, b)
        q, kv = moved[:, :128], moved[:, 128:]
        low = lane(kv.shape) < 64
        q = (q * cos + swap_halves(q) * sin) * 0.125
        kv = jnp.where(low, kv * cos + swap_halves(kv) * sin, kv)
        stream_qkv[at, 0:128] = q.astype(bf16)
        stream_qkv[at, 128:256] = kv.astype(bf16)
        other = pltpu.roll(kv, 64, 1)
        keys[at, :] = jnp.where(low, kv, other).astype(bf16)
        values[at, :] = jnp.where(low, other, 1.0).astype(bf16)

    @pl.loop(0, blocks)
    def _(b):
        at = pl.ds(pl.multiple_of(b * ROW, ROW), ROW)
        q = stream_qkv[at, 0:128]
        low = lane(q.shape) < 64
        zero = jnp.zeros_like(q)
        q0, q1 = jnp.where(low, q, zero), jnp.where(low, zero, q)
        place = sublane((ROW, 1)) + b * ROW
        start = sequence_start(place, lengths)
        first = sequence_start(b * ROW, lengths) // CHUNK
        last = (b * ROW + ROW - 1) // CHUNK + 1

        def step(j, totals):
            t0, t1 = totals
            here = pl.ds(pl.multiple_of(j * CHUNK, CHUNK), CHUNK)
            k, v = keys[here, :], values[here, :]
            key = lane((ROW, CHUNK)) + j * CHUNK
            allowed = (key <= place) & (key >= start)
            e0 = jnp.where(allowed, jnp.exp(dot(q0, k, ((1,), (1,)))), 0.0).astype(bf16)
            e1 = jnp.where(allowed, jnp.exp(dot(q1, k, ((1,), (1,)))), 0.0).astype(bf16)
            return t0 + dot(e0, v), t1 + dot(e1, v)

        none = jnp.zeros((ROW, 128), f32)
        t0, t1 = lax.fori_loop(first, last, step, (none, none))
        low = lane((ROW, 128)) < 64
        other0, other1 = pltpu.roll(t0, 64, 1), pltpu.roll(t1, 64, 1)
        total = jnp.where(low, other0, t1)
        out = jnp.where(low, t0, other1) / total
        log_total[at, :] = jnp.log(total)
        mixed_stream[at, :] = out.astype(bf16)

    @pl.loop(0, blocks)
    def _(b):
        at = pl.ds(pl.multiple_of(b * ROW, ROW), ROW)
        moves = jnp.where(order_col[at, :] == lane((ROW, rows)), 1.0, 0.0).astype(bf16)
        mixed[at, :] = dot(moves, mixed_stream[...]).astype(bf16)


def attend(lengths, x, small, first_all, table, block, order_row, order_col):
    rows, width = x.shape
    return pl.pallas_call(
        attend_kernel,
        out_shape=[
            jax.ShapeDtypeStruct((rows, width), bf16),
            jax.ShapeDtypeStruct((rows, 256), f32),
            jax.ShapeDtypeStruct((rows, 256), bf16),
            jax.ShapeDtypeStruct((rows, 128), bf16),
            jax.ShapeDtypeStruct((rows, 128), f32),
            jax.ShapeDtypeStruct((rows, 128), bf16),
            jax.ShapeDtypeStruct((width, 256), bf16),
        ],
        in_specs=[pl.BlockSpec(memory_space=pltpu.SMEM)] + whole(7),
        out_specs=whole(7),
        scratch_shapes=[
            pltpu.VMEM((rows, 256), bf16),
            pltpu.VMEM((rows, 128), bf16),
            pltpu.VMEM((rows, 128), bf16),
        ],
        compiler_params=pltpu.CompilerParams(vmem_limit_bytes=56 << 20),
        cost_estimate=pl.CostEstimate(flops=1000, bytes_accessed=1000, transcendentals=0),
        name="attend",
    )(lengths, x, small, first_all, table, block, order_row, order_col)


def attend_back_kernel(
    lengths, mixed_grad, stream_qkv, mixed_stream, log_total, proj, first_all, table, block,
    order_row, order_col, normed, wqkv, small, turn_grad,
    proj_grad, wqkv_grad, small_grad,
    gain_grad, keys, values, out_grad, query_grad, key_grad, value_grad, attn_gain,
):
    rows = proj.shape[0]
    blocks = rows // ROW
    q_gain, k_gain = head_gains(first_all)
    key_grad[...] = jnp.zeros_like(key_grad)
    value_grad[...] = jnp.zeros_like(value_grad)

    @pl.loop(0, blocks)
    def _(b):
        at = pl.ds(pl.multiple_of(b * ROW, ROW), ROW)
        place = sublane((ROW, rows)) + b * ROW
        moves = jnp.where(order_row[...] == place, 1.0, 0.0).astype(bf16)
        out_grad[at, :] = dot(moves, mixed_grad[...]).astype(bf16)
        kv = stream_qkv[at, 128:256].astype(f32)
        low = lane(kv.shape) < 64
        other = pltpu.roll(kv, 64, 1)
        keys[at, :] = jnp.where(low, kv, other).astype(bf16)
        values[at, :] = jnp.where(low, other, kv).astype(bf16)

    @pl.loop(0, blocks)
    def _(b):
        at = pl.ds(pl.multiple_of(b * ROW, ROW), ROW)
        q, g = stream_qkv[at, 0:128], out_grad[at, :]
        low = lane(q.shape) < 64
        zero = jnp.zeros_like(q)
        qs = jnp.where(low, q, zero), jnp.where(low, zero, q)
        gs = jnp.where(low, g, zero), jnp.where(low, zero, g)
        product = jnp.transpose(g.astype(f32) * mixed_stream[at, :].astype(f32))
        inner = (
            jnp.sum(product[:64], axis=0, keepdims=True),
            jnp.sum(product[64:], axis=0, keepdims=True),
        )
        logs = jnp.transpose(log_total[at, :])
        logs = logs[0:1], logs[64:65]
        place = lane((1, ROW)) + b * ROW
        start = sequence_start(place, lengths)
        first = sequence_start(b * ROW, lengths) // CHUNK
        last = (b * ROW + ROW - 1) // CHUNK + 1

        def step(j, totals):
            here = pl.ds(pl.multiple_of(j * CHUNK, CHUNK), CHUNK)
            k, v = keys[here, :], values[here, :]
            key = sublane((CHUNK, ROW)) + j * CHUNK
            allowed = (key <= place) & (key >= start)
            done = []
            kt, vt = key_grad[here, :], value_grad[here, :]
            for h in range(2):
                p = jnp.exp(dot(k, qs[h], ((1,), (1,))) - logs[h])
                p = jnp.where(allowed, p, 0.0)
                d = p * (dot(v, gs[h], ((1,), (1,))) - inner[h])
                p, d = p.astype(bf16), d.astype(bf16)
                vt = vt + dot(p, gs[h])
                kt = kt + dot(d, qs[h])
                done.append(totals[h] + dot(k, d, ((0,), (0,))))
            key_grad[here, :] = kt
            value_grad[here, :] = vt
            return tuple(done)

        none = jnp.zeros((128, ROW), f32)
        t0, t1 = lax.fori_loop(first, last, step, (none, none))
        grad = jnp.where(sublane((128, ROW)) < 64, t0, t1) * 0.125
        cos, sin = turned(table, block, b)
        cos, sin = jnp.transpose(cos), jnp.transpose(sin)
        swapped = jnp.concatenate([grad[32:64], grad[0:32], grad[96:128], grad[64:96]], axis=0)
        query_grad[:, at] = (grad * cos - swapped * sin).astype(bf16)

    gain_grad[...] = jnp.zeros_like(gain_grad)
    attn_gain[...] = jnp.zeros_like(attn_gain)

    @pl.loop(0, blocks)
    def _(b):
        at = pl.ds(pl.multiple_of(b * ROW, ROW), ROW)
        key, value = key_grad[at, :], value_grad[at, :]
        low = lane(key.shape) < 64
        key = key + pltpu.roll(key, 64, 1)
        cos, sin = turned(table, block, b)
        key = key * cos - swap_halves(key) * sin
        keys[at, :] = jnp.where(low, key, value + pltpu.roll(value, 64, 1)).astype(bf16)

    @pl.loop(0, blocks)
    def _(b):
        at = pl.ds(pl.multiple_of(b * ROW, ROW), ROW)
        moves = jnp.where(order_col[at, :] == lane((ROW, rows)), 1.0, 0.0).astype(bf16)
        dq = dot(moves, query_grad[...], ((1,), (1,)))
        dkv = dot(moves, keys[...])

        def back(grad, value, scales, heads):
            r = lax.rsqrt(head_mean(value * value, heads) + EPS)
            scaled = value * r
            weighted = grad * scales
            result = r * (weighted - scaled * head_mean(weighted * scaled, heads))
            return result, jnp.sum(grad * scaled, axis=0, keepdims=True)

        q_result, q_sum = back(dq, proj[at, 0:128], q_gain, 2)
        k_result, k_sum = back(dkv, proj[at, 128:256], k_gain, 1)
        q_low = q_result.astype(bf16)
        k_low = jnp.where(lane(dkv.shape) < 64, k_result, dkv).astype(bf16)
        proj_grad[at, 0:128] = q_low
        proj_grad[at, 128:256] = k_low
        gain_grad[0:1, :] += q_sum
        gain_grad[1:2, :] += k_sum
        part = dot(jnp.concatenate([q_low, k_low], axis=1), wqkv[...], ((1,), (1,)))
        part = part * normed[at, :].astype(f32)
        attn_gain[0:1, :] += jnp.sum(part, axis=0, keepdims=True)

    @pl.loop(0, normed.shape[1] // 256)
    def _(c):
        at = pl.ds(pl.multiple_of(c * 256, 256), 256)
        part = dot(normed[:, at], proj_grad[...], ((0,), (0,))).astype(bf16)
        own = pl.ds(c * 4, 4)
        wqkv_grad[own, 0] = part[:, 0:128].reshape(4, 64, 128)
        wqkv_grad[own, 1] = part[:, 128:256].reshape(4, 64, 128)

    heads = gain_grad[...]
    low = lane(heads.shape) < 64
    heads = jnp.concatenate(
        [
            jnp.where(low[0:1], heads[0:1], 0.0),
            jnp.where(low[0:1], pltpu.roll(heads[0:1], 64, 1), 0.0),
            jnp.where(low[0:1], heads[1:2], 0.0),
            jnp.zeros((5, 128), f32),
        ],
        axis=0,
    )
    spots = []
    for pair in range(GROUPS // 2):
        even = pltpu.roll(heads, (128 - 8 * pair) % 128, 1)
        odd = pltpu.roll(heads, (188 - 8 * pair) % 128, 1)
        at = lane(heads.shape)
        spots.append(jnp.where(at < 4, even, jnp.where((at >= 64) & (at < 68), odd, 0.0)))
    lines = [turn_grad[...], attn_gain[...] / small[0:1, :], jnp.concatenate(spots, axis=1)]
    lines.append(jnp.zeros((128 - 56, small.shape[1]), f32))
    small_grad[...] = jnp.transpose(jnp.concatenate(lines, axis=0))


def attend_back(
    lengths, mixed_grad, stream_qkv, mixed_stream, log_total, proj, first_all, table, block,
    order_row, order_col, normed, wqkv, small, turn_grad,
):
    rows, width = normed.shape
    return pl.pallas_call(
        attend_back_kernel,
        out_shape=[
            jax.ShapeDtypeStruct((rows, 256), bf16),
            jax.ShapeDtypeStruct((GROUPS, 2, width // GROUPS, 128), bf16),
            jax.ShapeDtypeStruct((width, 128), f32),
        ],
        in_specs=[pl.BlockSpec(memory_space=pltpu.SMEM)] + whole(14),
        out_specs=whole(3),
        scratch_shapes=[
            pltpu.VMEM((8, 128), f32),
            pltpu.VMEM((rows, 128), bf16),
            pltpu.VMEM((rows, 128), bf16),
            pltpu.VMEM((rows, 128), bf16),
            pltpu.VMEM((128, rows), bf16),
            pltpu.VMEM((rows, 128), f32),
            pltpu.VMEM((rows, 128), f32),
            pltpu.VMEM((8, width), f32),
        ],
        compiler_params=pltpu.CompilerParams(vmem_limit_bytes=56 << 20),
        cost_estimate=pl.CostEstimate(flops=1000, bytes_accessed=1000, transcendentals=0),
        name="attend_back",
    )(
        lengths, mixed_grad, stream_qkv, mixed_stream, log_total, proj, first_all, table, block,
        order_row, order_col, normed, wqkv, small, turn_grad,
    )


def experts_kernel(
    rank, rows_in, cot_in, routes, small, w,
    out_part, copy_part, wg,
    xs, us, weights, grads, x_buf, u_buf, og_s, inner_s, dgu_s, ranks, sem,
):
    e = pl.program_id(0)
    experts = pl.num_programs(0)
    blocks, held, width = xs.shape
    hidden = inner_s.shape[1]
    local = held // CAP

    def fetch(b, slot):
        return (
            pltpu.make_async_copy(rows_in.at[b], x_buf.at[slot], sem.at[0, slot]),
            pltpu.make_async_copy(cot_in.at[b], u_buf.at[slot], sem.at[1, slot]),
        )

    def table_of(b, i):
        slot = sublane((CAP, ROW))
        return ranks[b, pl.ds(i, 1), :] == slot

    @pl.when(e == 0)
    def _():
        for copy in fetch(0, 0):
            copy.start()
        pick = sublane((8, 32)) + rank[0] * local == lane((8, 32))
        pick = jnp.where(pick & (sublane((8, 32)) < local), 1.0, 0.0)
        before = jnp.where(sublane((ROW, ROW)) < lane((ROW, ROW)), 1.0, 0.0).astype(bf16)
        router = small[8:40, :].astype(bf16)

        @pl.loop(0, blocks)
        def _(b):
            slot = lax.rem(b, 2)

            @pl.when(b + 1 < blocks)
            def _():
                for copy in fetch(b + 1, 1 - slot):
                    copy.start()

            for copy in fetch(b, slot):
                copy.wait()
            x = x_buf[slot]
            named = named_of(routes[b])
            gates = gates_of(named, dot(router, x, ((1,), (1,))))
            own = lax.dot_general(
                pick,
                gates,
                (((1,), (0,)), ((), ())),
                precision=lax.Precision.HIGHEST,
                preferred_element_type=f32,
            )
            place = jnp.where(named > 0.5, dot(named.astype(bf16), before), -1.0)
            place = dot(pick.astype(bf16), place.astype(bf16))
            ranks[b] = place.astype(jnp.int32)
            u = u_buf[slot]
            for i in range(local):
                hit = table_of(b, i)
                table = jnp.where(hit, 1.0, 0.0).astype(bf16)
                here = pl.ds(i * CAP, CAP)
                xs[b, here, :] = dot(table, x).astype(bf16)
                us[b, here, :] = dot(table, u).astype(bf16)
                gate = jnp.sum(jnp.where(hit, own[i : i + 1], 0.0), axis=1, keepdims=True)
                weights[b, here, :] = jnp.broadcast_to(gate, (CAP, 128))

    group = blocks // 2
    tile = group * CAP

    @pl.loop(0, 2)
    def _(t):
        part = pl.ds(t * group, group)
        here = pl.ds(pl.multiple_of(e * CAP, CAP), CAP)
        flat = pl.ds(pl.multiple_of(t * tile, tile), tile)
        x = xs[part, here, :].reshape(tile, width)
        u = us[part, here, :].reshape(tile, width).astype(f32)
        gate = weights[part, here, :].reshape(tile, 128)[:, 0:1]
        gate_act = dot(x, w[0, 0])
        up_act = dot(x, w[0, 1])
        sig = 1.0 / (1.0 + jnp.exp(-gate_act))
        silu = gate_act * sig
        inner = (silu * up_act).astype(bf16)
        inner_s[flat, :] = inner
        result = dot(inner, w[0, 2], ((1,), (1,)))
        grad = jnp.sum(u * result, axis=1, keepdims=True)
        grads[part, here, :] = jnp.broadcast_to(grad, (tile, 128)).reshape(group, CAP, 128)
        us[part, here, :] = (gate * result).astype(bf16).reshape(group, CAP, width)
        og = (gate * u).astype(bf16)
        og_s[flat, :] = og
        inner_grad = dot(og, w[0, 2])
        dg = (inner_grad * up_act * (sig * (1.0 + gate_act * (1.0 - sig)))).astype(bf16)
        du = (inner_grad * silu).astype(bf16)
        dgu_s[flat, 0:hidden] = dg
        dgu_s[flat, hidden : 2 * hidden] = du

    col = 256

    @pl.loop(0, width // col)
    def _(c):
        at = pl.ds(pl.multiple_of(c * col, col), col)
        here = pl.ds(pl.multiple_of(e * CAP, CAP), CAP)
        x = xs[:, here, at].reshape(blocks * CAP, col)
        both = dot(x, dgu_s[...], ((0,), (0,)))
        wg[0, 0, at, :] = both[:, :hidden].astype(bf16)
        wg[0, 1, at, :] = both[:, hidden:].astype(bf16)
        wg[0, 2, at, :] = dot(og_s[:, at], inner_s[...], ((0,), (0,))).astype(bf16)

    @pl.loop(0, 2)
    def _(t):
        part = pl.ds(t * group, group)
        here = pl.ds(pl.multiple_of(e * CAP, CAP), CAP)
        flat = pl.ds(pl.multiple_of(t * tile, tile), tile)
        copy_grad = dot(dgu_s[flat, 0:hidden], w[0, 0], ((1,), (1,)))
        copy_grad += dot(dgu_s[flat, hidden : 2 * hidden], w[0, 1], ((1,), (1,)))
        xs[part, here, :] = copy_grad.astype(bf16).reshape(group, CAP, width)

    @pl.when(e == experts - 1)
    def _():
        def leave(b, slot):
            return (
                pltpu.make_async_copy(
                    x_buf.at[slot], copy_part.at[b, pl.ds(0, ROW)], sem.at[0, slot]
                ),
                pltpu.make_async_copy(u_buf.at[slot], out_part.at[b], sem.at[1, slot]),
            )

        def extra(b, slot):
            return pltpu.make_async_copy(
                og_s.at[pl.ds(slot * 16, 16)], copy_part.at[b, pl.ds(ROW, 16)], sem.at[2, slot]
            )

        @pl.loop(0, blocks)
        def _(b):
            slot = lax.rem(b, 2)

            @pl.when(b >= 2)
            def _():
                for copy in leave(b - 2, slot):
                    copy.wait()
                extra(b - 2, slot).wait()

            tables, lines = [], []
            for i in range(local):
                hit = table_of(b, i)
                tables.append(jnp.where(hit, 1.0, 0.0).astype(bf16))
                column = grads[b, pl.ds(i * CAP, CAP), :][:, 0:1]
                lines.append(jnp.sum(jnp.where(hit, column, 0.0), axis=0, keepdims=True))
            table = jnp.concatenate(tables, axis=0)
            x_buf[slot] = dot(table, xs[b], ((0,), (0,))).astype(bf16)
            u_buf[slot] = dot(table, us[b], ((0,), (0,))).astype(bf16)
            row = sublane((16, ROW))
            line = jnp.zeros((16, ROW), f32)
            for i in range(local):
                line = jnp.where(row == i, lines[i], line)
            high = line.astype(bf16).astype(f32)
            both = jnp.concatenate(
                [high, line - high, jnp.zeros((16, width - 2 * ROW), f32)], axis=1
            )
            og_s[pl.ds(pl.multiple_of(slot * 16, 16), 16), :] = both.astype(bf16)
            for copy in leave(b, slot):
                copy.start()
            extra(b, slot).start()

        for b in (blocks - 2, blocks - 1):
            for copy in leave(b, b % 2):
                copy.wait()
            extra(b, b % 2).wait()


def experts_part(rank, rows_in, cot_in, routes, small, expert_full):
    blocks, rows, width = rows_in.shape
    local, _, _, hidden = expert_full.shape
    slots = blocks * CAP
    any_space = pl.BlockSpec(memory_space=pl.ANY)
    one_expert = pl.BlockSpec((1, 3, width, hidden), lambda e: (e, 0, 0, 0))
    return pl.pallas_call(
        experts_kernel,
        grid=(local,),
        out_shape=[
            jax.ShapeDtypeStruct((blocks, rows, width), bf16),
            jax.ShapeDtypeStruct((blocks, rows + 16, width), bf16),
            jax.ShapeDtypeStruct((local, 3, width, hidden), bf16),
        ],
        in_specs=[pl.BlockSpec(memory_space=pltpu.SMEM), any_space, any_space] + whole(2) + [one_expert],
        out_specs=[any_space, any_space, one_expert],
        scratch_shapes=[
            pltpu.VMEM((blocks, local * CAP, width), bf16),
            pltpu.VMEM((blocks, local * CAP, width), bf16),
            pltpu.VMEM((blocks, local * CAP, 128), f32),
            pltpu.VMEM((blocks, local * CAP, 128), f32),
            pltpu.VMEM((2, rows, width), bf16),
            pltpu.VMEM((2, rows, width), bf16),
            pltpu.VMEM((slots, width), bf16),
            pltpu.VMEM((slots, hidden), bf16),
            pltpu.VMEM((slots, 2 * hidden), bf16),
            pltpu.VMEM((blocks, 8, ROW), jnp.int32),
            pltpu.SemaphoreType.DMA((3, 2)),
        ],
        compiler_params=pltpu.CompilerParams(vmem_limit_bytes=60 << 20),
        cost_estimate=pl.CostEstimate(
            flops=30_000_000_000, bytes_accessed=50 << 20, transcendentals=2_000_000
        ),
        name="experts",
    )(rank, rows_in, cot_in, routes, small, expert_full)


def exchange(x):
    return lax.all_to_all(x, "tensor", 0, 0, tiled=False)


def per_device(
    tokens,
    lengths,
    token_order,
    routes,
    cotangent,
    attn_gain,
    ffn_gain,
    router,
    w_query,
    w_key,
    w_value,
    w_output,
    query_gain,
    key_gain,
    w_gate,
    w_up,
    w_down,
):
    rows, width = tokens.shape
    group_rows = rows * RANKS
    experts = router.shape[1]
    rank = lax.axis_index("tensor")

    wkv = jnp.concatenate([w_key, w_value], axis=1)
    small_own = jnp.concatenate([attn_gain[:, None], ffn_gain[:, None], router], axis=1)
    small_own = jnp.pad(small_own, ((0, 0), (0, 128 - small_own.shape[1])))
    heads_own = jnp.concatenate([query_gain, key_gain], axis=0)
    heads_own = jnp.pad(heads_own, ((0, 5), (0, 124)))
    routes_own = routes.T.reshape(8, 2, 128).transpose(1, 0, 2).reshape(16, 128).astype(bf16)
    payload = jnp.concatenate(
        [w_query, wkv, small_own, heads_own, w_output.T, routes_own], axis=0
    )
    own_experts = jnp.stack([w_gate, w_up, w_down.transpose(0, 2, 1)], axis=1)
    expert_full = lax.all_gather(own_experts, "dp", axis=2, tiled=True)
    tokens_all, tiny_all, first_all, rest_all = opening(tokens, payload)
    first_all = first_all.reshape((GROUPS,) + first_all.shape[3:])
    rest_all = rest_all.reshape((GROUPS,) + rest_all.shape[3:])
    small = rest_all[:, :, 0:8, : 2 + experts].reshape(width, 2 + experts).T.astype(f32)
    small = jnp.concatenate([small[:2], jnp.zeros((6, width), f32), small[2:]], axis=0)
    cot_copies, tokens_all = lax.optimization_barrier((cotangent, tokens_all))
    cot_all = exchange(jnp.broadcast_to(cot_copies, (RANKS,) + cotangent.shape))

    feature = jnp.arange(128, dtype=jnp.int32) % 32
    frequency = ROTARY_BASE ** (-feature.astype(f32) / 32.0)
    within = jnp.arange(ROW, dtype=f32)[:, None] * frequency
    table = jnp.stack([jnp.cos(within), jnp.sin(within)])
    starts = (jnp.arange(8, dtype=f32) * ROW)[:, None] * frequency
    block = jnp.stack([jnp.cos(starts), jnp.sin(starts)])
    order_row, order_col = token_order, token_order.T
    normed_all, proj, stream_qkv, mixed_stream, log_total, mixed, wqkv = attend(
        lengths[0], tokens_all.reshape(group_rows, width), small, first_all, table, block,
        order_row, order_col,
    )
    mixed_own, hidden, normed2_all = middle(
        mixed.reshape(RANKS, rows, 128), rest_all, tokens, small
    )

    wqkv_cols, normed2_all = lax.optimization_barrier((tiny_all[:, :128], normed2_all))
    wqkv_all = lax.all_gather(wqkv_cols, "dp", axis=0, tiled=False)
    routes_all = tiny_all[:, 208:]
    out_part, copy_part, expert_grads = experts_part(
        rank[None], normed2_all, cot_all, routes_all, small, expert_full
    )
    expert_sums = lax.psum_scatter(expert_grads, "dp", scatter_dimension=2, tiled=True).astype(f32)
    back = exchange(copy_part)
    hidden_grad, mixed_grad, wo_grad, turn_grad = turn(
        back, hidden, cotangent, routes_own, small, mixed_own, rest_all
    )
    out_part, mixed_grad = lax.optimization_barrier((out_part, mixed_grad))
    out_pieces = exchange(out_part)

    proj_grad, wqkv_grad, small_grad = attend_back(
        lengths[0], mixed_grad.reshape(group_rows, 128), stream_qkv, mixed_stream, log_total,
        proj, first_all, table, block, order_row, order_col, normed_all, wqkv, small, turn_grad,
    )
    wide = jnp.concatenate([wo_grad, wqkv_grad], axis=1)
    grad_tokens, wqkv_sum, wo_sum, small_sum, head_sum = closing(
        proj_grad.reshape(RANKS, rows, 256), wide.reshape((4, 2, 2) + wide.shape[1:]),
        small_grad.reshape(4, 2, 2, -1, 128), wqkv_all, tokens, small, hidden_grad,
    )
    out_pieces, grad_tokens = lax.optimization_barrier((out_pieces, grad_tokens))
    layer_out = hidden + jnp.sum(out_pieces.astype(f32), axis=0)
    return (
        layer_out,
        grad_tokens,
        small_sum[:, 40],
        small_sum[:, 0],
        small_sum[:, 8:40],
        wqkv_sum[:, :128],
        wqkv_sum[:, 128:192],
        wqkv_sum[:, 192:256],
        wo_sum.T,
        head_sum[:4, 48:50].T,
        head_sum[:4, 50:51].T,
        expert_sums[:, 0],
        expert_sums[:, 1],
        expert_sums[:, 2].transpose(0, 2, 1),
    )


def solution(mesh):
    both = ("dp", "tensor")
    return jax.shard_map(
        per_device,
        mesh=mesh,
        in_specs=(
            P(both, None),
            P("dp", None),
            P("dp", None),
            P(both, None),
            P(both, None),
            P(both),
            P(both),
            P(both, None),
            P("dp", "tensor"),
            P("dp", "tensor"),
            P("dp", "tensor"),
            P("tensor", "dp"),
            P("tensor", "dp"),
            P("tensor", "dp"),
            P("tensor", "dp", None),
            P("tensor", "dp", None),
            P("tensor", None, "dp"),
        ),
        out_specs=(
            P(both, None),
            P(both, None),
            P(both),
            P(both),
            P(both, None),
            P("dp", "tensor"),
            P("dp", "tensor"),
            P("dp", "tensor"),
            P("tensor", "dp"),
            P("tensor", "dp"),
            P("tensor", "dp"),
            P("tensor", "dp", None),
            P("tensor", "dp", None),
            P("tensor", None, "dp"),
        ),
        check_vma=False,
    )
```

```python
import functools

import jax
import jax.numpy as jnp
import numpy as np
from jax import lax
from jax.experimental import pallas as pl
from jax.experimental.pallas import tpu as pltpu
from jax.sharding import PartitionSpec as P

CAP = 80
EPS = 1e-06
ROTARY_BASE = 10000.0
MASKED = -1e30
ROW = 256
CHUNK = 512
RANKS = 8
GROUPS = 16
MESH = pl.DeviceIdType.MESH
bf16 = jnp.bfloat16
f32 = jnp.float32


def dot(a, b, dims=((1,), (0,)), out=f32):
    return lax.dot_general(a, b, (dims, ((), ())), preferred_element_type=out)


def lane(shape):
    return lax.broadcasted_iota(jnp.int32, shape, len(shape) - 1)


def sublane(shape):
    return lax.broadcasted_iota(jnp.int32, shape, len(shape) - 2)


def cost_of(microseconds):
    return pl.CostEstimate(
        flops=microseconds * 1_100_000_000, bytes_accessed=1 << 20, transcendentals=0
    )


def whole(n):
    return [pl.BlockSpec(memory_space=pltpu.VMEM) for _ in range(n)]


def anywhere(n):
    return [pl.BlockSpec(memory_space=pl.ANY) for _ in range(n)]


def meet(ranks, groups):
    barrier = pltpu.get_barrier_semaphore()
    for peer in ranks:
        pl.semaphore_signal(barrier, inc=1, device_id={"tensor": peer}, device_id_type=MESH)
    for peer in groups:
        pl.semaphore_signal(barrier, inc=1, device_id={"dp": peer}, device_id_type=MESH)
    pl.semaphore_wait(barrier, len(ranks) + len(groups))


def push(src, dst, sems, index, peer):
    copy = pltpu.make_async_remote_copy(
        src_ref=src,
        dst_ref=dst,
        send_sem=sems[0].at[index],
        recv_sem=sems[1].at[index],
        device_id=peer,
        device_id_type=MESH,
    )
    copy.start()
    return copy


def keep(src, dst, sem):
    copy = pltpu.make_async_copy(src, dst, sem)
    copy.start()
    return copy


def others(name, size):
    me = lax.axis_index(name)
    return [lax.rem(me + k, size) for k in range(1, size)]


def neighbours():
    me = lax.axis_index("tensor")
    z = lax.rem(me, 4)
    here = me - z
    there = 4 - here
    right, left = lax.rem(z + 1, 4), lax.rem(z + 3, 4)
    return me, here, there, there + z, right, left


def row_copy(index, x, o, sems):
    me, here, there, partner, right, left = neighbours()
    half = o.shape[1] // 2
    low, high = pl.ds(0, half), pl.ds(half, half)
    both = pl.ds(0, 2 * half)
    to_right, to_left = {"tensor": here + right}, {"tensor": here + left}
    block, part, peer = (
        (me, both, {"tensor": partner}),
        (me, both, to_right),
        (me, both, to_left),
        (partner, both, to_right),
        (partner, both, to_left),
        (here + left, low, to_right),
        (here + right, high, to_left),
        (there + left, low, to_right),
        (there + right, high, to_left),
    )[index]
    return pltpu.make_async_remote_copy(
        src_ref=x if index < 3 else o.at[block, part],
        dst_ref=o.at[block, part],
        send_sem=sems[0].at[index],
        recv_sem=sems[1].at[index],
        device_id=peer,
        device_id_type=MESH,
    )


def rows_begin(x, o, sems):
    for index in range(3):
        row_copy(index, x, o, sems).start()


def rows_on(x, o, sems, arrived, leaving):
    for index, later in zip(arrived, leaving):
        row_copy(index, x, o, sems).wait_recv()
        for other in later:
            row_copy(other, x, o, sems).start()


def rows_near(x, o, sems):
    rows_on(x, o, sems, (1, 2, 0), ((5,), (6,), (3, 4)))


def rows_far(x, o, sems):
    rows_on(x, o, sems, (3, 4), ((7,), (8,)))


def rows_end(x, o, sems):
    for index in range(5, 9):
        row_copy(index, x, o, sems).wait_recv()
    for index in range(9):
        row_copy(index, x, o, sems).wait_send()


class RowSums:
    def __init__(self, blocks, far, near, leaving, landed, sems):
        self.blocks, self.far, self.near = blocks, far, near
        self.leaving, self.landed, self.sems = leaving, landed, sems
        self.me, here, there, self.partner, self.right, self.left = neighbours()
        self.here, self.z, self.bases = here, self.me - here, (there, here)
        self.half = blocks.shape[1] // 2
        self.parts = pl.ds(0, self.half), pl.ds(self.half, self.half)

    def copy(self, src, dst, index, peer):
        return pltpu.make_async_remote_copy(
            src_ref=src,
            dst_ref=dst,
            send_sem=self.sems[0].at[index],
            recv_sem=self.sems[1].at[index],
            device_id={"tensor": peer},
            device_id_type=MESH,
        )

    def far_copy(self, side, way):
        block = self.bases[side] + lax.rem(self.z + 2, 4)
        peer = self.here + (self.right, self.left)[way]
        src = self.blocks.at[block, self.parts[way]]
        return self.copy(src, self.far.at[side, way], side * 4 + way, peer)

    def near_copy(self, side, way):
        step = (self.right, self.left)[way]
        src = self.blocks.at[self.bases[side] + step]
        return self.copy(src, self.near.at[side, way], side * 4 + 2 + way, self.here + step)

    def cross_copy(self):
        return self.copy(self.leaving, self.landed, 8, self.partner)

    def begin(self, side):
        for way in range(2):
            self.far_copy(side, way).start()

    def go_on(self, side):
        for way in range(2):
            self.far_copy(side, way).wait_recv()
            at = self.bases[side] + (self.right, self.left)[way]
            total = self.blocks[at, self.parts[way], :].astype(f32)
            total = total + self.far[side, way].astype(f32)
            self.blocks[at, self.parts[way], :] = total.astype(bf16)
            self.near_copy(side, way).start()

    def total(self, side):
        total = self.blocks[self.bases[side] + self.z].astype(f32)
        for way in range(2):
            self.near_copy(side, way).wait_recv()
            total = total + self.near[side, way].astype(f32)
        return total

    def cross(self):
        self.leaving[...] = self.total(0).astype(bf16)
        self.cross_copy().start()

    def finish(self):
        total = self.total(1)
        self.cross_copy().wait_recv()
        total = total + self.landed[...].astype(f32)
        for side in range(2):
            for way in range(2):
                self.far_copy(side, way).wait_send()
                self.near_copy(side, way).wait_send()
        self.cross_copy().wait_send()
        return total


def row_sum_scratch(rows, width):
    dma = pltpu.SemaphoreType.DMA
    return [
        pltpu.VMEM((2, 2, rows // 2, width), bf16),
        pltpu.VMEM((2, 2, rows, width), bf16),
        pltpu.VMEM((rows, width), bf16),
        pltpu.VMEM((rows, width), bf16),
        dma((9,)),
        dma((9,)),
    ]


def group_place():
    group = lax.axis_index("dp")
    core, side, y = lax.rem(group, 2), lax.rem(group // 2, 2), group // 4
    across = {"dp": group + 2 - 4 * side}
    other = {"dp": group + 1 - 2 * core}
    column = [(lax.rem(y + k, 4), {"dp": lax.rem(y + k, 4) * 4 + side * 2 + core}) for k in (2, 1, 3)]
    return y, side, core, across, column, other


def gather_first(src, o, sems):
    y, side, core, across, _, _ = group_place()
    return push(src, o.at[y, side, core], sems, 0, across)


def gather_second(first, own, o, sems):
    y, _, core, _, column, _ = group_place()
    first.wait_recv()
    own.wait()
    part = o.at[y, :, core]
    return [push(part, part, sems, 1 + k, peer) for k, (_, peer) in enumerate(column)]


def gather_third(second, o, sems):
    _, _, core, _, _, other = group_place()
    for copy in second:
        copy.wait_recv()
    part = o.at[:, :, core]
    return push(part, part, sems, 4, other)


def opening_kernel(
    tokens, w_query, w_key, w_value, w_output, attn_gain, ffn_gain, router, query_gain, key_gain, routes,
    tokens_all, qkv_all, tiny_all, first_all, rest_all, small, routes_own,
    payload, lines, small_rows,
    row_send, row_recv, qkv_send, qkv_recv, tiny_send, tiny_recv, first_send, first_recv,
    rest_send, rest_recv, local,
):
    me = lax.axis_index("tensor")
    y, side, core, across, column, other = group_place()
    ranks = others("tensor", RANKS)
    lines[...] = jnp.zeros_like(lines)
    lines[0, 0:1, 0:8] = attn_gain[...].astype(f32)
    lines[0, 1:2, 0:8] = ffn_gain[...].astype(f32)
    lines[1, :, 0:32] = router[...].astype(f32)
    lines[2, 0:2, 0:4] = query_gain[...].astype(f32)
    lines[2, 2:3, 0:4] = key_gain[...].astype(f32)
    lines[3, :, 0:8] = jnp.transpose(lines[0])[0:8]
    block = lines[3] + pltpu.roll(lines[1], 2, 1)
    payload[0:64] = w_query[...]
    payload[64:128, 0:64] = w_key[...]
    payload[64:128, 64:128] = w_value[...]
    payload[128:144] = jnp.concatenate([block, lines[2]], axis=0).astype(bf16)
    payload[144:208] = jnp.transpose(w_output[...].astype(f32)).astype(bf16)
    picks = routes[...].astype(f32)
    picks = jnp.concatenate([picks[:, 0:128], picks[:, 128:256]], axis=0).astype(bf16)
    payload[208:224] = picks
    routes_own[...] = picks
    meet(ranks, [across["dp"], other["dp"]] + [peer["dp"] for _, peer in column])
    own, qkv, rest = payload.at[0:144], payload.at[0:128], payload.at[128:224]
    tiny = [
        push(rest, tiny_all.at[me], (tiny_send, tiny_recv), k, {"tensor": peer})
        for k, peer in enumerate(ranks)
    ]
    first_sems, rest_sems = (first_send, first_recv), (rest_send, rest_recv)
    first_one = gather_first(own, first_all, first_sems)
    row_sems = row_send, row_recv
    rows_begin(tokens, tokens_all, row_sems)
    tiny_own = keep(rest, tiny_all.at[me], local.at[0])
    first_own = keep(own, first_all.at[y, side, core], local.at[1])
    kept = [
        keep(tokens, tokens_all.at[me], local.at[2]),
        keep(qkv, qkv_all.at[me], local.at[3]),
    ]
    for copy in tiny:
        copy.wait_recv()
    tiny_own.wait()
    part = tiny_all.at[:, pl.ds(0, 80)]
    rest_one = gather_first(part, rest_all, rest_sems)
    rest_own = keep(part, rest_all.at[y, side, core], local.at[4])
    first_two = gather_second(first_one, first_own, first_all, first_sems)
    rows_near(tokens, tokens_all, row_sems)
    rest_two = gather_second(rest_one, rest_own, rest_all, rest_sems)
    first_three = gather_third(first_two, first_all, first_sems)
    qkv_sent = [
        push(qkv, qkv_all.at[me], (qkv_send, qkv_recv), k, {"tensor": peer})
        for k, peer in enumerate(ranks)
    ]
    rows_far(tokens, tokens_all, row_sems)
    rest_three = gather_third(rest_two, rest_all, rest_sems)
    rest_three.wait_recv()
    gathered = keep(rest_all.at[:, :, :, :, pl.ds(0, 16)], small_rows, local.at[5])
    gathered.wait()
    turned_rows = jnp.transpose(small_rows[:, :, :, :, 0:8, :].astype(f32).reshape(-1, 128))
    small[0:8] = turned_rows[0:8]
    small[8:40] = turned_rows[2:34]
    rows_end(tokens, tokens_all, row_sems)
    first_three.wait()
    rest_three.wait_send()
    for copy in qkv_sent:
        copy.wait()
    for copy in (*tiny, first_one, rest_one, *first_two, *rest_two):
        copy.wait_send()
    for copy in kept:
        copy.wait()


def opening(tokens, *weights):
    dma = pltpu.SemaphoreType.DMA
    like = jax.ShapeDtypeStruct
    return pl.pallas_call(
        opening_kernel,
        out_shape=[
            like((RANKS,) + tokens.shape, bf16),
            like((RANKS, 128, 128), bf16),
            like((RANKS, 96, 128), bf16),
            like((4, 2, 2, 144, 128), bf16),
            like((4, 2, 2, RANKS, 80, 128), bf16),
            like((40, tokens.shape[1]), f32),
            like((16, 128), bf16),
        ],
        in_specs=anywhere(1) + whole(10),
        out_specs=anywhere(5) + whole(2),
        scratch_shapes=[
            pltpu.VMEM((224, 128), bf16),
            pltpu.VMEM((4, 8, 128), f32),
            pltpu.VMEM((4, 2, 2, RANKS, 16, 128), bf16),
            dma((9,)),
            dma((9,)),
        ]
        + [dma((7,))] * 4
        + [dma((5,))] * 4
        + [dma((6,))],
        compiler_params=pltpu.CompilerParams(
            collective_id=1, has_side_effects=True, vmem_limit_bytes=40 << 20
        ),
        cost_estimate=cost_of(50),
        name="opening",
    )(tokens, *weights)


def middle_kernel(
    mixed, rest, tokens, small,
    mixed_own, hidden, normed2_all, done,
    landed, normed2, mix_send, mix_recv, row_send, row_recv, local,
):
    me, here, _, partner, right, left = neighbours()
    ranks = others("tensor", RANKS)
    meet(ranks, [])
    sent = [
        push(mixed.at[peer], landed.at[me], (mix_send, mix_recv), k, {"tensor": peer})
        for k, peer in enumerate(ranks)
    ]
    own = keep(mixed.at[me], landed.at[me], local.at[0])
    for copy in sent:
        copy.wait_recv()
    own.wait()
    total = tokens[...].astype(f32)
    for s in range(RANKS):
        weight = rest[:, s, 16:80, :].reshape(-1, 128)
        total = total + dot(landed[s], weight, ((1,), (1,)))
    mixed_own[...] = landed[...]
    hidden[...] = total
    scale = lax.rsqrt(jnp.mean(total * total, axis=1, keepdims=True) + EPS)
    normed2[...] = (total * scale * small[1:2, :]).astype(bf16)
    row_sems = row_send, row_recv
    rows_begin(normed2, normed2_all, row_sems)
    kept = keep(normed2, normed2_all.at[me], local.at[1])
    rows_near(normed2, normed2_all, row_sems)
    rows_far(normed2, normed2_all, row_sems)
    rows_end(normed2, normed2_all, row_sems)
    for copy in sent:
        copy.wait_send()
    kept.wait()
    done[...] = jnp.zeros_like(done)


def middle(mixed, rest, tokens, small):
    dma = pltpu.SemaphoreType.DMA
    rows, width = tokens.shape
    return pl.pallas_call(
        middle_kernel,
        out_shape=[
            jax.ShapeDtypeStruct(mixed.shape, bf16),
            jax.ShapeDtypeStruct((rows, width), f32),
            jax.ShapeDtypeStruct((RANKS, rows, width), bf16),
            jax.ShapeDtypeStruct((8, 128), f32),
        ],
        in_specs=anywhere(1) + whole(3),
        out_specs=whole(2) + anywhere(1) + whole(1),
        scratch_shapes=[
            pltpu.VMEM(mixed.shape, bf16),
            pltpu.VMEM((rows, width), bf16),
            dma((7,)),
            dma((7,)),
            dma((9,)),
            dma((9,)),
            dma((2,)),
        ],
        compiler_params=pltpu.CompilerParams(
            collective_id=2, has_side_effects=True, vmem_limit_bytes=40 << 20
        ),
        cost_estimate=cost_of(40),
        name="middle",
    )(mixed, rest, tokens, small)


def named_of(routes):
    picks = routes.astype(f32)
    picks = jnp.concatenate([picks[0:8], picks[8:16]], axis=1)
    expert = sublane((32, ROW)).astype(f32)
    found = jnp.zeros((32, ROW), f32)
    for k in range(8):
        found = jnp.where(picks[k : k + 1] == expert, 1.0, found)
    return found


def gates_of(named, logits):
    logits = jnp.where(named > 0.5, logits, MASKED)
    odds = jnp.where(named > 0.5, jnp.exp(logits - jnp.max(logits, axis=0, keepdims=True)), 0.0)
    return odds / jnp.sum(odds, axis=0, keepdims=True)


def norm_back(value, scales, grad):
    scale = lax.rsqrt(jnp.mean(value * value, axis=1, keepdims=True) + EPS)
    scaled = value * scale
    weighted = grad * scales
    moved = scale * (weighted - scaled * jnp.mean(weighted * scaled, axis=1, keepdims=True))
    return moved, scaled


def turn_kernel(
    back, hidden, cotangent, routes, small, mixed_own, rest,
    hidden_grad, mixed_grad, wo_grad, small_grad,
    leaving, landed, mix_send, mix_recv, local,
):
    me = lax.axis_index("tensor")
    ranks = others("tensor", RANKS)
    meet(ranks, [])
    value = hidden[...]
    gain = small[1:2, :]
    router = small[8:40, :].astype(bf16)
    scale = lax.rsqrt(jnp.mean(value * value, axis=1, keepdims=True) + EPS)
    normed2 = (value * scale * gain).astype(bf16)
    gates = gates_of(named_of(routes[...]), dot(router, normed2, ((1,), (1,))))
    pieces = back[ROW:, 0 : 2 * ROW]
    gate_grad = pieces[:, :ROW] + pieces[:, ROW:]
    inner = jnp.sum(gates * gate_grad, axis=0, keepdims=True)
    logit_grad = (gates * (gate_grad - inner)).astype(bf16)
    grad = dot(logit_grad, router, ((0,), (0,)))
    grad = grad + back[0:ROW, :]
    moved, scaled = norm_back(value, gain, grad)
    total = cotangent[...].astype(f32) + moved
    branch = total.astype(bf16)
    for s in range(RANKS):
        weight = rest[:, s, 16:80, :].reshape(-1, 128)
        leaving[s] = dot(branch, weight).astype(bf16)
    sent = [
        push(leaving.at[peer], landed.at[me], (mix_send, mix_recv), k, {"tensor": peer})
        for k, peer in enumerate(ranks)
    ]
    own = keep(leaving.at[me], landed.at[me], local.at[0])
    hidden_grad[...] = total
    small_grad[0:8, :] = jnp.broadcast_to(
        jnp.sum(grad * scaled, axis=0, keepdims=True), (8, grad.shape[1])
    )
    small_grad[8:40, :] = dot(logit_grad, normed2)
    for s in range(RANKS):
        part = dot(branch, mixed_own[s], ((0,), (0,)))
        wo_grad[:, s] = part.astype(bf16).reshape(GROUPS, -1, 128)
    for copy in sent:
        copy.wait()
    own.wait()
    mixed_grad[...] = landed[...]


def turn(back, hidden, cotangent, routes, small, mixed_own, rest):
    dma = pltpu.SemaphoreType.DMA
    rows, width = hidden.shape
    return pl.pallas_call(
        turn_kernel,
        out_shape=[
            jax.ShapeDtypeStruct((rows, width), f32),
            jax.ShapeDtypeStruct(mixed_own.shape, bf16),
            jax.ShapeDtypeStruct((GROUPS, RANKS, width // GROUPS, 128), bf16),
            jax.ShapeDtypeStruct((40, width), f32),
        ],
        in_specs=whole(7),
        out_specs=whole(4),
        scratch_shapes=[
            pltpu.VMEM(mixed_own.shape, bf16),
            pltpu.VMEM(mixed_own.shape, bf16),
            dma((7,)),
            dma((7,)),
            dma((1,)),
        ],
        compiler_params=pltpu.CompilerParams(
            collective_id=3, has_side_effects=True, vmem_limit_bytes=48 << 20
        ),
        cost_estimate=cost_of(15),
        name="turn",
    )(back, hidden, cotangent, routes, small, mixed_own, rest)


def closing_kernel(
    proj_grad, wo_grad, wqkv_grad, small_grad, wqkv_all, tokens, small, hidden_grad,
    grad_tokens, wqkv_sum, wo_sum, small_sum, head_sum,
    proj_in,
    wo_core, wo_y, wo_x, wo_half, wo_pair,
    wqkv_core, wqkv_y, wqkv_x, wqkv_half, wqkv_pair,
    small_core, small_y, small_x, small_half, small_pair,
    wo_out, small_out, wo_last, small_last,
    proj_send, proj_recv, group_send, group_recv, last_send, last_recv, local,
):
    me = lax.axis_index("tensor")
    y, side, core, across, column, other = group_place()
    ranks = others("tensor", RANKS)
    meet(ranks, [across["dp"], other["dp"]] + [peer["dp"] for _, peer in column])
    away = 1 - core
    arrays = (
        (wo_grad, wo_core, wo_half, wo_y, wo_pair, wo_x),
        (wqkv_grad, wqkv_core, wqkv_half, wqkv_y, wqkv_pair, wqkv_x),
        (small_grad, small_core, small_half, small_y, small_pair, small_x),
    )
    sems = [(group_send.at[a], group_recv.at[a]) for a in range(3)]
    first = [
        push(array[0].at[:, :, away], array[1], sems[a], 0, other) for a, array in enumerate(arrays)
    ]
    proj = [
        push(proj_grad.at[peer], proj_in.at[me], (proj_send, proj_recv), k, {"tensor": peer})
        for k, peer in enumerate(ranks)
    ]
    proj_own = keep(proj_grad.at[me], proj_in.at[me], local.at[0])
    second = []
    for a, (whole_grad, landed, half, down, _, _) in enumerate(arrays):
        first[a].wait_recv()
        total = whole_grad[:, :, core].astype(f32) + landed[...].astype(f32)
        half[...] = total.astype(half.dtype)
        second.append(
            [push(half.at[at], down.at[k], sems[a], 1 + k, peer) for k, (at, peer) in enumerate(column)]
        )
    third = []
    for a, (_, _, half, down, pair, far) in enumerate(arrays):
        for copy in second[a]:
            copy.wait_recv()
        total = half[y].astype(f32)
        for k in range(3):
            total = total + down[k].astype(f32)
        pair[...] = total.astype(pair.dtype)
        third.append(push(pair.at[1 - side], far, sems[a], 4, across))
    for copy in proj:
        copy.wait_recv()
    proj_own.wait()
    grad = jnp.zeros(grad_tokens.shape, f32)
    for s in range(RANKS):
        query = wqkv_all[:, s, 0:64, :].reshape(-1, 128)
        rest = wqkv_all[:, s, 64:128, :].reshape(-1, 128)
        grad = grad + dot(proj_in[s, :, 0:128], query, ((1,), (1,)))
        grad = grad + dot(proj_in[s, :, 128:256], rest, ((1,), (1,)))
    moved, _ = norm_back(tokens[...].astype(f32), small[0:1, :], grad)
    grad_tokens[...] = hidden_grad[...] + moved
    sums = []
    for a, (_, _, _, _, pair, far) in enumerate(arrays):
        third[a].wait_recv()
        sums.append(pair[side].astype(f32) + far[...].astype(f32))
    wo_out[...] = sums[0].astype(bf16)
    head_sum[...] = sums[2][0:8]
    small_out[...] = sums[2].reshape(small_out.shape)
    last = []
    for a, (src, dst) in enumerate(((wo_out, wo_last), (small_out, small_last))):
        pair = last_send.at[a], last_recv.at[a]
        last += [
            push(src.at[peer], dst.at[me], pair, k, {"tensor": peer}) for k, peer in enumerate(ranks)
        ]
    kept = [
        keep(wo_out.at[me], wo_last.at[me], local.at[1]),
        keep(small_out.at[me], small_last.at[me], local.at[2]),
    ]
    wqkv_sum[:, 0:128] = sums[1][0]
    wqkv_sum[:, 128:256] = sums[1][1]
    for copy in last:
        copy.wait_recv()
    for copy in kept:
        copy.wait()
    total = jnp.zeros(wo_sum.shape, f32)
    small_total = jnp.zeros(small_sum.shape, f32)
    for s in range(RANKS):
        total = total + wo_last[s].astype(f32)
        small_total = small_total + small_last[s]
    wo_sum[...] = total
    small_sum[...] = small_total
    for copy in (*proj, *first, *third, *last):
        copy.wait_send()
    for copies in second:
        for copy in copies:
            copy.wait_send()


def closing(proj_grad, wo_grad, wqkv_grad, small_grad, wqkv_all, tokens, small, hidden_grad):
    dma = pltpu.SemaphoreType.DMA
    shard = wo_grad.shape[4]
    rows = shard // RANKS
    steps = []
    for array in (wo_grad, wqkv_grad, small_grad):
        block = array.shape[3:]
        for lead in ((4, 2), (3, 2), (), (4, 2), (2,)):
            steps.append(pltpu.VMEM(lead + block, array.dtype))
    return pl.pallas_call(
        closing_kernel,
        out_shape=[
            jax.ShapeDtypeStruct(hidden_grad.shape, f32),
            jax.ShapeDtypeStruct((shard, 256), f32),
            jax.ShapeDtypeStruct((shard, 128), f32),
            jax.ShapeDtypeStruct((rows, 128), f32),
            jax.ShapeDtypeStruct((8, 128), f32),
        ],
        in_specs=whole(8),
        out_specs=whole(5),
        scratch_shapes=[
            pltpu.VMEM(proj_grad.shape, bf16),
            *steps,
            pltpu.VMEM((RANKS, shard, 128), bf16),
            pltpu.VMEM((RANKS, rows, 128), f32),
            pltpu.VMEM((RANKS, shard, 128), bf16),
            pltpu.VMEM((RANKS, rows, 128), f32),
            dma((7,)),
            dma((7,)),
            dma((3, 5)),
            dma((3, 5)),
            dma((2, 7)),
            dma((2, 7)),
            dma((3,)),
        ],
        compiler_params=pltpu.CompilerParams(
            collective_id=4, has_side_effects=True, vmem_limit_bytes=62 << 20
        ),
        cost_estimate=cost_of(45),
        name="closing",
    )(proj_grad, wo_grad, wqkv_grad, small_grad, wqkv_all, tokens, small, hidden_grad)


def sequence_start(place, lengths):
    first, second = lengths[0], lengths[0] + lengths[1]
    return jnp.where(place < first, 0, jnp.where(place < second, first, second))


def swap_halves(x):
    return jnp.where(lane(x.shape) % 64 < 32, pltpu.roll(x, 96, 1), pltpu.roll(x, 32, 1))


def head_mean(x, heads):
    low = lane(x.shape) < 64
    first = jnp.sum(jnp.where(low, x, 0.0), axis=1, keepdims=True) / 64
    if heads == 1:
        return jnp.where(low, first, 0.0)
    second = jnp.sum(jnp.where(low, 0.0, x), axis=1, keepdims=True) / 64
    return jnp.where(low, first, second)


def head_gains(first_all):
    total = jnp.zeros((8, 128), f32)
    for g in range(GROUPS):
        piece = first_all[g, 128:144, :].astype(f32)[8:16]
        total = total + pltpu.roll(jnp.where(lane(piece.shape) < 4, piece, 0.0), 4 * g, 1)
    low = lane((1, 128)) < 64
    return jnp.where(low, total[0:1], pltpu.roll(total[1:2], 64, 1)), total[2:3]


def turned(table, block, b):
    within_cos, within_sin = table[0], table[1]
    block_cos, block_sin = block[0, pl.ds(b, 1), :], block[1, pl.ds(b, 1), :]
    cos = within_cos * block_cos - within_sin * block_sin
    sin = within_sin * block_cos + within_cos * block_sin
    return cos, jnp.where(lane(sin.shape) % 64 < 32, -sin, sin)


def attend_kernel(
    lengths, x, small, first_all, table, block, order_row, order_col,
    normed, proj, stream_qkv, mixed_stream, log_total, mixed, wqkv,
    token_qkv, keys, values,
):
    rows = x.shape[0]
    blocks = rows // ROW
    q_gain, k_gain = head_gains(first_all)
    wqkv[:, 0:128] = first_all[:, 0:64, :].reshape(-1, 128)
    wqkv[:, 128:256] = first_all[:, 64:128, :].reshape(-1, 128)

    @pl.loop(0, blocks)
    def _(b):
        at = pl.ds(pl.multiple_of(b * ROW, ROW), ROW)
        v = x[at, :].astype(f32)
        r = lax.rsqrt(jnp.mean(v * v, axis=1, keepdims=True) + EPS)
        n = (v * r * small[0:1, :]).astype(bf16)
        normed[at, :] = n
        p = dot(n, wqkv[...])
        proj[at, :] = p
        q, kv = p[:, :128], p[:, 128:]
        low = lane(kv.shape) < 64
        q = q * lax.rsqrt(head_mean(q * q, 2) + EPS) * q_gain
        k = kv * lax.rsqrt(head_mean(kv * kv, 1) + EPS) * k_gain
        token_qkv[at, 0:128] = q.astype(bf16)
        token_qkv[at, 128:256] = jnp.where(low, k, kv).astype(bf16)

    @pl.loop(0, blocks)
    def _(b):
        at = pl.ds(pl.multiple_of(b * ROW, ROW), ROW)
        place = sublane((ROW, rows)) + b * ROW
        moves = jnp.where(order_row[...] == place, 1.0, 0.0).astype(bf16)
        moved = dot(moves, token_qkv[...])
        cos, sin = turned(table, block, b)
        q, kv = moved[:, :128], moved[:, 128:]
        low = lane(kv.shape) < 64
        q = (q * cos + swap_halves(q) * sin) * 0.125
        kv = jnp.where(low, kv * cos + swap_halves(kv) * sin, kv)
        stream_qkv[at, 0:128] = q.astype(bf16)
        stream_qkv[at, 128:256] = kv.astype(bf16)
        other = pltpu.roll(kv, 64, 1)
        keys[at, :] = jnp.where(low, kv, other).astype(bf16)
        values[at, :] = jnp.where(low, other, 1.0).astype(bf16)

    @pl.loop(0, blocks)
    def _(b):
        at = pl.ds(pl.multiple_of(b * ROW, ROW), ROW)
        q = stream_qkv[at, 0:128]
        low = lane(q.shape) < 64
        zero = jnp.zeros_like(q)
        q0, q1 = jnp.where(low, q, zero), jnp.where(low, zero, q)
        place = sublane((ROW, 1)) + b * ROW
        start = sequence_start(place, lengths)
        first = sequence_start(b * ROW, lengths) // CHUNK
        last = (b * ROW + ROW - 1) // CHUNK + 1

        def step(j, totals):
            t0, t1 = totals
            here = pl.ds(pl.multiple_of(j * CHUNK, CHUNK), CHUNK)
            k, v = keys[here, :], values[here, :]
            key = lane((ROW, CHUNK)) + j * CHUNK
            allowed = (key <= place) & (key >= start)
            e0 = jnp.where(allowed, jnp.exp(dot(q0, k, ((1,), (1,)))), 0.0).astype(bf16)
            e1 = jnp.where(allowed, jnp.exp(dot(q1, k, ((1,), (1,)))), 0.0).astype(bf16)
            return t0 + dot(e0, v), t1 + dot(e1, v)

        none = jnp.zeros((ROW, 128), f32)
        t0, t1 = lax.fori_loop(first, last, step, (none, none))
        low = lane((ROW, 128)) < 64
        other0, other1 = pltpu.roll(t0, 64, 1), pltpu.roll(t1, 64, 1)
        total = jnp.where(low, other0, t1)
        out = jnp.where(low, t0, other1) / total
        log_total[at, :] = jnp.log(total)
        mixed_stream[at, :] = out.astype(bf16)

    @pl.loop(0, blocks)
    def _(b):
        at = pl.ds(pl.multiple_of(b * ROW, ROW), ROW)
        moves = jnp.where(order_col[at, :] == lane((ROW, rows)), 1.0, 0.0).astype(bf16)
        mixed[at, :] = dot(moves, mixed_stream[...]).astype(bf16)


def attend(lengths, x, small, first_all, table, block, order_row, order_col):
    rows, width = x.shape
    return pl.pallas_call(
        attend_kernel,
        out_shape=[
            jax.ShapeDtypeStruct((rows, width), bf16),
            jax.ShapeDtypeStruct((rows, 256), f32),
            jax.ShapeDtypeStruct((rows, 256), bf16),
            jax.ShapeDtypeStruct((rows, 128), bf16),
            jax.ShapeDtypeStruct((rows, 128), f32),
            jax.ShapeDtypeStruct((rows, 128), bf16),
            jax.ShapeDtypeStruct((width, 256), bf16),
        ],
        in_specs=[pl.BlockSpec(memory_space=pltpu.SMEM)] + whole(7),
        out_specs=whole(7),
        scratch_shapes=[
            pltpu.VMEM((rows, 256), bf16),
            pltpu.VMEM((rows, 128), bf16),
            pltpu.VMEM((rows, 128), bf16),
        ],
        compiler_params=pltpu.CompilerParams(vmem_limit_bytes=56 << 20),
        cost_estimate=cost_of(30),
        name="attend",
    )(lengths, x, small, first_all, table, block, order_row, order_col)


def attend_back_kernel(
    lengths, mixed_grad, stream_qkv, mixed_stream, log_total, proj, first_all, table, block,
    order_row, order_col, normed, wqkv, small, turn_grad,
    proj_grad, wqkv_grad, small_grad,
    gain_grad, keys, values, out_grad, query_grad, key_grad, value_grad, attn_gain,
):
    rows = proj.shape[0]
    blocks = rows // ROW
    q_gain, k_gain = head_gains(first_all)
    key_grad[...] = jnp.zeros_like(key_grad)
    value_grad[...] = jnp.zeros_like(value_grad)

    @pl.loop(0, blocks)
    def _(b):
        at = pl.ds(pl.multiple_of(b * ROW, ROW), ROW)
        place = sublane((ROW, rows)) + b * ROW
        moves = jnp.where(order_row[...] == place, 1.0, 0.0).astype(bf16)
        out_grad[at, :] = dot(moves, mixed_grad[...]).astype(bf16)
        kv = stream_qkv[at, 128:256].astype(f32)
        low = lane(kv.shape) < 64
        other = pltpu.roll(kv, 64, 1)
        keys[at, :] = jnp.where(low, kv, other).astype(bf16)
        values[at, :] = jnp.where(low, other, kv).astype(bf16)

    @pl.loop(0, blocks)
    def _(b):
        at = pl.ds(pl.multiple_of(b * ROW, ROW), ROW)
        q, g = stream_qkv[at, 0:128], out_grad[at, :]
        low = lane(q.shape) < 64
        zero = jnp.zeros_like(q)
        qs = jnp.where(low, q, zero), jnp.where(low, zero, q)
        gs = jnp.where(low, g, zero), jnp.where(low, zero, g)
        product = jnp.transpose(g.astype(f32) * mixed_stream[at, :].astype(f32))
        inner = (
            jnp.sum(product[:64], axis=0, keepdims=True),
            jnp.sum(product[64:], axis=0, keepdims=True),
        )
        logs = jnp.transpose(log_total[at, :])
        logs = logs[0:1], logs[64:65]
        place = lane((1, ROW)) + b * ROW
        start = sequence_start(place, lengths)
        first = sequence_start(b * ROW, lengths) // CHUNK
        last = (b * ROW + ROW - 1) // CHUNK + 1

        def step(j, totals):
            here = pl.ds(pl.multiple_of(j * CHUNK, CHUNK), CHUNK)
            k, v = keys[here, :], values[here, :]
            key = sublane((CHUNK, ROW)) + j * CHUNK
            allowed = (key <= place) & (key >= start)
            done = []
            kt, vt = key_grad[here, :], value_grad[here, :]
            for h in range(2):
                p = jnp.exp(dot(k, qs[h], ((1,), (1,))) - logs[h])
                p = jnp.where(allowed, p, 0.0)
                d = p * (dot(v, gs[h], ((1,), (1,))) - inner[h])
                p, d = p.astype(bf16), d.astype(bf16)
                vt = vt + dot(p, gs[h])
                kt = kt + dot(d, qs[h])
                done.append(totals[h] + dot(k, d, ((0,), (0,))))
            key_grad[here, :] = kt
            value_grad[here, :] = vt
            return tuple(done)

        none = jnp.zeros((128, ROW), f32)
        t0, t1 = lax.fori_loop(first, last, step, (none, none))
        grad = jnp.where(sublane((128, ROW)) < 64, t0, t1) * 0.125
        cos, sin = turned(table, block, b)
        cos, sin = jnp.transpose(cos), jnp.transpose(sin)
        swapped = jnp.concatenate([grad[32:64], grad[0:32], grad[96:128], grad[64:96]], axis=0)
        query_grad[:, at] = (grad * cos - swapped * sin).astype(bf16)

    gain_grad[...] = jnp.zeros_like(gain_grad)
    attn_gain[...] = jnp.zeros_like(attn_gain)

    @pl.loop(0, blocks)
    def _(b):
        at = pl.ds(pl.multiple_of(b * ROW, ROW), ROW)
        key, value = key_grad[at, :], value_grad[at, :]
        low = lane(key.shape) < 64
        key = key + pltpu.roll(key, 64, 1)
        cos, sin = turned(table, block, b)
        key = key * cos - swap_halves(key) * sin
        keys[at, :] = jnp.where(low, key, value + pltpu.roll(value, 64, 1)).astype(bf16)

    @pl.loop(0, blocks)
    def _(b):
        at = pl.ds(pl.multiple_of(b * ROW, ROW), ROW)
        moves = jnp.where(order_col[at, :] == lane((ROW, rows)), 1.0, 0.0).astype(bf16)
        dq = dot(moves, query_grad[...], ((1,), (1,)))
        dkv = dot(moves, keys[...])

        def back(grad, value, scales, heads):
            r = lax.rsqrt(head_mean(value * value, heads) + EPS)
            scaled = value * r
            weighted = grad * scales
            result = r * (weighted - scaled * head_mean(weighted * scaled, heads))
            return result, jnp.sum(grad * scaled, axis=0, keepdims=True)

        q_result, q_sum = back(dq, proj[at, 0:128], q_gain, 2)
        k_result, k_sum = back(dkv, proj[at, 128:256], k_gain, 1)
        q_low = q_result.astype(bf16)
        k_low = jnp.where(lane(dkv.shape) < 64, k_result, dkv).astype(bf16)
        proj_grad[at, 0:128] = q_low
        proj_grad[at, 128:256] = k_low
        gain_grad[0:1, :] += q_sum
        gain_grad[1:2, :] += k_sum
        part = dot(jnp.concatenate([q_low, k_low], axis=1), wqkv[...], ((1,), (1,)))
        part = part * normed[at, :].astype(f32)
        attn_gain[0:1, :] += jnp.sum(part, axis=0, keepdims=True)

    @pl.loop(0, normed.shape[1] // 256)
    def _(c):
        at = pl.ds(pl.multiple_of(c * 256, 256), 256)
        part = dot(normed[:, at], proj_grad[...], ((0,), (0,))).astype(bf16)
        own = pl.ds(c * 4, 4)
        wqkv_grad[own, 0] = part[:, 0:128].reshape(4, 64, 128)
        wqkv_grad[own, 1] = part[:, 128:256].reshape(4, 64, 128)

    heads = gain_grad[...]
    low = lane(heads.shape) < 64
    heads = jnp.concatenate(
        [
            jnp.where(low[0:1], heads[0:1], 0.0),
            jnp.where(low[0:1], pltpu.roll(heads[0:1], 64, 1), 0.0),
            jnp.where(low[0:1], heads[1:2], 0.0),
            jnp.zeros((5, 128), f32),
        ],
        axis=0,
    )
    spots = []
    for pair in range(GROUPS // 2):
        even = pltpu.roll(heads, (128 - 8 * pair) % 128, 1)
        odd = pltpu.roll(heads, (188 - 8 * pair) % 128, 1)
        at = lane(heads.shape)
        spots.append(jnp.where(at < 4, even, jnp.where((at >= 64) & (at < 68), odd, 0.0)))
    lines = [turn_grad[...], attn_gain[...] / small[0:1, :], jnp.concatenate(spots, axis=1)]
    lines.append(jnp.zeros((128 - 56, small.shape[1]), f32))
    small_grad[...] = jnp.transpose(jnp.concatenate(lines, axis=0))


def attend_back(
    lengths, mixed_grad, stream_qkv, mixed_stream, log_total, proj, first_all, table, block,
    order_row, order_col, normed, wqkv, small, turn_grad,
):
    rows, width = normed.shape
    return pl.pallas_call(
        attend_back_kernel,
        out_shape=[
            jax.ShapeDtypeStruct((rows, 256), bf16),
            jax.ShapeDtypeStruct((GROUPS, 2, width // GROUPS, 128), bf16),
            jax.ShapeDtypeStruct((width, 128), f32),
        ],
        in_specs=[pl.BlockSpec(memory_space=pltpu.SMEM)] + whole(14),
        out_specs=whole(3),
        scratch_shapes=[
            pltpu.VMEM((8, 128), f32),
            pltpu.VMEM((rows, 128), bf16),
            pltpu.VMEM((rows, 128), bf16),
            pltpu.VMEM((rows, 128), bf16),
            pltpu.VMEM((128, rows), bf16),
            pltpu.VMEM((rows, 128), f32),
            pltpu.VMEM((rows, 128), f32),
            pltpu.VMEM((8, width), f32),
        ],
        compiler_params=pltpu.CompilerParams(vmem_limit_bytes=56 << 20),
        cost_estimate=cost_of(40),
        name="attend_back",
    )(
        lengths, mixed_grad, stream_qkv, mixed_stream, log_total, proj, first_all, table, block,
        order_row, order_col, normed, wqkv, small, turn_grad,
    )


def experts_kernel(
    rows_in, cotangent, hidden_in, routes, small, w,
    cot_all, layer_out, copy_part, xs_out, us_out, inner_out, dgu_out,
    xs, us, ys, weights, grads, acts, inner_s, dgu_s, ranks, x_buf, u_buf,
    outs, far, near, leaving, landed, sum_send, sum_recv,
    row_send, row_recv, sem, local_sem, out_sem,
):
    step = pl.program_id(0)
    me = lax.axis_index("tensor")
    blocks, held, width = xs.shape
    local = held // CAP
    hidden = inner_s.shape[1]
    e = lax.rem(step, local)
    here = pl.ds(pl.multiple_of(e * CAP, CAP), CAP)
    slots = blocks * CAP
    group = blocks // 2
    tile = group * CAP
    row_sems = row_send, row_recv
    long = ROW + 32

    def fetch_rows(b, slot):
        return pltpu.make_async_copy(rows_in.at[b], x_buf.at[slot], sem.at[0, slot])

    def fetch_cot(b, slot):
        return pltpu.make_async_copy(cot_all.at[b], u_buf.at[slot], sem.at[1, slot])

    sums = RowSums(outs, far, near, leaving, landed, (sum_send, sum_recv))

    def save_xs(b):
        return pltpu.make_async_copy(xs.at[b], xs_out.at[b], out_sem.at[0, b])

    def save_us(b):
        return pltpu.make_async_copy(us.at[b], us_out.at[b], out_sem.at[1, b])

    def save_tile(k):
        flat = pl.ds(pl.multiple_of(k * tile, tile), tile)
        return (
            pltpu.make_async_copy(dgu_s.at[flat], dgu_out.at[flat], out_sem.at[2, k]),
            pltpu.make_async_copy(inner_s.at[flat], inner_out.at[flat], out_sem.at[3, k]),
        )

    def save_back(b):
        flat = pl.ds(pl.multiple_of(b * long, 32), long)
        return pltpu.make_async_copy(acts.at[flat], copy_part.at[b], out_sem.at[4, b])

    def hits_of(b):
        slot = sublane((CAP, ROW))
        return [ranks[b, i : i + 1, :] == slot for i in range(local)]

    def table_of(hits):
        return jnp.concatenate([jnp.where(hit, 1.0, 0.0).astype(bf16) for hit in hits], axis=0)

    @pl.when(step == 0)
    def _():
        _, near, _, partner, right, left = neighbours()
        meet(others("tensor", blocks), [])
        rows_begin(cotangent, cot_all, row_sems)
        keep(cotangent, cot_all.at[me], local_sem.at[0])
        fetch_rows(0, 0).start()
        pick = (sublane((8, 32)) + me * local == lane((8, 32))) & (sublane((8, 32)) < local)
        pick = jnp.where(pick, 1.0, 0.0)
        before = jnp.where(sublane((ROW, ROW)) < lane((ROW, ROW)), 1.0, 0.0).astype(bf16)
        router = small[8:40, :].astype(bf16)

        @pl.loop(0, blocks)
        def _(b):
            slot = lax.rem(b, 2)

            @pl.when(b + 1 < blocks)
            def _():
                fetch_rows(b + 1, 1 - slot).start()

            fetch_rows(b, slot).wait()
            x = x_buf[slot]
            named = named_of(routes[b, 80:96, :])
            gates = gates_of(named, dot(router, x, ((1,), (1,))))
            own = lax.dot_general(
                pick,
                gates,
                (((1,), (0,)), ((), ())),
                precision=lax.Precision.HIGHEST,
                preferred_element_type=f32,
            )
            place = jnp.where(named > 0.5, dot(named.astype(bf16), before), -1.0)
            place = dot(pick.astype(bf16), place.astype(bf16))
            ranks[b] = place.astype(jnp.int32)
            hits = hits_of(b)
            xs[b] = dot(table_of(hits), x).astype(bf16)
            save_xs(b).start()
            for i in range(local):
                gate = jnp.sum(jnp.where(hits[i], own[i : i + 1], 0.0), axis=1, keepdims=True)
                weights[b, pl.ds(i * CAP, CAP), :] = jnp.broadcast_to(gate, (CAP, 128))

    @pl.when(step == 1)
    def _():
        rows_near(cotangent, cot_all, row_sems)

    @pl.when(step == 3)
    def _():
        rows_far(cotangent, cot_all, row_sems)

    @pl.when(step < local)
    def _():
        @pl.loop(0, 2)
        def _(t):
            part = pl.ds(t * group, group)
            flat = pl.ds(pl.multiple_of(e * slots + t * tile, tile), tile)
            x = xs[part, here, :].reshape(tile, width)
            gate_act = dot(x, w[0, 0])
            up_act = dot(x, w[0, 1])
            acts[flat, 0:hidden] = gate_act.astype(bf16)
            acts[flat, hidden : 2 * hidden] = up_act.astype(bf16)
            inner = gate_act / (1.0 + jnp.exp(-gate_act)) * up_act
            result = dot(inner.astype(bf16), w[0, 2], ((1,), (1,)))
            gate = weights[part, here, :].reshape(tile, 128)[:, 0:1]
            ys[part, here, :] = (gate * result).astype(bf16).reshape(group, CAP, width)

    @pl.when(step == local)
    def _():
        @pl.loop(0, blocks)
        def _(b):
            outs[b] = dot(table_of(hits_of(b)), ys[b], ((0,), (0,))).astype(bf16)

        rows_end(cotangent, cot_all, row_sems)
        sums.begin(0)
        sums.begin(1)
        pltpu.make_async_copy(cotangent, cot_all.at[me], local_sem.at[0]).wait()
        fetch_cot(0, 0).start()

        @pl.loop(0, blocks)
        def _(b):
            slot = lax.rem(b, 2)

            @pl.when(b + 1 < blocks)
            def _():
                fetch_cot(b + 1, 1 - slot).start()

            table = table_of(hits_of(b))
            fetch_cot(b, slot).wait()
            us[b] = dot(table, u_buf[slot]).astype(bf16)
            save_us(b).start()

    @pl.when(step >= local)
    def _():
        @pl.loop(0, 2)
        def _(t):
            part = pl.ds(t * group, group)
            flat = pl.ds(pl.multiple_of(e * slots + t * tile, tile), tile)
            gate_act = acts[flat, 0:hidden].astype(f32)
            up_act = acts[flat, hidden : 2 * hidden].astype(f32)
            u = us[part, here, :].reshape(tile, width)
            gate = weights[part, here, :].reshape(tile, 128)[:, 0:1]
            pulled = dot(u, w[0, 2])
            sig = 1.0 / (1.0 + jnp.exp(-gate_act))
            silu = gate_act * sig
            inner = silu * up_act
            grad = jnp.sum(inner * pulled, axis=1, keepdims=True)
            grads[part, here, :] = jnp.broadcast_to(grad, (tile, 128)).reshape(group, CAP, 128)
            inner_s[flat, :] = (gate * inner).astype(bf16)
            pulled = gate * pulled
            dg = (pulled * up_act * (sig * (1.0 + gate_act * (1.0 - sig)))).astype(bf16)
            du = (pulled * silu).astype(bf16)
            dgu_s[flat, 0:hidden] = dg
            dgu_s[flat, hidden : 2 * hidden] = du
            for copy in save_tile(e * 2 + t):
                copy.start()
            copy_grad = dot(dg, w[0, 0], ((1,), (1,))) + dot(du, w[0, 1], ((1,), (1,)))
            ys[part, here, :] = copy_grad.astype(bf16).reshape(group, CAP, width)

    @pl.when(step == local)
    def _():
        sums.go_on(0)

    @pl.when(step == local + 1)
    def _():
        sums.go_on(1)

    @pl.when(step == 2 * local - 1)
    def _():
        sums.cross()

        @pl.loop(0, blocks)
        def _(b):
            hits = hits_of(b)
            row = sublane((32, ROW)) - me * local
            line = jnp.zeros((32, ROW), f32)
            for i in range(local):
                column = grads[b, pl.ds(i * CAP, CAP), :][:, 0:1]
                total = jnp.sum(jnp.where(hits[i], column, 0.0), axis=0, keepdims=True)
                line = jnp.where(row == i, total, line)
            high = line.astype(bf16).astype(f32)
            both = jnp.concatenate(
                [high, line - high, jnp.zeros((32, width - 2 * ROW), f32)], axis=1
            )
            start = pl.multiple_of(b * long, 32)
            acts[pl.ds(start, ROW), :] = dot(table_of(hits), ys[b], ((0,), (0,))).astype(bf16)
            acts[pl.ds(pl.multiple_of(start + ROW, 32), 32), :] = both.astype(bf16)
            save_back(b).start()

        for b in range(blocks):
            save_xs(b).wait()
            save_us(b).wait()
            for copy in save_tile(b):
                copy.wait()
            save_back(b).wait()
        layer_out[...] = hidden_in[...] + sums.finish()


def experts_part(rows_in, cotangent, hidden_in, routes, small, expert_full):
    blocks, rows, width = rows_in.shape
    local, _, _, hidden = expert_full.shape
    slots = blocks * CAP
    dma = pltpu.SemaphoreType.DMA
    like = jax.ShapeDtypeStruct
    return pl.pallas_call(
        experts_kernel,
        grid=(2 * local,),
        out_shape=[
            like((blocks, rows, width), bf16),
            like((rows, width), f32),
            like((blocks, rows + 32, width), bf16),
            like((blocks, local * CAP, width), bf16),
            like((blocks, local * CAP, width), bf16),
            like((local * slots, hidden), bf16),
            like((local * slots, 2 * hidden), bf16),
        ],
        in_specs=anywhere(2)
        + [pl.BlockSpec((rows, width), lambda s: (0, 0), pipeline_mode=pl.Buffered(1))]
        + whole(2)
        + [pl.BlockSpec((1, 3, width, hidden), lambda s: (lax.rem(s, local), 0, 0, 0))],
        out_specs=anywhere(1)
        + [pl.BlockSpec((rows, width), lambda s: (0, 0), pipeline_mode=pl.Buffered(1))]
        + anywhere(5),
        scratch_shapes=[
            pltpu.VMEM((blocks, local * CAP, width), bf16),
            pltpu.VMEM((blocks, local * CAP, width), bf16),
            pltpu.VMEM((blocks, local * CAP, width), bf16),
            pltpu.VMEM((blocks, local * CAP, 128), f32),
            pltpu.VMEM((blocks, local * CAP, 128), f32),
            pltpu.VMEM((local * slots, 2 * hidden), bf16),
            pltpu.VMEM((local * slots, hidden), bf16),
            pltpu.VMEM((local * slots, 2 * hidden), bf16),
            pltpu.VMEM((blocks, 8, ROW), jnp.int32),
            pltpu.VMEM((2, rows, width), bf16),
            pltpu.VMEM((2, rows, width), bf16),
            pltpu.VMEM((blocks, rows, width), bf16),
            *row_sum_scratch(rows, width),
            dma((9,)),
            dma((9,)),
            dma((2, 2)),
            dma((1,)),
            dma((5, blocks)),
        ],
        compiler_params=pltpu.CompilerParams(
            collective_id=5, has_side_effects=True, vmem_limit_bytes=62 << 20
        ),
        cost_estimate=cost_of(65),
        name="experts",
    )(rows_in, cotangent, hidden_in, routes, small, expert_full)[1:]


def weight_grads_kernel(
    x, u, inner, dgu, copy_part,
    back, out,
    made, got, rows_s, far, near, leaving, landed, row_send, row_recv,
    core_send, core_recv, local, out_sem,
):
    e, c = pl.program_id(0), pl.program_id(1)
    experts, parts = pl.num_programs(0), pl.num_programs(1)
    step = e * parts + c
    _, here, _, partner, right, left = neighbours()
    _, _, core, _, _, other = group_place()
    hidden, rows = inner.shape[1], inner.shape[0]
    share = made.shape[1] // 2
    sums = RowSums(rows_s, far, near, leaving, landed, (row_send, row_recv))

    def core_push(e, c):
        part = pl.ds(c * share, share)
        return pltpu.make_async_remote_copy(
            src_ref=made.at[e, part, 1 - core],
            dst_ref=got.at[e, part],
            send_sem=core_send.at[e, c],
            recv_sem=core_recv.at[e, c],
            device_id=other,
            device_id_type=MESH,
        )

    def save(e):
        return pltpu.make_async_copy(made.at[e, :, core], out.at[:, e], out_sem.at[e])

    def add_core(e):
        for half in range(2):
            core_push(e, half).wait_recv()

        @pl.loop(0, 2 * share)
        def _(k):
            total = made[e, k, core].astype(f32) + got[e, k].astype(f32)
            made[e, k, core] = total.astype(bf16)

        save(e).start()

    @pl.when(step == 0)
    def _():
        load = pltpu.make_async_copy(copy_part, rows_s, local)
        load.start()
        meet([partner, here + right, here + left], [other["dp"]])
        load.wait()
        sums.begin(0)
        sums.begin(1)

    both = dot(x[...].reshape(rows, -1), dgu[...], ((0,), (0,)))
    part = pl.ds(c * share, share)
    shape = (share, 2, -1, hidden)
    made[e, part, :, 0] = both[:, :hidden].astype(bf16).reshape(shape)
    made[e, part, :, 1] = both[:, hidden:].astype(bf16).reshape(shape)
    down = dot(u[...].reshape(rows, -1), inner[...], ((0,), (0,)))
    made[e, part, :, 2] = down.astype(bf16).reshape(shape)
    core_push(e, c).start()

    @pl.when(step == 3)
    def _():
        sums.go_on(0)

    @pl.when(step == 5)
    def _():
        sums.go_on(1)

    @pl.when((e > 0) & (c == parts - 1))
    def _():
        add_core(e - 1)

    @pl.when(step == experts * parts - 1)
    def _():
        add_core(e)
        sums.cross()
        back[...] = sums.finish()
        for k in range(made.shape[0]):
            for half in range(2):
                core_push(k, half).wait_send()
            save(k).wait()


def weight_grads(xs, us, inner, dgu, copy_part):
    blocks, held, width = xs.shape
    local, hidden, slots = held // CAP, inner.shape[1], blocks * CAP
    col = width // 2
    long = copy_part.shape[1]
    shard = width // GROUPS
    rows = pl.BlockSpec((blocks, CAP, col), lambda e, c: (0, e, c))
    dma = pltpu.SemaphoreType.DMA
    return pl.pallas_call(
        weight_grads_kernel,
        grid=(local, width // col),
        out_shape=[
            jax.ShapeDtypeStruct((long, width), f32),
            jax.ShapeDtypeStruct((GROUPS // 2, local, 3, shard, hidden), bf16),
        ],
        in_specs=[
            rows,
            rows,
            pl.BlockSpec((slots, hidden), lambda e, c: (e, 0)),
            pl.BlockSpec((slots, 2 * hidden), lambda e, c: (e, 0)),
        ]
        + anywhere(1),
        out_specs=[pl.BlockSpec((long, width), lambda e, c: (0, 0))] + anywhere(1),
        scratch_shapes=[
            pltpu.VMEM((local, GROUPS // 2, 2, 3, shard, hidden), bf16),
            pltpu.VMEM((local, GROUPS // 2, 3, shard, hidden), bf16),
            pltpu.VMEM((blocks, long, width), bf16),
            *row_sum_scratch(long, width),
            dma((local, 2)),
            dma((local, 2)),
            dma,
            dma((local,)),
        ],
        compiler_params=pltpu.CompilerParams(
            collective_id=6, has_side_effects=True, vmem_limit_bytes=62 << 20
        ),
        cost_estimate=cost_of(45),
        name="weight_grads",
    )(xs, us, inner, dgu, copy_part)


def per_device(
    tokens,
    lengths,
    token_order,
    routes,
    cotangent,
    attn_gain,
    ffn_gain,
    router,
    w_query,
    w_key,
    w_value,
    w_output,
    query_gain,
    key_gain,
    w_gate,
    w_up,
    w_down,
):
    rows, width = tokens.shape
    group_rows = rows * RANKS

    own_experts = jnp.stack([w_gate, w_up, w_down.transpose(0, 2, 1)], axis=1)
    expert_full = lax.all_gather(own_experts, "dp", axis=2, tiled=True)
    tokens_all, qkv_cols, tiny_all, first_all, rest_all, small, routes_own = opening(
        tokens, w_query, w_key, w_value, w_output, attn_gain[None], ffn_gain[None], router,
        query_gain, key_gain, routes.T,
    )
    first_all = first_all.reshape((GROUPS,) + first_all.shape[3:])
    rest_all = rest_all.reshape((GROUPS,) + rest_all.shape[3:])

    frequency = ROTARY_BASE ** (-(np.arange(128) % 32) / 32.0)
    within = np.arange(ROW)[:, None] * frequency
    starts = (np.arange(group_rows // ROW) * ROW)[:, None] * frequency
    table = np.stack([np.cos(within), np.sin(within)]).astype(np.float32)
    block = np.stack([np.cos(starts), np.sin(starts)]).astype(np.float32)
    order_row, order_col = token_order, token_order.T
    normed_all, proj, stream_qkv, mixed_stream, log_total, mixed, wqkv = attend(
        lengths[0], tokens_all.reshape(group_rows, width), small, first_all, table, block,
        order_row, order_col,
    )
    mixed_own, hidden, normed2_all, done = middle(
        mixed.reshape(RANKS, rows, 128), rest_all, tokens, small
    )

    qkv_cols, _ = lax.optimization_barrier((qkv_cols, done))
    wqkv_all = lax.all_gather(qkv_cols, "dp", axis=0, tiled=False)
    layer_out, copy_part, xs, us, inner, dgu = experts_part(
        normed2_all, cotangent, hidden, tiny_all, small, expert_full
    )
    back, expert_grads = weight_grads(xs, us, inner, dgu, copy_part)
    groups = [[core + 2 * k for k in range(GROUPS // 2)] for core in range(2)]
    expert_sums = lax.psum_scatter(
        expert_grads, "dp", scatter_dimension=0, axis_index_groups=groups, tiled=False
    ).astype(f32)
    hidden_grad, mixed_grad, wo_grad, turn_grad = turn(
        back, hidden, cotangent, routes_own, small, mixed_own, rest_all
    )

    proj_grad, wqkv_grad, small_grad = attend_back(
        lengths[0], mixed_grad.reshape(group_rows, 128), stream_qkv, mixed_stream, log_total,
        proj, first_all, table, block, order_row, order_col, normed_all, wqkv, small, turn_grad,
    )
    grad_tokens, wqkv_sum, wo_sum, small_sum, head_sum = closing(
        proj_grad.reshape(RANKS, rows, 256), wo_grad.reshape((4, 2, 2) + wo_grad.shape[1:]),
        wqkv_grad.reshape((4, 2, 2) + wqkv_grad.shape[1:]), small_grad.reshape(4, 2, 2, -1, 128),
        wqkv_all, tokens, small, hidden_grad,
    )
    return (
        layer_out,
        grad_tokens,
        small_sum[:, 40],
        small_sum[:, 0],
        small_sum[:, 8:40],
        wqkv_sum[:, :128],
        wqkv_sum[:, 128:192],
        wqkv_sum[:, 192:256],
        wo_sum.T,
        head_sum[:4, 48:50].T,
        head_sum[:4, 50:51].T,
        expert_sums[:, 0],
        expert_sums[:, 1],
        expert_sums[:, 2].transpose(0, 2, 1),
    )


def solution(mesh):
    both = ("dp", "tensor")
    return jax.shard_map(
        per_device,
        mesh=mesh,
        in_specs=(
            P(both, None),
            P("dp", None),
            P("dp", None),
            P(both, None),
            P(both, None),
            P(both),
            P(both),
            P(both, None),
            P("dp", "tensor"),
            P("dp", "tensor"),
            P("dp", "tensor"),
            P("tensor", "dp"),
            P("tensor", "dp"),
            P("tensor", "dp"),
            P("tensor", "dp", None),
            P("tensor", "dp", None),
            P("tensor", None, "dp"),
        ),
        out_specs=(
            P(both, None),
            P(both, None),
            P(both),
            P(both),
            P(both, None),
            P("dp", "tensor"),
            P("dp", "tensor"),
            P("dp", "tensor"),
            P("tensor", "dp"),
            P("tensor", "dp"),
            P("tensor", "dp"),
            P("tensor", "dp", None),
            P("tensor", "dp", None),
            P("tensor", None, "dp"),
        ),
        check_vma=False,
    )
```

```python
import functools

import jax
import jax.numpy as jnp
import numpy as np
from jax import lax
from jax.experimental import pallas as pl
from jax.experimental.pallas import tpu as pltpu
from jax.sharding import PartitionSpec as P

CAP = 80
EPS = 1e-06
ROTARY_BASE = 10000.0
MASKED = -1e30
ROW = 256
CHUNK = 512
RANKS = 8
GROUPS = 16
MESH = pl.DeviceIdType.MESH
bf16 = jnp.bfloat16
f32 = jnp.float32


def dot(a, b, dims=((1,), (0,)), out=f32):
    return lax.dot_general(a, b, (dims, ((), ())), preferred_element_type=out)


def lane(shape):
    return lax.broadcasted_iota(jnp.int32, shape, len(shape) - 1)


def sublane(shape):
    return lax.broadcasted_iota(jnp.int32, shape, len(shape) - 2)


def cost_of(microseconds):
    return pl.CostEstimate(
        flops=microseconds * 1_100_000_000, bytes_accessed=1 << 20, transcendentals=0
    )


def whole(n):
    return [pl.BlockSpec(memory_space=pltpu.VMEM) for _ in range(n)]


def anywhere(n):
    return [pl.BlockSpec(memory_space=pl.ANY) for _ in range(n)]


def meet(ranks, groups):
    barrier = pltpu.get_barrier_semaphore()
    for peer in ranks:
        pl.semaphore_signal(barrier, inc=1, device_id={"tensor": peer}, device_id_type=MESH)
    for peer in groups:
        pl.semaphore_signal(barrier, inc=1, device_id={"dp": peer}, device_id_type=MESH)
    pl.semaphore_wait(barrier, len(ranks) + len(groups))


def push(src, dst, sems, index, peer):
    copy = pltpu.make_async_remote_copy(
        src_ref=src,
        dst_ref=dst,
        send_sem=sems[0].at[index],
        recv_sem=sems[1].at[index],
        device_id=peer,
        device_id_type=MESH,
    )
    copy.start()
    return copy


def keep(src, dst, sem):
    copy = pltpu.make_async_copy(src, dst, sem)
    copy.start()
    return copy


def others(name, size):
    me = lax.axis_index(name)
    return [lax.rem(me + k, size) for k in range(1, size)]


def neighbours():
    me = lax.axis_index("tensor")
    z = lax.rem(me, 4)
    here = me - z
    there = 4 - here
    right, left = lax.rem(z + 1, 4), lax.rem(z + 3, 4)
    return me, here, there, there + z, right, left


def row_copy(index, x, o, sems):
    me, here, there, partner, right, left = neighbours()
    half = o.shape[1] // 2
    low, high = pl.ds(0, half), pl.ds(half, half)
    both = pl.ds(0, 2 * half)
    to_right, to_left = {"tensor": here + right}, {"tensor": here + left}
    block, part, peer = (
        (me, both, {"tensor": partner}),
        (me, both, to_right),
        (me, both, to_left),
        (partner, both, to_right),
        (partner, both, to_left),
        (here + left, low, to_right),
        (here + right, high, to_left),
        (there + left, low, to_right),
        (there + right, high, to_left),
    )[index]
    return pltpu.make_async_remote_copy(
        src_ref=x if index < 3 else o.at[block, part],
        dst_ref=o.at[block, part],
        send_sem=sems[0].at[index],
        recv_sem=sems[1].at[index],
        device_id=peer,
        device_id_type=MESH,
    )


def rows_begin(x, o, sems):
    for index in range(3):
        row_copy(index, x, o, sems).start()


def rows_on(x, o, sems, arrived, leaving):
    for index, later in zip(arrived, leaving):
        row_copy(index, x, o, sems).wait_recv()
        for other in later:
            row_copy(other, x, o, sems).start()


def rows_near(x, o, sems):
    rows_on(x, o, sems, (1, 2, 0), ((5,), (6,), (3, 4)))


def rows_far(x, o, sems):
    rows_on(x, o, sems, (3, 4), ((7,), (8,)))


def rows_end(x, o, sems):
    for index in range(5, 9):
        row_copy(index, x, o, sems).wait_recv()
    for index in range(9):
        row_copy(index, x, o, sems).wait_send()


class RowSums:
    def __init__(self, blocks, far, near, leaving, landed, sems):
        self.blocks, self.far, self.near = blocks, far, near
        self.leaving, self.landed, self.sems = leaving, landed, sems
        self.me, here, there, self.partner, self.right, self.left = neighbours()
        self.here, self.z, self.bases = here, self.me - here, (there, here)
        self.half = blocks.shape[1] // 2
        self.parts = pl.ds(0, self.half), pl.ds(self.half, self.half)

    def copy(self, src, dst, index, peer):
        return pltpu.make_async_remote_copy(
            src_ref=src,
            dst_ref=dst,
            send_sem=self.sems[0].at[index],
            recv_sem=self.sems[1].at[index],
            device_id={"tensor": peer},
            device_id_type=MESH,
        )

    def far_copy(self, side, way):
        block = self.bases[side] + lax.rem(self.z + 2, 4)
        peer = self.here + (self.right, self.left)[way]
        src = self.blocks.at[block, self.parts[way]]
        return self.copy(src, self.far.at[side, way], side * 4 + way, peer)

    def near_copy(self, side, way):
        step = (self.right, self.left)[way]
        src = self.blocks.at[self.bases[side] + step]
        return self.copy(src, self.near.at[side, way], side * 4 + 2 + way, self.here + step)

    def cross_copy(self):
        return self.copy(self.leaving, self.landed, 8, self.partner)

    def begin(self, side):
        for way in range(2):
            self.far_copy(side, way).start()

    def go_on(self, side):
        for way in range(2):
            self.far_copy(side, way).wait_recv()
            at = self.bases[side] + (self.right, self.left)[way]
            total = self.blocks[at, self.parts[way], :].astype(f32)
            total = total + self.far[side, way].astype(f32)
            self.blocks[at, self.parts[way], :] = total.astype(bf16)
            self.near_copy(side, way).start()

    def total(self, side):
        total = self.blocks[self.bases[side] + self.z].astype(f32)
        for way in range(2):
            self.near_copy(side, way).wait_recv()
            total = total + self.near[side, way].astype(f32)
        return total

    def cross(self):
        self.leaving[...] = self.total(0).astype(bf16)
        self.cross_copy().start()

    def finish(self):
        total = self.total(1)
        self.cross_copy().wait_recv()
        total = total + self.landed[...].astype(f32)
        for side in range(2):
            for way in range(2):
                self.far_copy(side, way).wait_send()
                self.near_copy(side, way).wait_send()
        self.cross_copy().wait_send()
        return total


def row_sum_scratch(rows, width):
    dma = pltpu.SemaphoreType.DMA
    return [
        pltpu.VMEM((2, 2, rows // 2, width), bf16),
        pltpu.VMEM((2, 2, rows, width), bf16),
        pltpu.VMEM((rows, width), bf16),
        pltpu.VMEM((rows, width), bf16),
        dma((9,)),
        dma((9,)),
    ]


def group_place():
    group = lax.axis_index("dp")
    core, side, y = lax.rem(group, 2), lax.rem(group // 2, 2), group // 4
    across = {"dp": group + 2 - 4 * side}
    other = {"dp": group + 1 - 2 * core}
    column = [(lax.rem(y + k, 4), {"dp": lax.rem(y + k, 4) * 4 + side * 2 + core}) for k in (2, 1, 3)]
    return y, side, core, across, column, other


def gather_first(src, o, sems):
    y, side, core, across, _, _ = group_place()
    return push(src, o.at[y, side, core], sems, 0, across)


def gather_second(first, own, o, sems):
    y, _, core, _, column, _ = group_place()
    first.wait_recv()
    own.wait()
    part = o.at[y, :, core]
    return [push(part, part, sems, 1 + k, peer) for k, (_, peer) in enumerate(column)]


def gather_third(second, o, sems):
    _, _, core, _, _, other = group_place()
    for copy in second:
        copy.wait_recv()
    part = o.at[:, :, core]
    return push(part, part, sems, 4, other)


def opening_kernel(
    tokens, w_query, w_key, w_value, w_output, attn_gain, ffn_gain, router, query_gain, key_gain, routes,
    tokens_all, qkv_all, tiny_all, first_all, rest_all, small, routes_own,
    payload, lines, small_rows,
    row_send, row_recv, qkv_send, qkv_recv, tiny_send, tiny_recv, first_send, first_recv,
    rest_send, rest_recv, local,
):
    me = lax.axis_index("tensor")
    y, side, core, across, column, other = group_place()
    ranks = others("tensor", RANKS)
    lines[...] = jnp.zeros_like(lines)
    lines[0, 0:1, 0:8] = attn_gain[...].astype(f32)
    lines[0, 1:2, 0:8] = ffn_gain[...].astype(f32)
    lines[1, :, 0:32] = router[...].astype(f32)
    lines[2, 0:2, 0:4] = query_gain[...].astype(f32)
    lines[2, 2:3, 0:4] = key_gain[...].astype(f32)
    lines[3, :, 0:8] = jnp.transpose(lines[0])[0:8]
    block = lines[3] + pltpu.roll(lines[1], 2, 1)
    payload[0:64] = w_query[...]
    payload[64:128, 0:64] = w_key[...]
    payload[64:128, 64:128] = w_value[...]
    payload[128:144] = jnp.concatenate([block, lines[2]], axis=0).astype(bf16)
    payload[144:208] = w_output[...]
    picks = routes[...].astype(f32)
    picks = jnp.concatenate([picks[:, 0:128], picks[:, 128:256]], axis=0).astype(bf16)
    payload[208:224] = picks
    routes_own[...] = picks
    meet(ranks, [across["dp"], other["dp"]] + [peer["dp"] for _, peer in column])
    own, qkv, rest = payload.at[0:144], payload.at[0:128], payload.at[128:224]
    tiny = [
        push(rest, tiny_all.at[me], (tiny_send, tiny_recv), k, {"tensor": peer})
        for k, peer in enumerate(ranks)
    ]
    first_sems, rest_sems = (first_send, first_recv), (rest_send, rest_recv)
    first_one = gather_first(own, first_all, first_sems)
    row_sems = row_send, row_recv
    rows_begin(tokens, tokens_all, row_sems)
    tiny_own = keep(rest, tiny_all.at[me], local.at[0])
    first_own = keep(own, first_all.at[y, side, core], local.at[1])
    kept = [
        keep(tokens, tokens_all.at[me], local.at[2]),
        keep(qkv, qkv_all.at[me], local.at[3]),
    ]
    for copy in tiny:
        copy.wait_recv()
    tiny_own.wait()
    part = tiny_all.at[:, pl.ds(0, 80)]
    rest_one = gather_first(part, rest_all, rest_sems)
    rest_own = keep(part, rest_all.at[y, side, core], local.at[4])
    first_two = gather_second(first_one, first_own, first_all, first_sems)
    rows_near(tokens, tokens_all, row_sems)
    rest_two = gather_second(rest_one, rest_own, rest_all, rest_sems)
    first_three = gather_third(first_two, first_all, first_sems)
    qkv_sent = [
        push(qkv, qkv_all.at[me], (qkv_send, qkv_recv), k, {"tensor": peer})
        for k, peer in enumerate(ranks)
    ]
    rows_far(tokens, tokens_all, row_sems)
    rest_three = gather_third(rest_two, rest_all, rest_sems)
    rest_three.wait_recv()
    gathered = keep(rest_all.at[:, :, :, :, pl.ds(0, 16)], small_rows, local.at[5])
    gathered.wait()
    turned_rows = jnp.transpose(small_rows[:, :, :, :, 0:8, :].astype(f32).reshape(-1, 128))
    small[0:8] = turned_rows[0:8]
    small[8:40] = turned_rows[2:34]
    rows_end(tokens, tokens_all, row_sems)
    first_three.wait()
    rest_three.wait_send()
    for copy in qkv_sent:
        copy.wait()
    for copy in (*tiny, first_one, rest_one, *first_two, *rest_two):
        copy.wait_send()
    for copy in kept:
        copy.wait()


def opening(tokens, *weights):
    dma = pltpu.SemaphoreType.DMA
    like = jax.ShapeDtypeStruct
    return pl.pallas_call(
        opening_kernel,
        out_shape=[
            like((RANKS,) + tokens.shape, bf16),
            like((RANKS, 128, 128), bf16),
            like((RANKS, 96, 128), bf16),
            like((4, 2, 2, 144, 128), bf16),
            like((4, 2, 2, RANKS, 80, 128), bf16),
            like((40, tokens.shape[1]), f32),
            like((16, 128), bf16),
        ],
        in_specs=anywhere(1) + whole(10),
        out_specs=anywhere(5) + whole(2),
        scratch_shapes=[
            pltpu.VMEM((224, 128), bf16),
            pltpu.VMEM((4, 8, 128), f32),
            pltpu.VMEM((4, 2, 2, RANKS, 16, 128), bf16),
            dma((9,)),
            dma((9,)),
        ]
        + [dma((7,))] * 4
        + [dma((5,))] * 4
        + [dma((6,))],
        compiler_params=pltpu.CompilerParams(
            collective_id=1, has_side_effects=True, vmem_limit_bytes=63 << 20
        ),
        cost_estimate=cost_of(50),
        name="opening",
    )(tokens, *weights)


def middle_kernel(
    mixed, rest, tokens, small,
    mixed_own, hidden, normed2_all, done,
    landed, normed2, mix_send, mix_recv, row_send, row_recv, local,
):
    me, here, _, partner, right, left = neighbours()
    ranks = others("tensor", RANKS)
    meet(ranks, [])
    sent = [
        push(mixed.at[peer], landed.at[me], (mix_send, mix_recv), k, {"tensor": peer})
        for k, peer in enumerate(ranks)
    ]
    own = keep(mixed.at[me], landed.at[me], local.at[0])
    for copy in sent:
        copy.wait_recv()
    own.wait()
    total = tokens[...].astype(f32)
    for s in range(RANKS):
        weight = rest[:, s, 16:80, :].reshape(-1, 128)
        total = total + dot(landed[s], weight, ((1,), (1,)))
    mixed_own[...] = landed[...]
    hidden[...] = total
    scale = lax.rsqrt(jnp.mean(total * total, axis=1, keepdims=True) + EPS)
    normed2[...] = (total * scale * small[1:2, :]).astype(bf16)
    row_sems = row_send, row_recv
    rows_begin(normed2, normed2_all, row_sems)
    kept = keep(normed2, normed2_all.at[me], local.at[1])
    rows_near(normed2, normed2_all, row_sems)
    rows_far(normed2, normed2_all, row_sems)
    rows_end(normed2, normed2_all, row_sems)
    for copy in sent:
        copy.wait_send()
    kept.wait()
    done[...] = jnp.zeros_like(done)


def middle(mixed, rest, tokens, small):
    dma = pltpu.SemaphoreType.DMA
    rows, width = tokens.shape
    return pl.pallas_call(
        middle_kernel,
        out_shape=[
            jax.ShapeDtypeStruct(mixed.shape, bf16),
            jax.ShapeDtypeStruct((rows, width), f32),
            jax.ShapeDtypeStruct((RANKS, rows, width), bf16),
            jax.ShapeDtypeStruct((8, 128), f32),
        ],
        in_specs=anywhere(1) + whole(3),
        out_specs=whole(2) + anywhere(1) + whole(1),
        scratch_shapes=[
            pltpu.VMEM(mixed.shape, bf16),
            pltpu.VMEM((rows, width), bf16),
            dma((7,)),
            dma((7,)),
            dma((9,)),
            dma((9,)),
            dma((2,)),
        ],
        compiler_params=pltpu.CompilerParams(
            collective_id=2, has_side_effects=True, vmem_limit_bytes=63 << 20
        ),
        cost_estimate=cost_of(40),
        name="middle",
    )(mixed, rest, tokens, small)


def named_of(routes):
    picks = routes.astype(f32)
    picks = jnp.concatenate([picks[0:8], picks[8:16]], axis=1)
    expert = sublane((32, ROW)).astype(f32)
    found = jnp.zeros((32, ROW), f32)
    for k in range(8):
        found = jnp.where(picks[k : k + 1] == expert, 1.0, found)
    return found


def gates_of(named, logits):
    logits = jnp.where(named > 0.5, logits, MASKED)
    odds = jnp.where(named > 0.5, jnp.exp(logits - jnp.max(logits, axis=0, keepdims=True)), 0.0)
    return odds / jnp.sum(odds, axis=0, keepdims=True)


def norm_back(value, scales, grad):
    scale = lax.rsqrt(jnp.mean(value * value, axis=1, keepdims=True) + EPS)
    scaled = value * scale
    weighted = grad * scales
    moved = scale * (weighted - scaled * jnp.mean(weighted * scaled, axis=1, keepdims=True))
    return moved, scaled


def turn_kernel(
    back, hidden, cotangent, routes, small, mixed_own, rest,
    hidden_grad, mixed_grad, wo_grad, small_grad,
    leaving, landed, mix_send, mix_recv, local,
):
    me = lax.axis_index("tensor")
    ranks = others("tensor", RANKS)
    meet(ranks, [])
    value = hidden[...]
    gain = small[1:2, :]
    router = small[8:40, :].astype(bf16)
    scale = lax.rsqrt(jnp.mean(value * value, axis=1, keepdims=True) + EPS)
    normed2 = (value * scale * gain).astype(bf16)
    gates = gates_of(named_of(routes[...]), dot(router, normed2, ((1,), (1,))))
    pieces = back[ROW:, 0 : 2 * ROW]
    gate_grad = pieces[:, :ROW] + pieces[:, ROW:]
    inner = jnp.sum(gates * gate_grad, axis=0, keepdims=True)
    logit_grad = (gates * (gate_grad - inner)).astype(bf16)
    grad = dot(logit_grad, router, ((0,), (0,)))
    grad = grad + back[0:ROW, :]
    moved, scaled = norm_back(value, gain, grad)
    total = cotangent[...].astype(f32) + moved
    branch = total.astype(bf16)
    for s in range(RANKS):
        weight = rest[:, s, 16:80, :].reshape(-1, 128)
        leaving[s] = dot(branch, weight).astype(bf16)
    sent = [
        push(leaving.at[peer], landed.at[me], (mix_send, mix_recv), k, {"tensor": peer})
        for k, peer in enumerate(ranks)
    ]
    own = keep(leaving.at[me], landed.at[me], local.at[0])
    hidden_grad[...] = total
    small_grad[0:8, :] = jnp.broadcast_to(
        jnp.sum(grad * scaled, axis=0, keepdims=True), (8, grad.shape[1])
    )
    small_grad[8:40, :] = dot(logit_grad, normed2)
    for s in range(RANKS):
        part = dot(branch, mixed_own[s], ((0,), (0,)))
        wo_grad[:, s] = part.astype(bf16).reshape(GROUPS, -1, 128)
    for copy in sent:
        copy.wait()
    own.wait()
    mixed_grad[...] = landed[...]


def turn(back, hidden, cotangent, routes, small, mixed_own, rest):
    dma = pltpu.SemaphoreType.DMA
    rows, width = hidden.shape
    return pl.pallas_call(
        turn_kernel,
        out_shape=[
            jax.ShapeDtypeStruct((rows, width), f32),
            jax.ShapeDtypeStruct(mixed_own.shape, bf16),
            jax.ShapeDtypeStruct((GROUPS, RANKS, width // GROUPS, 128), bf16),
            jax.ShapeDtypeStruct((40, width), f32),
        ],
        in_specs=whole(7),
        out_specs=whole(4),
        scratch_shapes=[
            pltpu.VMEM(mixed_own.shape, bf16),
            pltpu.VMEM(mixed_own.shape, bf16),
            dma((7,)),
            dma((7,)),
            dma((1,)),
        ],
        compiler_params=pltpu.CompilerParams(
            collective_id=3, has_side_effects=True, vmem_limit_bytes=63 << 20
        ),
        cost_estimate=cost_of(15),
        name="turn",
    )(back, hidden, cotangent, routes, small, mixed_own, rest)


def closing_kernel(
    proj_grad, wo_grad, wqkv_grad, small_grad, wqkv_all, tokens, small, hidden_grad, expert_pair,
    grad_tokens, wqkv_sum, wo_sum, small_sum, head_sum, expert_far,
    proj_in,
    wo_core, wo_y, wo_x, wo_half, wo_pair,
    wqkv_core, wqkv_y, wqkv_x, wqkv_half, wqkv_pair,
    small_core, small_y, small_x, small_half, small_pair,
    wo_out, small_out, wo_last, small_last,
    proj_send, proj_recv, group_send, group_recv, last_send, last_recv, far_sems, local,
):
    me = lax.axis_index("tensor")
    y, side, core, across, column, other = group_place()
    ranks = others("tensor", RANKS)
    meet(ranks, [across["dp"], other["dp"]] + [peer["dp"] for _, peer in column])
    crossing = pltpu.make_async_remote_copy(
        src_ref=expert_pair.at[1 - side],
        dst_ref=expert_far,
        send_sem=far_sems.at[0],
        recv_sem=far_sems.at[1],
        device_id=across,
        device_id_type=MESH,
    )
    crossing.start()
    away = 1 - core
    arrays = (
        (wo_grad, wo_core, wo_half, wo_y, wo_pair, wo_x),
        (wqkv_grad, wqkv_core, wqkv_half, wqkv_y, wqkv_pair, wqkv_x),
        (small_grad, small_core, small_half, small_y, small_pair, small_x),
    )
    sems = [(group_send.at[a], group_recv.at[a]) for a in range(3)]
    first = [
        push(array[0].at[:, :, away], array[1], sems[a], 0, other) for a, array in enumerate(arrays)
    ]
    proj = [
        push(proj_grad.at[peer], proj_in.at[me], (proj_send, proj_recv), k, {"tensor": peer})
        for k, peer in enumerate(ranks)
    ]
    proj_own = keep(proj_grad.at[me], proj_in.at[me], local.at[0])
    second = []
    for a, (whole_grad, landed, half, down, _, _) in enumerate(arrays):
        first[a].wait_recv()
        total = whole_grad[:, :, core].astype(f32) + landed[...].astype(f32)
        half[...] = total.astype(half.dtype)
        second.append(
            [push(half.at[at], down.at[k], sems[a], 1 + k, peer) for k, (at, peer) in enumerate(column)]
        )
    third = []
    for a, (_, _, half, down, pair, far) in enumerate(arrays):
        for copy in second[a]:
            copy.wait_recv()
        total = half[y].astype(f32)
        for k in range(3):
            total = total + down[k].astype(f32)
        pair[...] = total.astype(pair.dtype)
        third.append(push(pair.at[1 - side], far, sems[a], 4, across))
    for copy in proj:
        copy.wait_recv()
    proj_own.wait()
    grad = jnp.zeros(grad_tokens.shape, f32)
    for s in range(RANKS):
        query = wqkv_all[:, s, 0:64, :].reshape(-1, 128)
        rest = wqkv_all[:, s, 64:128, :].reshape(-1, 128)
        grad = grad + dot(proj_in[s, :, 0:128], query, ((1,), (1,)))
        grad = grad + dot(proj_in[s, :, 128:256], rest, ((1,), (1,)))
    moved, _ = norm_back(tokens[...].astype(f32), small[0:1, :], grad)
    grad_tokens[...] = hidden_grad[...] + moved
    sums = []
    for a, (_, _, _, _, pair, far) in enumerate(arrays):
        third[a].wait_recv()
        sums.append(pair[side].astype(f32) + far[...].astype(f32))
    wo_out[...] = sums[0].astype(bf16)
    head_sum[...] = sums[2][0:8]
    small_out[...] = sums[2].reshape(small_out.shape)
    last = []
    for a, (src, dst) in enumerate(((wo_out, wo_last), (small_out, small_last))):
        pair = last_send.at[a], last_recv.at[a]
        last += [
            push(src.at[peer], dst.at[me], pair, k, {"tensor": peer}) for k, peer in enumerate(ranks)
        ]
    kept = [
        keep(wo_out.at[me], wo_last.at[me], local.at[1]),
        keep(small_out.at[me], small_last.at[me], local.at[2]),
    ]
    wqkv_sum[:, 0:128] = sums[1][0]
    wqkv_sum[:, 128:256] = sums[1][1]
    for copy in last:
        copy.wait_recv()
    for copy in kept:
        copy.wait()
    total = jnp.zeros(wo_sum.shape, f32)
    small_total = jnp.zeros(small_sum.shape, f32)
    for s in range(RANKS):
        total = total + wo_last[s].astype(f32)
        small_total = small_total + small_last[s]
    wo_sum[...] = total
    small_sum[...] = small_total
    for copy in (*proj, *first, *third, *last):
        copy.wait_send()
    for copies in second:
        for copy in copies:
            copy.wait_send()
    crossing.wait()


def closing(
    proj_grad, wo_grad, wqkv_grad, small_grad, wqkv_all, tokens, small, hidden_grad, expert_pair
):
    dma = pltpu.SemaphoreType.DMA
    shard = wo_grad.shape[4]
    rows = shard // RANKS
    steps = []
    for array in (wo_grad, wqkv_grad, small_grad):
        block = array.shape[3:]
        for lead in ((4, 2), (3, 2), (), (4, 2), (2,)):
            steps.append(pltpu.VMEM(lead + block, array.dtype))
    return pl.pallas_call(
        closing_kernel,
        out_shape=[
            jax.ShapeDtypeStruct(hidden_grad.shape, f32),
            jax.ShapeDtypeStruct((shard, 256), f32),
            jax.ShapeDtypeStruct((shard, 128), f32),
            jax.ShapeDtypeStruct((rows, 128), f32),
            jax.ShapeDtypeStruct((8, 128), f32),
            jax.ShapeDtypeStruct(expert_pair.shape[1:], bf16),
        ],
        in_specs=whole(8) + anywhere(1),
        out_specs=whole(5) + anywhere(1),
        scratch_shapes=[
            pltpu.VMEM(proj_grad.shape, bf16),
            *steps,
            pltpu.VMEM((RANKS, shard, 128), bf16),
            pltpu.VMEM((RANKS, rows, 128), f32),
            pltpu.VMEM((RANKS, shard, 128), bf16),
            pltpu.VMEM((RANKS, rows, 128), f32),
            dma((7,)),
            dma((7,)),
            dma((3, 5)),
            dma((3, 5)),
            dma((2, 7)),
            dma((2, 7)),
            dma((2,)),
            dma((3,)),
        ],
        compiler_params=pltpu.CompilerParams(
            collective_id=4, has_side_effects=True, vmem_limit_bytes=63 << 20
        ),
        cost_estimate=cost_of(45),
        name="closing",
    )(
        proj_grad, wo_grad, wqkv_grad, small_grad, wqkv_all, tokens, small, hidden_grad, expert_pair
    )


def sequence_start(place, lengths):
    first, second = lengths[0], lengths[0] + lengths[1]
    return jnp.where(place < first, 0, jnp.where(place < second, first, second))


def swap_halves(x):
    return jnp.where(lane(x.shape) % 64 < 32, pltpu.roll(x, 96, 1), pltpu.roll(x, 32, 1))


def head_mean(x, heads):
    low = lane(x.shape) < 64
    first = jnp.sum(jnp.where(low, x, 0.0), axis=1, keepdims=True) / 64
    if heads == 1:
        return jnp.where(low, first, 0.0)
    second = jnp.sum(jnp.where(low, 0.0, x), axis=1, keepdims=True) / 64
    return jnp.where(low, first, second)


def head_gains(first_all):
    total = jnp.zeros((8, 128), f32)
    for g in range(GROUPS):
        piece = first_all[g, 128:144, :].astype(f32)[8:16]
        total = total + pltpu.roll(jnp.where(lane(piece.shape) < 4, piece, 0.0), 4 * g, 1)
    low = lane((1, 128)) < 64
    return jnp.where(low, total[0:1], pltpu.roll(total[1:2], 64, 1)), total[2:3]


def turned(table, block, b):
    within_cos, within_sin = table[0], table[1]
    block_cos, block_sin = block[0, pl.ds(b, 1), :], block[1, pl.ds(b, 1), :]
    cos = within_cos * block_cos - within_sin * block_sin
    sin = within_sin * block_cos + within_cos * block_sin
    return cos, jnp.where(lane(sin.shape) % 64 < 32, -sin, sin)


def columns_of(row):
    return jnp.transpose(jnp.broadcast_to(row, (128, row.shape[1])))


def attend_kernel(
    lengths, x, small, first_all, table, block, order, cotangent,
    normed, proj, stream_qkv, mixed_stream, log_total, mixed, wqkv, cot_all,
    x_s, normed_s, proj_s, token_qkv, keys, values,
    row_send, row_recv, load_sem, save_sem, local,
):
    rows = x.shape[0]
    blocks = rows // ROW
    row_sems = row_send, row_recv

    def load(b):
        at = pl.ds(pl.multiple_of(b * ROW, ROW), ROW)
        return pltpu.make_async_copy(x.at[at], x_s.at[at], load_sem.at[b])

    def save(b):
        at = pl.ds(pl.multiple_of(b * ROW, ROW), ROW)
        return (
            pltpu.make_async_copy(normed_s.at[at], normed.at[at], save_sem.at[0, b]),
            pltpu.make_async_copy(proj_s.at[at], proj.at[at], save_sem.at[1, b]),
        )

    for b in range(blocks):
        load(b).start()
    me, here, _, partner, right, left = neighbours()
    own = pltpu.make_async_copy(cotangent, cot_all.at[me], local)
    own.start()
    q_gain, k_gain = head_gains(first_all)
    wqkv[:, 0:128] = first_all[:, 0:64, :].reshape(-1, 128)
    wqkv[:, 128:256] = first_all[:, 64:128, :].reshape(-1, 128)
    meet([partner, here + right, here + left], [])
    rows_begin(cotangent, cot_all, row_sems)

    @pl.loop(0, blocks)
    def _(b):
        at = pl.ds(pl.multiple_of(b * ROW, ROW), ROW)
        load(b).wait()
        v = x_s[at, :].astype(f32)
        r = lax.rsqrt(jnp.mean(v * v, axis=1, keepdims=True) + EPS)
        n = (v * r * small[0:1, :]).astype(bf16)
        normed_s[at, :] = n
        p = dot(n, wqkv[...])
        proj_s[at, :] = p
        for copy in save(b):
            copy.start()
        q, kv = p[:, :128], p[:, 128:]
        low = lane(kv.shape) < 64
        q = q * lax.rsqrt(head_mean(q * q, 2) + EPS) * q_gain
        k = kv * lax.rsqrt(head_mean(kv * kv, 1) + EPS) * k_gain
        token_qkv[at, 0:128] = q.astype(bf16)
        token_qkv[at, 128:256] = jnp.where(low, k, kv).astype(bf16)

    @pl.loop(0, blocks)
    def _(b):
        at = pl.ds(pl.multiple_of(b * ROW, ROW), ROW)
        place = sublane((ROW, rows)) + b * ROW
        moves = jnp.where(order[...] == place, 1.0, 0.0).astype(bf16)
        moved = dot(moves, token_qkv[...])
        cos, sin = turned(table, block, b)
        q, kv = moved[:, :128], moved[:, 128:]
        low = lane(kv.shape) < 64
        q = (q * cos + swap_halves(q) * sin) * 0.125
        kv = jnp.where(low, kv * cos + swap_halves(kv) * sin, kv)
        stream_qkv[at, 0:128] = q.astype(bf16)
        stream_qkv[at, 128:256] = kv.astype(bf16)
        other = pltpu.roll(kv, 64, 1)
        keys[at, :] = jnp.where(low, kv, other).astype(bf16)
        values[at, :] = jnp.where(low, other, 1.0).astype(bf16)

    @pl.loop(0, blocks)
    def _(b):
        at = pl.ds(pl.multiple_of(b * ROW, ROW), ROW)
        q = stream_qkv[at, 0:128]
        low = lane(q.shape) < 64
        zero = jnp.zeros_like(q)
        q0, q1 = jnp.where(low, q, zero), jnp.where(low, zero, q)
        place = sublane((ROW, 1)) + b * ROW
        start = sequence_start(place, lengths)

        def step(begin, size, totals, diagonal):
            t0, t1 = totals
            here = pl.ds(pl.multiple_of(begin, ROW), size)
            k, v = keys[here, :], values[here, :]
            key = lane((ROW, size)) + begin
            allowed = key >= start
            if diagonal:
                allowed = allowed & (key <= place)
            e0 = jnp.where(allowed, jnp.exp(dot(q0, k, ((1,), (1,)))), 0.0).astype(bf16)
            e1 = jnp.where(allowed, jnp.exp(dot(q1, k, ((1,), (1,)))), 0.0).astype(bf16)
            return t0 + dot(e0, v), t1 + dot(e1, v)

        none = jnp.zeros((ROW, 128), f32)
        totals = step(b * ROW, ROW, (none, none), True)
        totals = lax.fori_loop(
            0, b // 2, lambda j, t: step(j * CHUNK, CHUNK, t, False), totals
        )
        t0, t1 = lax.fori_loop(
            0, lax.rem(b, 2), lambda j, t: step((b - 1) * ROW, ROW, t, False), totals
        )
        low = lane((ROW, 128)) < 64
        other0, other1 = pltpu.roll(t0, 64, 1), pltpu.roll(t1, 64, 1)
        total = jnp.where(low, other0, t1)
        out = jnp.where(low, t0, other1) / total
        log_total[at, :] = jnp.log(total)
        mixed_stream[at, :] = out.astype(bf16)

        @pl.when(b == 0)
        def _():
            rows_on(cotangent, cot_all, row_sems, (1, 2), ((5,), (6,)))

        @pl.when(b == 2)
        def _():
            rows_on(cotangent, cot_all, row_sems, (0,), ((3, 4),))

        @pl.when(b == 6)
        def _():
            rows_far(cotangent, cot_all, row_sems)

    @pl.loop(0, blocks)
    def _(b):
        at = pl.ds(pl.multiple_of(b * ROW, ROW), ROW)
        column = columns_of(order[:, at].astype(f32))[:, 0:1]
        moves = jnp.where(column == lane((ROW, rows)).astype(f32), 1.0, 0.0).astype(bf16)
        mixed[at, :] = dot(moves, mixed_stream[...]).astype(bf16)

    for b in range(blocks):
        for copy in save(b):
            copy.wait()
    rows_end(cotangent, cot_all, row_sems)
    own.wait()


def attend(lengths, x, small, first_all, table, block, order, cotangent):
    rows, width = x.shape
    dma = pltpu.SemaphoreType.DMA
    return pl.pallas_call(
        attend_kernel,
        out_shape=[
            jax.ShapeDtypeStruct((rows, width), bf16),
            jax.ShapeDtypeStruct((rows, 256), f32),
            jax.ShapeDtypeStruct((rows, 256), bf16),
            jax.ShapeDtypeStruct((rows, 128), bf16),
            jax.ShapeDtypeStruct((rows, 128), f32),
            jax.ShapeDtypeStruct((rows, 128), bf16),
            jax.ShapeDtypeStruct((width, 256), bf16),
            jax.ShapeDtypeStruct((RANKS,) + cotangent.shape, bf16),
        ],
        in_specs=[pl.BlockSpec(memory_space=pltpu.SMEM)] + anywhere(1) + whole(5) + anywhere(1),
        out_specs=anywhere(2) + whole(5) + anywhere(1),
        scratch_shapes=[
            pltpu.VMEM((rows, width), bf16),
            pltpu.VMEM((rows, width), bf16),
            pltpu.VMEM((rows, 256), f32),
            pltpu.VMEM((rows, 256), bf16),
            pltpu.VMEM((rows, 128), bf16),
            pltpu.VMEM((rows, 128), bf16),
            dma((9,)),
            dma((9,)),
            dma((rows // ROW,)),
            dma((2, rows // ROW)),
            dma,
        ],
        compiler_params=pltpu.CompilerParams(
            collective_id=5, has_side_effects=True, vmem_limit_bytes=63 << 20
        ),
        cost_estimate=cost_of(30),
        name="attend",
    )(lengths, x, small, first_all, table, block, order, cotangent)


def attend_back_kernel(
    lengths, mixed_grad, stream_qkv, mixed_stream, log_total, proj, first_all, table, block,
    order, normed, wqkv, small, turn_grad, out_part, expert_grads,
    proj_grad, wqkv_grad, small_grad, out_sum, expert_pair,
    gain_grad, keys, values, out_grad, query_grad, key_grad, value_grad, attn_gain,
    normed_s, proj_s, outs, far, near, leaving, landed, sum_send, sum_recv, load_sem,
    far_w, near_w, near_in, own_w, y_send, y_recv,
):
    rows = proj.shape[0]
    blocks = rows // ROW
    sums = RowSums(outs, far, near, leaving, landed, (sum_send, sum_recv))
    loads = [
        keep(src, dst, load_sem.at[k])
        for k, (src, dst) in enumerate(((out_part, outs), (normed, normed_s), (proj, proj_s)))
    ]
    _, here, _, partner, right, left = neighbours()
    y, side, core, _, _, _ = group_place()
    ways = lax.rem(y + 1, 4), lax.rem(y + 3, 4)

    def y_copy(index, src, dst, way):
        return pltpu.make_async_remote_copy(
            src_ref=src,
            dst_ref=dst,
            send_sem=y_send.at[index],
            recv_sem=y_recv.at[index],
            device_id={"dp": ways[way] * 4 + side * 2 + core},
            device_id_type=MESH,
        )

    def far_y(way):
        opposite = pl.ds(lax.rem(y + 2, 4) * 2, 2)
        return y_copy(way, expert_grads.at[opposite, pl.ds(2 * way, 2)], far_w.at[way], way)

    def near_y(way):
        return y_copy(2 + way, near_w.at[way], near_in.at[way], way)

    w_loads = [
        keep(expert_grads.at[pl.ds(at * 2, 2)], dst, load_sem.at[3 + k])
        for k, (at, dst) in enumerate(
            ((ways[0], near_w.at[0]), (ways[1], near_w.at[1]), (y, own_w))
        )
    ]
    meet([partner, here + right, here + left], [at * 4 + side * 2 + core for at in ways])
    for way in range(2):
        far_y(way).start()
    loads[0].wait()
    sums.begin(0)
    sums.begin(1)
    q_gain, k_gain = head_gains(first_all)
    key_grad[...] = jnp.zeros_like(key_grad)
    value_grad[...] = jnp.zeros_like(value_grad)

    @pl.loop(0, blocks)
    def _(b):
        at = pl.ds(pl.multiple_of(b * ROW, ROW), ROW)
        place = sublane((ROW, rows)) + b * ROW
        moves = jnp.where(order[...] == place, 1.0, 0.0).astype(bf16)
        out_grad[at, :] = dot(moves, mixed_grad[...]).astype(bf16)
        kv = stream_qkv[at, 128:256].astype(f32)
        low = lane(kv.shape) < 64
        other = pltpu.roll(kv, 64, 1)
        keys[at, :] = jnp.where(low, kv, other).astype(bf16)
        values[at, :] = jnp.where(low, other, kv).astype(bf16)

    @pl.loop(0, blocks)
    def _(b):
        at = pl.ds(pl.multiple_of(b * ROW, ROW), ROW)
        q, g = stream_qkv[at, 0:128], out_grad[at, :]
        low = lane(q.shape) < 64
        zero = jnp.zeros_like(q)
        qs = jnp.where(low, q, zero), jnp.where(low, zero, q)
        gs = jnp.where(low, g, zero), jnp.where(low, zero, g)
        product = jnp.transpose(g.astype(f32) * mixed_stream[at, :].astype(f32))
        inner = (
            jnp.sum(product[:64], axis=0, keepdims=True),
            jnp.sum(product[64:], axis=0, keepdims=True),
        )
        logs = jnp.transpose(log_total[at, :])
        logs = logs[0:1], logs[64:65]
        place = lane((1, ROW)) + b * ROW
        start = sequence_start(place, lengths)

        def step(begin, size, totals, diagonal):
            here = pl.ds(pl.multiple_of(begin, ROW), size)
            k, v = keys[here, :], values[here, :]
            key = sublane((size, ROW)) + begin
            allowed = key >= start
            if diagonal:
                allowed = allowed & (key <= place)
            done = []
            kt, vt = key_grad[here, :], value_grad[here, :]
            for h in range(2):
                p = jnp.exp(dot(k, qs[h], ((1,), (1,))) - logs[h])
                p = jnp.where(allowed, p, 0.0)
                d = p * (dot(v, gs[h], ((1,), (1,))) - inner[h])
                p, d = p.astype(bf16), d.astype(bf16)
                vt = vt + dot(p, gs[h])
                kt = kt + dot(d, qs[h])
                done.append(totals[h] + dot(k, d, ((0,), (0,))))
            key_grad[here, :] = kt
            value_grad[here, :] = vt
            return tuple(done)

        none = jnp.zeros((128, ROW), f32)
        totals = step(b * ROW, ROW, (none, none), True)
        totals = lax.fori_loop(
            0, b // 2, lambda j, t: step(j * CHUNK, CHUNK, t, False), totals
        )
        t0, t1 = lax.fori_loop(
            0, lax.rem(b, 2), lambda j, t: step((b - 1) * ROW, ROW, t, False), totals
        )
        grad = jnp.where(sublane((128, ROW)) < 64, t0, t1) * 0.125
        cos, sin = turned(table, block, b)
        cos, sin = jnp.transpose(cos), jnp.transpose(sin)
        swapped = jnp.concatenate([grad[32:64], grad[0:32], grad[96:128], grad[64:96]], axis=0)
        query_grad[:, at] = (grad * cos - swapped * sin).astype(bf16)

        @pl.when(b == 2)
        def _():
            sums.go_on(0)

        @pl.when(b == 3)
        def _():
            sums.go_on(1)

        @pl.when(b == 4)
        def _():
            for way in range(2):
                w_loads[way].wait()
                far_y(way).wait_recv()
                part = pl.ds(2 * way, 2)
                total = near_w[way, :, part].astype(f32) + far_w[way].astype(f32)
                near_w[way, :, part] = total.astype(bf16)
                near_y(way).start()

        @pl.when(b == 6)
        def _():
            sums.cross()

    gain_grad[...] = jnp.zeros_like(gain_grad)
    attn_gain[...] = jnp.zeros_like(attn_gain)

    @pl.loop(0, blocks)
    def _(b):
        at = pl.ds(pl.multiple_of(b * ROW, ROW), ROW)
        key, value = key_grad[at, :], value_grad[at, :]
        low = lane(key.shape) < 64
        key = key + pltpu.roll(key, 64, 1)
        cos, sin = turned(table, block, b)
        key = key * cos - swap_halves(key) * sin
        keys[at, :] = jnp.where(low, key, value + pltpu.roll(value, 64, 1)).astype(bf16)

    for load in loads[1:]:
        load.wait()

    @pl.loop(0, blocks)
    def _(b):
        at = pl.ds(pl.multiple_of(b * ROW, ROW), ROW)
        column = columns_of(order[:, at].astype(f32))[:, 0:1]
        moves = jnp.where(column == lane((ROW, rows)).astype(f32), 1.0, 0.0).astype(bf16)
        dq = dot(moves, query_grad[...], ((1,), (1,)))
        dkv = dot(moves, keys[...])

        def back(grad, value, scales, heads):
            r = lax.rsqrt(head_mean(value * value, heads) + EPS)
            scaled = value * r
            weighted = grad * scales
            result = r * (weighted - scaled * head_mean(weighted * scaled, heads))
            return result, jnp.sum(grad * scaled, axis=0, keepdims=True)

        q_result, q_sum = back(dq, proj_s[at, 0:128], q_gain, 2)
        k_result, k_sum = back(dkv, proj_s[at, 128:256], k_gain, 1)
        q_low = q_result.astype(bf16)
        k_low = jnp.where(lane(dkv.shape) < 64, k_result, dkv).astype(bf16)
        proj_grad[at, 0:128] = q_low
        proj_grad[at, 128:256] = k_low
        gain_grad[0:1, :] += q_sum
        gain_grad[1:2, :] += k_sum
        part = dot(jnp.concatenate([q_low, k_low], axis=1), wqkv[...], ((1,), (1,)))
        part = part * normed_s[at, :].astype(f32)
        attn_gain[0:1, :] += jnp.sum(part, axis=0, keepdims=True)

    @pl.loop(0, normed.shape[1] // 256)
    def _(c):
        at = pl.ds(pl.multiple_of(c * 256, 256), 256)
        part = dot(normed_s[:, at], proj_grad[...], ((0,), (0,))).astype(bf16)
        own = pl.ds(c * 4, 4)
        wqkv_grad[own, 0] = part[:, 0:128].reshape(4, 64, 128)
        wqkv_grad[own, 1] = part[:, 128:256].reshape(4, 64, 128)

    heads = gain_grad[...]
    low = lane(heads.shape) < 64
    heads = jnp.concatenate(
        [
            jnp.where(low[0:1], heads[0:1], 0.0),
            jnp.where(low[0:1], pltpu.roll(heads[0:1], 64, 1), 0.0),
            jnp.where(low[0:1], heads[1:2], 0.0),
            jnp.zeros((5, 128), f32),
        ],
        axis=0,
    )
    spots = []
    for pair in range(GROUPS // 2):
        even = pltpu.roll(heads, (128 - 8 * pair) % 128, 1)
        odd = pltpu.roll(heads, (188 - 8 * pair) % 128, 1)
        at = lane(heads.shape)
        spots.append(jnp.where(at < 4, even, jnp.where((at >= 64) & (at < 68), odd, 0.0)))
    lines = [turn_grad[...], attn_gain[...] / small[0:1, :], jnp.concatenate(spots, axis=1)]
    lines.append(jnp.zeros((128 - 56, small.shape[1]), f32))
    small_grad[...] = jnp.transpose(jnp.concatenate(lines, axis=0))
    out_sum[...] = sums.finish()
    w_loads[2].wait()
    for way in range(2):
        near_y(way).wait_recv()
    for k in range(2):
        total = own_w[k].astype(f32) + near_in[0, k].astype(f32) + near_in[1, k].astype(f32)
        expert_pair[k] = total.astype(bf16)
    for way in range(2):
        far_y(way).wait_send()
        near_y(way).wait_send()


def attend_back(
    lengths, mixed_grad, stream_qkv, mixed_stream, log_total, proj, first_all, table, block,
    order, normed, wqkv, small, turn_grad, out_part, expert_grads,
):
    rows, width = normed.shape
    pair = (2,) + expert_grads.shape[1:]
    half = (2, 2) + expert_grads.shape[2:]
    return pl.pallas_call(
        attend_back_kernel,
        out_shape=[
            jax.ShapeDtypeStruct((rows, 256), bf16),
            jax.ShapeDtypeStruct((GROUPS, 2, width // GROUPS, 128), bf16),
            jax.ShapeDtypeStruct((width, 128), f32),
            jax.ShapeDtypeStruct(out_part.shape[1:], f32),
            jax.ShapeDtypeStruct(pair, bf16),
        ],
        in_specs=[pl.BlockSpec(memory_space=pltpu.SMEM)]
        + whole(4)
        + anywhere(1)
        + whole(4)
        + anywhere(1)
        + whole(3)
        + anywhere(2),
        out_specs=whole(5),
        scratch_shapes=[
            pltpu.VMEM((8, 128), f32),
            pltpu.VMEM((rows, 128), bf16),
            pltpu.VMEM((rows, 128), bf16),
            pltpu.VMEM((rows, 128), bf16),
            pltpu.VMEM((128, rows), bf16),
            pltpu.VMEM((rows, 128), f32),
            pltpu.VMEM((rows, 128), f32),
            pltpu.VMEM((8, width), f32),
            pltpu.VMEM(normed.shape, bf16),
            pltpu.VMEM(proj.shape, f32),
            pltpu.VMEM(out_part.shape, bf16),
            *row_sum_scratch(out_part.shape[1], width),
            pltpu.SemaphoreType.DMA((6,)),
            pltpu.VMEM((2,) + half, bf16),
            pltpu.VMEM((2,) + pair, bf16),
            pltpu.VMEM((2,) + pair, bf16),
            pltpu.VMEM(pair, bf16),
            pltpu.SemaphoreType.DMA((4,)),
            pltpu.SemaphoreType.DMA((4,)),
        ],
        compiler_params=pltpu.CompilerParams(
            collective_id=7, has_side_effects=True, vmem_limit_bytes=63 << 20
        ),
        cost_estimate=cost_of(40),
        name="attend_back",
    )(
        lengths, mixed_grad, stream_qkv, mixed_stream, log_total, proj, first_all, table, block,
        order, normed, wqkv, small, turn_grad, out_part, expert_grads,
    )


def experts_kernel(
    rows_in, cot_in, tiny, small, w,
    out_part, copy_part, xs_out, us_out, inner_out, dgu_out,
    stage_x, stage_u, xs, us, ys, cs, weights, grads, inner_s, dgu_s, logits, picks, ranks, own,
    in_sem, out_sem,
):
    e = pl.program_id(0)
    local = pl.num_programs(0)
    me = lax.axis_index("tensor")
    blocks, _, width = xs.shape
    hidden = inner_s.shape[2]
    here = pl.ds(pl.multiple_of(e * CAP, CAP), CAP)
    group = blocks // 2
    tile = group * CAP
    long = ROW + 32
    count = xs.shape[1] // CAP

    def load_x(b):
        return pltpu.make_async_copy(rows_in.at[b], stage_x.at[b], in_sem.at[0, b])

    def load_u(b):
        return pltpu.make_async_copy(cot_in.at[b], stage_u.at[b, 0:ROW], in_sem.at[1, b])

    def save_slots(b):
        return (
            pltpu.make_async_copy(xs.at[b], xs_out.at[b], out_sem.at[0, b]),
            pltpu.make_async_copy(us.at[b], us_out.at[b], out_sem.at[1, b]),
        )

    def save_tile(k):
        return (
            pltpu.make_async_copy(dgu_s.at[k], dgu_out.at[k], out_sem.at[2, k]),
            pltpu.make_async_copy(inner_s.at[k], inner_out.at[k], out_sem.at[3, k]),
        )

    def save_rows(b):
        return (
            pltpu.make_async_copy(stage_x.at[b], out_part.at[b], out_sem.at[4, b]),
            pltpu.make_async_copy(stage_u.at[b, 0:long], copy_part.at[b], out_sem.at[5, b]),
        )

    def span(b):
        return pl.ds(pl.multiple_of(b * ROW, ROW), ROW)

    def hits_of(b):
        slot = sublane((CAP, ROW))
        return [ranks[i : i + 1, span(b)] == slot for i in range(count)]

    def table_of(hits):
        return jnp.concatenate([jnp.where(hit, 1.0, 0.0).astype(bf16) for hit in hits], axis=0)

    @pl.when(e == 0)
    def _():
        for b in range(blocks):
            load_x(b).start()
            load_u(b).start()
        for b in range(blocks):
            named = tiny[b, 80:96, :].astype(f32)
            picks[:, b * ROW : b * ROW + 128] = named[0:8]
            picks[:, b * ROW + 128 : (b + 1) * ROW] = named[8:16]
        shape = (32, blocks * ROW)
        expert = sublane(shape).astype(f32)
        named = jnp.zeros(shape, f32)
        for k in range(8):
            named = jnp.where(picks[k : k + 1, :] == expert, 1.0, named)
        pick = (sublane((8, 32)) + me * count == lane((8, 32))) & (sublane((8, 32)) < count)
        pick = jnp.where(pick, 1.0, 0.0)
        before = jnp.where(sublane((ROW, ROW)) < lane((ROW, ROW)), 1.0, 0.0).astype(bf16)
        router = small[8:40, :].astype(bf16)
        for b in range(blocks):
            part = named[:, b * ROW : (b + 1) * ROW]
            place = jnp.where(part > 0.5, dot(part.astype(bf16), before), -1.0)
            place = dot(pick.astype(bf16), place.astype(bf16))
            ranks[:, b * ROW : (b + 1) * ROW] = place.astype(jnp.int32)
        for b in range(blocks):
            load_x(b).wait()
            logits[:, b * ROW : (b + 1) * ROW] = dot(router, stage_x[b], ((1,), (1,)))
        gates = gates_of(named, logits[...])
        own[...] = lax.dot_general(
            pick,
            gates,
            (((1,), (0,)), ((), ())),
            precision=lax.Precision.HIGHEST,
            preferred_element_type=f32,
        )
        for b in range(blocks):
            load_u(b).wait()

        @pl.loop(0, blocks, unroll=2)
        def _(b):
            hits = hits_of(b)
            table = table_of(hits)
            xs[b] = dot(table, stage_x[b]).astype(bf16)
            us[b] = dot(table, stage_u[b, 0:ROW]).astype(bf16)
            for copy in save_slots(b):
                copy.start()
            for i in range(count):
                gate = own[i : i + 1, span(b)]
                gate = jnp.sum(jnp.where(hits[i], gate, 0.0), axis=1, keepdims=True)
                weights[b, pl.ds(i * CAP, CAP), :] = jnp.broadcast_to(gate, (CAP, 128))

    for t in range(2):
        part = pl.ds(t * group, group)
        x = xs[part, here, :].reshape(tile, width)
        u = us[part, here, :].reshape(tile, width)
        gate = weights[part, here, :].reshape(tile, 128)[:, 0:1]
        gate_act = dot(x, w[0, 0])
        up_act = dot(x, w[0, 1])
        pulled = dot(u, w[0, 2])
        sig = 1.0 / (1.0 + jnp.exp(-gate_act))
        silu = gate_act * sig
        inner = silu * up_act
        result = dot(inner.astype(bf16), w[0, 2], ((1,), (1,)))
        ys[part, here, :] = (gate * result).astype(bf16).reshape(group, CAP, width)
        grad = jnp.sum(inner * pulled, axis=1, keepdims=True)
        grads[part, here, :] = jnp.broadcast_to(grad, (tile, 128)).reshape(group, CAP, 128)
        k = e * 2 + t
        inner_s[k] = (gate * inner).astype(bf16)
        pulled = gate * pulled
        dg = (pulled * up_act * (sig * (1.0 + gate_act * (1.0 - sig)))).astype(bf16)
        du = (pulled * silu).astype(bf16)
        dgu_s[k, :, 0:hidden] = dg
        dgu_s[k, :, hidden : 2 * hidden] = du
        for copy in save_tile(k):
            copy.start()
        copy_grad = dot(dg, w[0, 0], ((1,), (1,))) + dot(du, w[0, 1], ((1,), (1,)))
        cs[part, here, :] = copy_grad.astype(bf16).reshape(group, CAP, width)

    @pl.when(e == local - 1)
    def _():
        @pl.loop(0, blocks, unroll=2)
        def _(b):
            hits = hits_of(b)
            table = table_of(hits)
            stage_x[b] = dot(table, ys[b], ((0,), (0,))).astype(bf16)
            stage_u[b, 0:ROW] = dot(table, cs[b], ((0,), (0,))).astype(bf16)
            row = sublane((32, ROW)) - me * count
            line = jnp.zeros((32, ROW), f32)
            for i in range(count):
                column = grads[b, pl.ds(i * CAP, CAP), :][:, 0:1]
                total = jnp.sum(jnp.where(hits[i], column, 0.0), axis=0, keepdims=True)
                line = jnp.where(row == i, total, line)
            high = line.astype(bf16).astype(f32)
            both = jnp.concatenate(
                [high, line - high, jnp.zeros((32, width - 2 * ROW), f32)], axis=1
            )
            stage_u[b, ROW:long] = both.astype(bf16)
            for copy in save_rows(b):
                copy.start()

        for b in range(blocks):
            for copy in (*save_slots(b), *save_tile(b), *save_rows(b)):
                copy.wait()


def experts_part(rows_in, cot_in, tiny, small, expert_full):
    blocks, rows, width = rows_in.shape
    local, _, _, hidden = expert_full.shape
    dma = pltpu.SemaphoreType.DMA
    like = jax.ShapeDtypeStruct
    held = local * CAP
    tile = blocks // 2 * CAP
    return pl.pallas_call(
        experts_kernel,
        grid=(local,),
        out_shape=[
            like((blocks, rows, width), bf16),
            like((blocks, rows + 32, width), bf16),
            like((blocks, held, width), bf16),
            like((blocks, held, width), bf16),
            like((2 * local, tile, hidden), bf16),
            like((2 * local, tile, 2 * hidden), bf16),
        ],
        in_specs=anywhere(2)
        + whole(2)
        + [pl.BlockSpec((1, 3, width, hidden), lambda s: (s, 0, 0, 0))],
        out_specs=anywhere(6),
        scratch_shapes=[
            pltpu.VMEM((blocks, rows, width), bf16),
            pltpu.VMEM((blocks, rows + 32, width), bf16),
            pltpu.VMEM((blocks, held, width), bf16),
            pltpu.VMEM((blocks, held, width), bf16),
            pltpu.VMEM((blocks, held, width), bf16),
            pltpu.VMEM((blocks, held, width), bf16),
            pltpu.VMEM((blocks, held, 128), f32),
            pltpu.VMEM((blocks, held, 128), f32),
            pltpu.VMEM((2 * local, tile, hidden), bf16),
            pltpu.VMEM((2 * local, tile, 2 * hidden), bf16),
            pltpu.VMEM((32, blocks * rows), f32),
            pltpu.VMEM((8, blocks * rows), f32),
            pltpu.VMEM((8, blocks * rows), jnp.int32),
            pltpu.VMEM((8, blocks * rows), f32),
            dma((2, blocks)),
            dma((6, blocks)),
        ],
        compiler_params=pltpu.CompilerParams(vmem_limit_bytes=63 << 20),
        cost_estimate=cost_of(40),
        name="experts",
    )(rows_in, cot_in, tiny, small, expert_full)


def weight_grads_kernel(
    x, u, inner, dgu, copy_part,
    back, out,
    made, got, rows_s, far, near, leaving, landed, row_send, row_recv,
    core_send, core_recv, local, out_sem,
):
    e, c = pl.program_id(0), pl.program_id(1)
    experts, parts = pl.num_programs(0), pl.num_programs(1)
    step = e * parts + c
    _, here, _, partner, right, left = neighbours()
    _, _, core, _, _, other = group_place()
    hidden, rows = inner.shape[1], inner.shape[0]
    share = made.shape[1] // 2
    sums = RowSums(rows_s, far, near, leaving, landed, (row_send, row_recv))

    def core_push(e, c):
        part = pl.ds(c * share, share)
        return pltpu.make_async_remote_copy(
            src_ref=made.at[e, part, 1 - core],
            dst_ref=got.at[e, part],
            send_sem=core_send.at[e, c],
            recv_sem=core_recv.at[e, c],
            device_id=other,
            device_id_type=MESH,
        )

    def save(e):
        return pltpu.make_async_copy(made.at[e, :, core], out.at[:, e], out_sem.at[e])

    def add_core(e):
        for half in range(2):
            core_push(e, half).wait_recv()

        @pl.loop(0, 2 * share)
        def _(k):
            total = made[e, k, core].astype(f32) + got[e, k].astype(f32)
            made[e, k, core] = total.astype(bf16)

        save(e).start()

    @pl.when(step == 0)
    def _():
        load = pltpu.make_async_copy(copy_part, rows_s, local)
        load.start()
        meet([partner, here + right, here + left], [other["dp"]])
        load.wait()
        sums.begin(0)

    both = dot(x[...].reshape(rows, -1), dgu[...], ((0,), (0,)))
    part = pl.ds(c * share, share)
    shape = (share, 2, -1, hidden)
    made[e, part, :, 0] = both[:, :hidden].astype(bf16).reshape(shape)
    made[e, part, :, 1] = both[:, hidden:].astype(bf16).reshape(shape)
    down = dot(u[...].reshape(rows, -1), inner[...], ((0,), (0,)))
    made[e, part, :, 2] = down.astype(bf16).reshape(shape)
    core_push(e, c).start()

    @pl.when(step == 3)
    def _():
        sums.go_on(0)

    @pl.when(step == 4)
    def _():
        sums.begin(1)

    @pl.when((e > 0) & (c == parts - 1))
    def _():
        add_core(e - 1)

    @pl.when(step == experts * parts - 1)
    def _():
        add_core(e)
        sums.cross()
        sums.go_on(1)
        back[...] = sums.finish()
        for k in range(made.shape[0]):
            for half in range(2):
                core_push(k, half).wait_send()
            save(k).wait()


def weight_grads(xs, us, inner, dgu, copy_part):
    blocks, held, width = xs.shape
    local, hidden, slots = held // CAP, inner.shape[1], blocks * CAP
    col = width // 2
    long = copy_part.shape[1]
    shard = width // GROUPS
    rows = pl.BlockSpec((blocks, CAP, col), lambda e, c: (0, e, c))
    dma = pltpu.SemaphoreType.DMA
    return pl.pallas_call(
        weight_grads_kernel,
        grid=(local, width // col),
        out_shape=[
            jax.ShapeDtypeStruct((long, width), f32),
            jax.ShapeDtypeStruct((GROUPS // 2, local, 3, shard, hidden), bf16),
        ],
        in_specs=[
            rows,
            rows,
            pl.BlockSpec((slots, hidden), lambda e, c: (e, 0)),
            pl.BlockSpec((slots, 2 * hidden), lambda e, c: (e, 0)),
        ]
        + anywhere(1),
        out_specs=[pl.BlockSpec((long, width), lambda e, c: (0, 0))] + anywhere(1),
        scratch_shapes=[
            pltpu.VMEM((local, GROUPS // 2, 2, 3, shard, hidden), bf16),
            pltpu.VMEM((local, GROUPS // 2, 3, shard, hidden), bf16),
            pltpu.VMEM((blocks, long, width), bf16),
            *row_sum_scratch(long, width),
            dma((local, 2)),
            dma((local, 2)),
            dma,
            dma((local,)),
        ],
        compiler_params=pltpu.CompilerParams(
            collective_id=6, has_side_effects=True, vmem_limit_bytes=63 << 20
        ),
        cost_estimate=cost_of(45),
        name="weight_grads",
    )(xs, us, inner, dgu, copy_part)


def finish_kernel(
    hidden, out_sum, tokens_sum, wqkv_sum, wo_sum, small_sum, head_sum, expert_pair, expert_far,
    layer_out, grad_tokens, attn_grad, ffn_grad, router_grad, query_grad, key_grad, value_grad,
    output_grad, query_gains, key_gains, gate_grad, up_grad, down_grad,
):
    layer_out[...] = hidden[...] + out_sum[...]
    grad_tokens[...] = tokens_sum[...]
    small = small_sum[...]
    columns = jnp.transpose(small)
    attn_grad[...] = columns[40:41, :]
    ffn_grad[...] = columns[0:1, :]
    router_grad[...] = pltpu.roll(small, 120, 1)[:, 0:32]
    query_grad[...] = wqkv_sum[:, 0:128]
    key_grad[...] = wqkv_sum[:, 128:192]
    value_grad[...] = pltpu.roll(wqkv_sum[:, 128:256], 64, 1)[:, 0:64]
    output_grad[...] = wo_sum[...]
    heads = jnp.transpose(head_sum[...])
    query_gains[...] = heads[48:50, 0:4]
    key_gains[...] = heads[50:51, 0:4]
    _, side, _, _, _, _ = group_place()
    for k, out in enumerate((gate_grad, up_grad, down_grad)):
        out[...] = expert_pair[side, :, k].astype(f32) + expert_far[:, k].astype(f32)


def finish(
    hidden, out_sum, tokens_sum, wqkv_sum, wo_sum, small_sum, head_sum, expert_pair, expert_far
):
    rows = small_sum.shape[0]
    shard = wo_sum.shape[0]
    expert = (expert_far.shape[0],) + expert_far.shape[2:]
    shapes = (
        hidden.shape, hidden.shape, (1, rows), (1, rows), (rows, 32), (shard, 128), (shard, 64),
        (shard, 64), (shard, 128), (2, 4), (1, 4), expert, expert, expert,
    )
    return pl.pallas_call(
        finish_kernel,
        out_shape=[jax.ShapeDtypeStruct(shape, f32) for shape in shapes],
        in_specs=whole(9),
        out_specs=whole(len(shapes)),
        compiler_params=pltpu.CompilerParams(vmem_limit_bytes=63 << 20),
        cost_estimate=cost_of(5),
        name="finish",
    )(hidden, out_sum, tokens_sum, wqkv_sum, wo_sum, small_sum, head_sum, expert_pair, expert_far)


def per_device(
    tokens,
    lengths,
    token_order,
    routes,
    cotangent,
    attn_gain,
    ffn_gain,
    router,
    w_query,
    w_key,
    w_value,
    w_output,
    query_gain,
    key_gain,
    w_gate,
    w_up,
    w_down,
):
    rows, width = tokens.shape
    group_rows = rows * RANKS

    own_experts = jnp.stack([w_gate, w_up, w_down.transpose(0, 2, 1)], axis=1)
    expert_full = lax.all_gather(own_experts, "dp", axis=2, tiled=True)
    tokens_all, qkv_cols, tiny_all, first_all, rest_all, small, routes_own = opening(
        tokens, w_query, w_key, w_value, w_output.T, attn_gain[None], ffn_gain[None], router,
        query_gain, key_gain, routes.T,
    )
    first_all = first_all.reshape((GROUPS,) + first_all.shape[3:])
    rest_all = rest_all.reshape((GROUPS,) + rest_all.shape[3:])

    frequency = ROTARY_BASE ** (-(np.arange(128) % 32) / 32.0)
    within = np.arange(ROW)[:, None] * frequency
    starts = (np.arange(group_rows // ROW) * ROW)[:, None] * frequency
    table = np.stack([np.cos(within), np.sin(within)]).astype(np.float32)
    block = np.stack([np.cos(starts), np.sin(starts)]).astype(np.float32)
    (
        normed_all, proj, stream_qkv, mixed_stream, log_total, mixed, wqkv, cot_all,
    ) = attend(
        lengths[0], tokens_all.reshape(group_rows, width), small, first_all, table, block,
        token_order, cotangent,
    )
    mixed_own, hidden, normed2_all, done = middle(
        mixed.reshape(RANKS, rows, 128), rest_all, tokens, small
    )

    qkv_cols, _ = lax.optimization_barrier((qkv_cols, done))
    wqkv_all = lax.all_gather(qkv_cols, "dp", axis=0, tiled=False)
    out_part, copy_part, xs, us, inner, dgu = experts_part(
        normed2_all, cot_all, tiny_all, small, expert_full
    )
    back, expert_grads = weight_grads(
        xs, us, inner.reshape(-1, inner.shape[2]), dgu.reshape(-1, dgu.shape[2]), copy_part
    )
    hidden_grad, mixed_grad, wo_grad, turn_grad = turn(
        back, hidden, cotangent, routes_own, small, mixed_own, rest_all
    )

    proj_grad, wqkv_grad, small_grad, out_sum, expert_pair = attend_back(
        lengths[0], mixed_grad.reshape(group_rows, 128), stream_qkv, mixed_stream, log_total,
        proj, first_all, table, block, token_order, normed_all, wqkv, small, turn_grad, out_part,
        expert_grads,
    )
    grad_tokens, wqkv_sum, wo_sum, small_sum, head_sum, expert_far = closing(
        proj_grad.reshape(RANKS, rows, 256), wo_grad.reshape((4, 2, 2) + wo_grad.shape[1:]),
        wqkv_grad.reshape((4, 2, 2) + wqkv_grad.shape[1:]), small_grad.reshape(4, 2, 2, -1, 128),
        wqkv_all, tokens, small, hidden_grad, expert_pair,
    )
    (
        layer_out, grad_tokens, attn_grad, ffn_grad, router_grad, query_grad, key_grad, value_grad,
        output_grad, query_gains, key_gains, gate_grad, up_grad, down_grad,
    ) = finish(
        hidden, out_sum, grad_tokens, wqkv_sum, wo_sum, small_sum, head_sum, expert_pair, expert_far
    )
    return (
        layer_out,
        grad_tokens,
        attn_grad[0],
        ffn_grad[0],
        router_grad,
        query_grad,
        key_grad,
        value_grad,
        output_grad.T,
        query_gains,
        key_gains,
        gate_grad,
        up_grad,
        down_grad.transpose(0, 2, 1),
    )


def solution(mesh):
    both = ("dp", "tensor")
    return jax.shard_map(
        per_device,
        mesh=mesh,
        in_specs=(
            P(both, None),
            P("dp", None),
            P("dp", None),
            P(both, None),
            P(both, None),
            P(both),
            P(both),
            P(both, None),
            P("dp", "tensor"),
            P("dp", "tensor"),
            P("dp", "tensor"),
            P("tensor", "dp"),
            P("tensor", "dp"),
            P("tensor", "dp"),
            P("tensor", "dp", None),
            P("tensor", "dp", None),
            P("tensor", None, "dp"),
        ),
        out_specs=(
            P(both, None),
            P(both, None),
            P(both),
            P(both),
            P(both, None),
            P("dp", "tensor"),
            P("dp", "tensor"),
            P("dp", "tensor"),
            P("tensor", "dp"),
            P("tensor", "dp"),
            P("tensor", "dp"),
            P("tensor", "dp", None),
            P("tensor", "dp", None),
            P("tensor", None, "dp"),
        ),
        check_vma=False,
    )
```
